32 devices in a mesh: groups: 2 (over x), mp: 16 (over z, y, core).
Axes of the slice: x: 2, y: 2, z: 4, core: 2. Of those that a mesh axis runs over, the one named last changes fastest.
Arguments:
- features: bfloat16 [32, 256, 128, 128], P(None, ('groups', 'mp')), parts along dimension 1, may hold values from -6 to 6
- cotangent: bfloat16 [32, 256, 128, 128], P(None, ('groups', 'mp')), parts along dimension 1, may hold values from -9 to 9
- spectral_weight: float32 [256, 2, 16, 32, 32], P('mp'), may hold values from -9 to 9
- pointwise_weight: bfloat16 [32, 32], replicated, may hold values from -1 to 1
- biases: float32 [32], replicated, may hold values from -3 to 3
Outputs:
- features_grad: bfloat16 [32, 256, 128, 128], P(None, ('groups', 'mp')), parts along dimension 1
- spectral_grad: float32 [512, 2, 16, 32, 32], P(('groups', 'mp')), parts along dimension 0
- pointwise_grad: float32 [64, 32], P('groups'), parts along dimension 0
- biases_grad: float32 [64], P('groups'), parts along dimension 0
The draws below stay inside these ranges and needn't reach their ends.
There are 2 independent parts, one for each index of `groups`. The reference program is written for one: setup_inputs(seed, part) draws one part's arguments, and reference() takes and returns one part's arrays. A program takes and returns all parts, laid end to end along the dimension named above; an argument that names none is the same for every part. Nothing has to cross between parts.
All inputs are finite; a program needn't handle non-finite values.
Results may differ from the reference program's by a relative error of at most 0.007.
Values sent between devices are 32-bit elements; how exact they have to be, the bound alone decides.
A program may use at most 128 MiB of HBM per device.

```python
import math
import jax
import jax.numpy as jnp
from jax import lax

C = 32
NX = 128
NY = 128
NZ = 128
KX = 16
KY = 16
KZ = 16
PAIRS = 256


def draw_cotangent(key, part):
    ramp = 0.5 + jnp.arange(NX, dtype=jnp.float32) * (1.0 / (NX - 1))
    base = jnp.clip(jax.random.normal(key, (C, NX, NY, NZ), jnp.float32), -5.5, 5.5)
    return (base * ramp[None, :, None, None]).astype(jnp.bfloat16)


def shard_levels(key, shape, pieces, smallest, largest):
    loudness = 1.0
    for dim, shards_of in pieces:
        steps = jax.random.uniform(jax.random.fold_in(jax.random.fold_in(key, 6), dim), (shards_of,), jnp.float32, smallest / len(pieces), largest / len(pieces))
        loudness = loudness * jnp.repeat(jnp.exp(steps), shape[dim] // shards_of).reshape((-1,) + (1,) * (len(shape) - 1 - dim))
    return loudness


def gaussian(key, dims, deviation, reach, cuts=(), kind=jnp.bfloat16):
    result = jax.random.normal(key, dims, jnp.float32) * deviation
    if len(cuts) > 0:
        result = shard_levels(key, dims, cuts, -0.22, 0.18) * result
    return jnp.clip(result, min=-reach, max=reach).astype(kind)


def setup_inputs(seed: int = 0, part: int = 0) -> dict:
    seeds = jax.random.split(jax.random.key(seed), 6)
    own_keys = jax.random.split(jax.random.fold_in(seeds[5], part), 6)
    return {
        "features": gaussian(own_keys[0], (C, NX, NY, NZ), 1.0, 6.0, ((1, 16),)),
        "cotangent": draw_cotangent(jax.random.fold_in(jax.random.fold_in(seeds[5], part), 71), part),
        "spectral_weight": gaussian(seeds[2], (PAIRS, 2, KX, C, C), 1.5, 9.0, ((0, 16),), jnp.float32),
        "pointwise_weight": gaussian(seeds[3], (C, C), C ** -0.5, 1.0),
        "biases": gaussian(seeds[4], (C,), 0.5, 3.0, (), jnp.float32),
    }


precise = lax.Precision.HIGHEST

def axis_tables(length, mode_count, signed):
    freqs = jnp.arange(mode_count, dtype=jnp.int32) - (mode_count // 2 if signed else 0)
    spots = jnp.arange(length, dtype=jnp.int32)
    phases = (spots[:, None] * freqs[None, :] % length).astype(jnp.float32) * (2.0 * math.pi / length)
    return (jnp.cos(phases), jnp.sin(phases))

def spectrum_plane(data, z_cos, z_sin, y_cos, y_sin, z_scale):
    hold = data.astype(jnp.float32)
    z_real = jnp.einsum('cxyz,zk->kcxy', hold, z_cos, precision=precise) * z_scale[:, None, None, None]
    z_imag = -jnp.einsum('cxyz,zk->kcxy', hold, z_sin, precision=precise) * z_scale[:, None, None, None]
    y_real = jnp.einsum('kcxy,yj->jkcx', z_real, y_cos, precision=precise) + jnp.einsum('kcxy,yj->jkcx', z_imag, y_sin, precision=precise)
    y_imag = jnp.einsum('kcxy,yj->jkcx', z_imag, y_cos, precision=precise) - jnp.einsum('kcxy,yj->jkcx', z_real, y_sin, precision=precise)
    stacked = jnp.stack([y_real, y_imag], axis=2)
    return stacked.reshape(KY * KZ, 2, stacked.shape[3], stacked.shape[4])

def spectrum_lines(part, x_cos, x_sin):
    a_real = part[:, 0]
    a_imag = part[:, 1]
    v_real = jnp.einsum('pcx,xk->pck', a_real, x_cos, precision=precise) + jnp.einsum('pcx,xk->pck', a_imag, x_sin, precision=precise)
    v_imag = jnp.einsum('pcx,xk->pck', a_imag, x_cos, precision=precise) - jnp.einsum('pcx,xk->pck', a_real, x_sin, precision=precise)
    return jnp.stack([v_real, v_imag], axis=1)

def space_lines(spec, x_cos, x_sin):
    u_real = spec[:, 0]
    u_imag = spec[:, 1]
    b_real = jnp.einsum('pck,xk->pcx', u_real, x_cos, precision=precise) - jnp.einsum('pck,xk->pcx', u_imag, x_sin, precision=precise)
    b_imag = jnp.einsum('pck,xk->pcx', u_imag, x_cos, precision=precise) + jnp.einsum('pck,xk->pcx', u_real, x_sin, precision=precise)
    return jnp.stack([b_real, b_imag], axis=1)

def space_plane(stacked, y_cos, y_sin, z_cos, z_sin):
    grid = stacked.reshape(KY, KZ, 2, stacked.shape[2], stacked.shape[3])
    q_real = grid[:, :, 0]
    q_imag = grid[:, :, 1]
    b_real = jnp.einsum('jkcx,yj->kcxy', q_real, y_cos, precision=precise) - jnp.einsum('jkcx,yj->kcxy', q_imag, y_sin, precision=precise)
    b_imag = jnp.einsum('jkcx,yj->kcxy', q_imag, y_cos, precision=precise) + jnp.einsum('jkcx,yj->kcxy', q_real, y_sin, precision=precise)
    return jnp.einsum('kcxy,zk->cxyz', b_real, z_cos, precision=precise) - jnp.einsum('kcxy,zk->cxyz', b_imag, z_sin, precision=precise)

def modes_product(spec, weight):
    v_real, v_imag = (spec[:, 0], spec[:, 1])
    r_real, r_imag = (weight[:, 0], weight[:, 1])
    u_real = jnp.einsum('pck,pkco->pok', v_real, r_real, precision=precise) - jnp.einsum('pck,pkco->pok', v_imag, r_imag, precision=precise)
    u_imag = jnp.einsum('pck,pkco->pok', v_real, r_imag, precision=precise) + jnp.einsum('pck,pkco->pok', v_imag, r_real, precision=precise)
    return jnp.stack([u_real, u_imag], axis=1)

def modes_adjoint(dspec, weight):
    d_real, d_imag = (dspec[:, 0], dspec[:, 1])
    r_real, r_imag = (weight[:, 0], weight[:, 1])
    g_real = jnp.einsum('pok,pkco->pck', d_real, r_real, precision=precise) + jnp.einsum('pok,pkco->pck', d_imag, r_imag, precision=precise)
    g_imag = jnp.einsum('pok,pkco->pck', d_imag, r_real, precision=precise) - jnp.einsum('pok,pkco->pck', d_real, r_imag, precision=precise)
    return jnp.stack([g_real, g_imag], axis=1)

def modes_gradient(spec, dspec):
    v_real, v_imag = (spec[:, 0], spec[:, 1])
    d_real, d_imag = (dspec[:, 0], dspec[:, 1])
    w_real = jnp.einsum('pck,pok->pkco', v_real, d_real, precision=precise) + jnp.einsum('pck,pok->pkco', v_imag, d_imag, precision=precise)
    w_imag = jnp.einsum('pck,pok->pkco', v_real, d_imag, precision=precise) - jnp.einsum('pck,pok->pkco', v_imag, d_real, precision=precise)
    return jnp.stack([w_real, w_imag], axis=1)

def reference(features, cotangent, spectral_weight, pointwise_weight, biases):
    z_cos, z_sin = axis_tables(NZ, KZ, False)
    z_cos = lax.optimization_barrier(z_cos.astype(jnp.bfloat16)).astype(jnp.float32)
    z_sin = lax.optimization_barrier(z_sin.astype(jnp.bfloat16)).astype(jnp.float32)
    y_cos, y_sin = axis_tables(NY, KY, True)
    x_cos, x_sin = axis_tables(NX, KX, True)
    z_cos_full, z_sin_full = axis_tables(NZ, KZ, False)
    z_weight = jnp.where(jnp.arange(KZ) == 0, 1.0, 2.0).astype(jnp.float32) / float(NX * NY * NZ)
    unit_weight = jnp.ones((KZ,), jnp.float32)
    spec = spectrum_lines(spectrum_plane(features, z_cos, z_sin, y_cos, y_sin, unit_weight), x_cos, x_sin)
    mixed = modes_product(spec, spectral_weight)
    spectral = space_plane(space_lines(mixed, x_cos, x_sin), y_cos, y_sin, z_cos_full * z_weight[None, :], z_sin_full * z_weight[None, :])
    feats = features.astype(jnp.float32)
    mixer = pointwise_weight.astype(jnp.float32)
    preact = spectral + jnp.einsum('oc,cxyz->oxyz', mixer, feats, precision=precise) + biases[:, None, None, None]
    _, pullback = jax.vjp(jax.nn.gelu, preact)
    pre_grad = pullback(cotangent.astype(jnp.float32))[0].astype(jnp.bfloat16)
    dspec = spectrum_lines(spectrum_plane(pre_grad, z_cos, z_sin, y_cos, y_sin, z_weight), x_cos, x_sin)
    spectral_grad = modes_gradient(spec, dspec)
    dmixed = modes_adjoint(dspec, spectral_weight)
    grads_f = pre_grad.astype(jnp.float32)
    back = space_plane(space_lines(dmixed, x_cos, x_sin), y_cos, y_sin, z_cos_full, z_sin_full)
    features_grad = (back + jnp.einsum('oc,oxyz->cxyz', mixer, grads_f, precision=precise)).astype(jnp.bfloat16)
    factor = float(NX * NY * NZ) ** (-0.5)
    pointwise_grad = jnp.einsum('oxyz,cxyz->oc', grads_f, feats, precision=precise) * factor
    biases_grad = lax.optimization_barrier(jnp.sum(grads_f, axis=(1, 2, 3))) * factor
    return (features_grad, spectral_grad, pointwise_grad, biases_grad)
```

```python
import functools
import math

import jax
import jax.numpy as jnp
import ml_dtypes
import numpy as np
from jax import lax
from jax.experimental import pallas as pl
from jax.experimental.pallas import tpu as pltpu
from jax.sharding import PartitionSpec as P

C = 32
NX = 128
NY = 128
NZ = 128
KX = 16
KY = 16
KZ = 16
SCALE = 1.0 / (NX * NY * NZ)
OCT = 8
GROUPS = C // OCT
GLANES = 2 * OCT * KZ
LANES = 128
SAVES = 4
BF = jnp.bfloat16
F32 = jnp.float32
precise = lax.Precision.HIGHEST
VMEM = pl.BlockSpec(memory_space=pltpu.VMEM)
HBM = pl.BlockSpec(memory_space=pl.ANY)


def trig(length, mode_count, signed):
    freqs = np.arange(mode_count) - (mode_count // 2 if signed else 0)
    spots = np.arange(length)
    phases = (spots[:, None] * freqs[None, :] % length) * (2.0 * math.pi / length)
    return np.cos(phases), np.sin(phases)


def low(table):
    return np.asarray(table, np.float32).astype(ml_dtypes.bfloat16)


def tables(rows):
    zc, zs = trig(NZ, KZ, False)
    yc, ys = trig(NY, KY, True)
    xc, xs = trig(NX, KX, True)
    wz = np.where(np.arange(KZ) == 0, 1.0, 2.0) * SCALE
    eye = np.eye(rows)
    fy = np.einsum("syj,xw->sjxwy", np.stack([yc, ys]), eye).reshape(2 * KY * rows, rows * NY)
    gy = np.einsum("syj,xw->xysjw", np.stack([yc, -ys]), eye).reshape(rows * NY, 2 * KY * rows)
    zc_low = low(zc).astype(np.float64)
    zs_low = low(zs).astype(np.float64)
    oct_eye = np.eye(OCT)
    block = np.stack([np.stack([zc_low, -zs_low]), np.stack([-zs_low, -zc_low])])
    fz = np.einsum("srzk,ab->aszrbk", block, oct_eye).reshape(OCT * 2 * NZ, 2 * OCT * KZ)
    fz_w = (fz.reshape(-1, KZ) * wz).reshape(fz.shape)
    fz_k = np.einsum("srzk,ab->aszrkb", block, oct_eye).reshape(fz.shape)
    back = np.stack([np.stack([zc, zs]), np.stack([-zs, zc])])
    gz = np.einsum("rqzk,ab->rakbqz", back, oct_eye).reshape(2 * OCT * KZ, OCT * 2 * NZ)
    gz_w = (np.einsum("rqzk,ab,k->rakbqz", back, oct_eye, wz)).reshape(gz.shape)
    gz_k = np.einsum("rqzk,ab->rkabqz", back, oct_eye).reshape(gz.shape)
    fx = np.concatenate([xc.T, xs.T], 0).astype(np.float32)
    gx = np.concatenate([xc, xs], 0).astype(np.float32)
    fx2 = np.block([[xc.T, xs.T], [-xs.T, xc.T]]).astype(np.float32)
    gx2 = np.block([[xc, -xs], [xs, xc]]).astype(np.float32)
    return low(fy), low(gy), low(fz), low(fz_w), low(gz), low(gz_w), fx, gx, fx2, gx2, low(fz_k), low(gz_k)


def dot(a, b):
    return jnp.dot(a, b, preferred_element_type=F32)


def forward_group(src, g, fy, fz, lines):
    parts = []
    for q in range(0, OCT, 2):
        pair = jnp.concatenate([src[g * OCT + q], src[g * OCT + q + 1]], axis=1)
        both = dot(fy[...], pair).astype(BF)
        for h in range(2):
            piece = both[:, h * NZ : (h + 1) * NZ]
            parts += [piece[:lines], piece[lines:]]
    return dot(jnp.concatenate(parts, axis=1), fz[...])


def plane_back(src, gz, gy, out):
    @pl.loop(0, GROUPS)
    def _(g):
        lhs = src[:, pl.ds(pl.multiple_of(g * GLANES, GLANES), GLANES)].astype(BF)
        u = dot(lhs, gz[...]).astype(BF)
        for q in range(0, OCT, 2):
            cols = []
            for h in range(2):
                o = q + h
                cols.append(
                    jnp.concatenate(
                        [u[:, (2 * o + r) * NZ : (2 * o + r + 1) * NZ] for r in range(2)], axis=0
                    )
                )
            res = dot(gy[...], jnp.concatenate(cols, axis=1))
            out[g * OCT + q] = res[:, :NZ]
            out[g * OCT + q + 1] = res[:, NZ:]


def plain_forward(src, fy, fz, out, lines):
    @pl.loop(0, GROUPS)
    def _(g):
        at = pl.multiple_of(g * GLANES, GLANES)
        out[:, pl.ds(at, GLANES)] = forward_group(src, g, fy, fz, lines)


def load_groups(hbm, buf, sems):
    copies = []
    for g in range(GROUPS):
        part = pl.ds(g * OCT, OCT)
        copies.append(pltpu.make_async_copy(hbm.at[part], buf.at[part], sems.at[g]))
        copies[-1].start()
    return copies


def greet(n):
    me = lax.axis_index("mp")

    @pl.loop(1, n)
    def _(s):
        pl.semaphore_signal(
            pltpu.get_barrier_semaphore(),
            inc=1,
            device_id={"mp": lax.rem(me + s, n)},
            device_id_type=pl.DeviceIdType.MESH,
        )


def remote(src, dst, send, recv, peer):
    return pltpu.make_async_remote_copy(
        src_ref=src,
        dst_ref=dst,
        send_sem=send,
        recv_sem=recv,
        device_id={"mp": peer},
        device_id_type=pl.DeviceIdType.MESH,
    )


def forward_kernel(rows, feat, fy, fz, out):
    plain_forward(feat, fy, fz, out, KY * rows)


TILE = 16
STEP = 4


def tile_of(ref, t):
    at = pl.multiple_of(t * TILE, TILE)
    return ref[:, pl.ds(at, TILE), :].reshape(C * TILE, NZ)


def put_tile(ref, t, value):
    at = pl.multiple_of(t * TILE, TILE)
    ref[:, pl.ds(at, TILE), :] = value.reshape(C, TILE, NZ)


def widen(weight):
    n = C * TILE
    row = lax.broadcasted_iota(jnp.int32, (n, C), 0) // TILE
    up = jnp.where(row == lax.broadcasted_iota(jnp.int32, (n, C), 1), 1.0, 0.0).astype(BF)
    left = dot(up, weight).astype(BF)
    full = lax.dot_general(left, up, (((1,), (1,)), ((), ())), preferred_element_type=F32)
    ri = lax.broadcasted_iota(jnp.int32, (n, n), 0)
    ci = lax.broadcasted_iota(jnp.int32, (n, n), 1)
    return jnp.where(ri % TILE == ci % TILE, full, 0.0).astype(BF)


def middle_kernel(
    rows, feat_hbm, cot_hbm, modes, weight, bias, gz, gy, fy, fz, pg_hbm, part, sums,
    field, acc, bacc, kron, feat, cot, pg, fsem, csem, psem,
):
    loads = load_groups(feat_hbm, feat, fsem) + load_groups(cot_hbm, cot, csem)
    kron[...] = widen(weight[...])
    acc[...] = jnp.zeros_like(acc)
    bacc[...] = jnp.zeros_like(bacc)
    plane_back(modes, gz, gy, field)
    for copy in loads:
        copy.wait()

    @pl.loop(0, rows * NY // (STEP * TILE))
    def _(s):
        f = jnp.concatenate([tile_of(feat, STEP * s + h) for h in range(STEP)], axis=1)
        mix = dot(kron[...], f)
        gs = []
        for h in range(STEP):
            t = STEP * s + h
            x = mix[:, h * NZ : (h + 1) * NZ] + tile_of(field, t) + bias[...]
            x2 = x * x
            a = math.sqrt(2.0 / math.pi)
            th = jnp.tanh(x * (a + (a * 0.044715) * x2))
            d = (0.5 + 0.5 * th) * (1.0 + (x * (1.0 - th)) * (a + (3.0 * a * 0.044715) * x2))
            g = (tile_of(cot, t).astype(F32) * d).astype(BF)
            put_tile(pg, t, g)
            gs.append(g)
        bacc[...] += sum(g.astype(F32) for g in gs)
        g = jnp.concatenate(gs, axis=1)
        acc[...] += lax.dot_general(g, f, (((1,), (1,)), ((), ())), preferred_element_type=F32)

    save = pltpu.make_async_copy(pg, pg_hbm, psem)
    save.start()
    size = C * TILE
    ri = lax.broadcasted_iota(jnp.int32, (size, size), 0)
    ci = lax.broadcasted_iota(jnp.int32, (size, size), 1)
    masked = jnp.where(ri % TILE == ci % TILE, acc[...], 0.0)
    rows_sum = jnp.sum(masked.reshape(C, TILE, size), axis=1)
    fold = jnp.where(
        lax.broadcasted_iota(jnp.int32, (size, LANES), 0) // TILE
        == lax.broadcasted_iota(jnp.int32, (size, LANES), 1),
        1.0,
        0.0,
    ).astype(F32)
    pw = jnp.dot(rows_sum, fold, precision=precise, preferred_element_type=F32)
    by_row = jnp.sum(bacc[...].reshape(C, TILE, NZ), axis=1)
    lane = lax.broadcasted_iota(jnp.int32, (C, LANES), 1)
    sums[...] = pw + jnp.where(lane == C, jnp.sum(by_row, axis=1, keepdims=True), 0.0)
    plain_forward(pg, fy, fz, part, KY * rows)
    save.wait()


def last_kernel(rows, pg_hbm, modes, weight, gz, gy, out_hbm, field, kron, pg, out, fsem, osem):
    loads = load_groups(pg_hbm, pg, fsem)
    kron[...] = widen(weight[...])
    plane_back(modes, gz, gy, field)
    for copy in loads:
        copy.wait()
    saves = []
    cells = rows * NY // SAVES
    for piece in range(SAVES):

        @pl.loop(0, cells // (STEP * TILE))
        def _(i):
            s = piece * (cells // (STEP * TILE)) + i
            f = jnp.concatenate([tile_of(pg, STEP * s + h) for h in range(STEP)], axis=1)
            mix = dot(kron[...], f)
            for h in range(STEP):
                t = STEP * s + h
                r = mix[:, h * NZ : (h + 1) * NZ] + tile_of(field, t)
                put_tile(out, t, r.astype(BF))

        at = pl.ds(piece * cells, cells)
        saves.append(pltpu.make_async_copy(out.at[:, at], out_hbm.at[:, at], osem.at[piece]))
        saves[-1].start()
    for copy in saves:
        copy.wait()


def exchange_kernel(n, arrays, *refs):
    me = lax.axis_index("mp")
    greet(n)
    srcs = refs[:arrays]
    dsts = refs[arrays : 2 * arrays]
    send, recv, own = refs[2 * arrays :]
    pl.semaphore_wait(pltpu.get_barrier_semaphore(), n - 1)

    @pl.loop(1, n)
    def _(s):
        peer = lax.rem(me + s, n)
        for i in range(arrays):
            remote(
                srcs[i].at[peer], dsts[i].at[me], send.at[i, peer], recv.at[i, me], peer
            ).start()

    for i in range(arrays):
        mine = pltpu.make_async_copy(srcs[i].at[me], dsts[i].at[me], own.at[i])
        mine.start()
        mine.wait()

    @pl.loop(1, n)
    def _(s):
        peer = lax.rem(me + s, n)
        for i in range(arrays):
            both = remote(
                srcs[i].at[peer], dsts[i].at[peer], send.at[i, peer], recv.at[i, peer], peer
            )
            both.wait_recv()
            both.wait_send()


def exchange(xs, n, cid):
    shapes = [jax.ShapeDtypeStruct(x.shape, x.dtype) for x in xs]
    return pl.pallas_call(
        functools.partial(exchange_kernel, n, len(xs)),
        out_shape=shapes,
        in_specs=[VMEM] * len(xs),
        out_specs=[VMEM] * len(xs),
        scratch_shapes=[
            pltpu.SemaphoreType.DMA((len(xs), n)),
            pltpu.SemaphoreType.DMA((len(xs), n)),
            pltpu.SemaphoreType.DMA((len(xs),)),
        ],
        compiler_params=pltpu.CompilerParams(
            collective_id=cid, has_side_effects=True, vmem_limit_bytes=16 << 20
        ),
        name=f"exchange{cid}",
    )(*xs)


def call(kernel, rows, outs, scratch, args, name, far=(), far_out=(), cid=None):
    outs = list(outs)
    params = {} if cid is None else {"collective_id": cid, "has_side_effects": True}
    return pl.pallas_call(
        functools.partial(kernel, rows),
        out_shape=outs,
        in_specs=[HBM if i in far else VMEM for i in range(len(args))],
        out_specs=[HBM if i in far_out else VMEM for i in range(len(outs))],
        scratch_shapes=scratch,
        compiler_params=pltpu.CompilerParams(vmem_limit_bytes=60 << 20, **params),
        name=name,
    )(*args)


def owner_blocks(part, n, rows):
    subs = n // KY
    if subs > 1:
        v = part.reshape(KY, rows, 2 * C, subs, KZ // subs)
        part = jnp.transpose(v, (0, 3, 1, 2, 4))
    return part.reshape(n, rows, 2 * C * KZ // subs)


def plane_blocks(got, n, rows):
    subs = n // KY
    if subs > 1:
        v = got.reshape(KY, subs, rows, 2 * C, KZ // subs)
        got = jnp.transpose(v, (0, 2, 3, 1, 4))
    return got.reshape(KY * rows, 2 * C * KZ)


def lines_forward(g, fx):
    g = g.reshape(NX, -1)
    t = jnp.einsum("qx,xl->ql", fx, g, precision=precise).reshape(2, KX, GROUPS, 2, OCT, -1)
    real = t[0, :, :, 0] + t[1, :, :, 1]
    imag = t[0, :, :, 1] - t[1, :, :, 0]
    real, imag = (jnp.transpose(v.reshape(KX, C, -1), (2, 0, 1)) for v in (real, imag))
    return real, imag


def lines_back(real, imag, gx, n, rows):
    u = jnp.stack([real, imag]).reshape(2, real.shape[0], KX, GROUPS, OCT)
    u = jnp.transpose(u, (2, 3, 0, 4, 1)).reshape(KX, -1)
    b = jnp.einsum("qa,al->ql", gx, u, precision=precise).reshape(2, NX, GROUPS, 2, -1)
    lines = jnp.stack([b[0, :, :, 0] - b[1, :, :, 1], b[0, :, :, 1] + b[1, :, :, 0]], 2)
    return lines.reshape(n, rows, -1)


HALF = OCT * KZ
FULL = 2 * KX * C
ONE = 1.0 / SCALE
RING = 4
PAIR = 2 * NZ
CHUNK = 256
SUB = 128
ROOT = math.sqrt(2.0 / math.pi)


def sharp(a, b):
    return jnp.dot(a, b, precision=precise, preferred_element_type=F32)


def lane_weight():
    k = lax.broadcasted_iota(jnp.int32, (1, GLANES), 1) % HALF // OCT
    return jnp.where(k == 0, SCALE, 2.0 * SCALE)


def send_group(n, turn, g, src, dst, send, recv):
    me = lax.axis_index("mp")

    @pl.loop(1, n)
    def _(s):
        peer = lax.rem(me + s, n)
        remote(src.at[g, peer], dst.at[g, me], send.at[turn, g], recv.at[turn, g], peer).start()

    pltpu.make_async_copy(src.at[g, me], dst.at[g, me], recv.at[turn, g]).start()


def wait_bytes(ref, sem):
    pltpu.make_async_copy(ref, ref, sem).wait()


def wait_sent(n, turn, g, src, send):
    wait_bytes(src.at[g, pl.ds(0, n - 1)], send.at[turn, g])


def spectrum(dst, g, fx2):
    pair = [dst[g, :, :, r * HALF : (r + 1) * HALF].reshape(NX, HALF) for r in range(2)]
    return sharp(fx2[...], jnp.concatenate(pair, axis=0))


def gather_channels(parts, k):
    lane = lax.broadcasted_iota(jnp.int32, (2 * KX, LANES), 1) // OCT
    out = jnp.zeros((2 * KX, LANES), F32)
    for g in range(GROUPS):
        shift = (g * OCT - k * OCT) % LANES
        moved = pltpu.roll(parts[g], shift, 1) if shift else parts[g]
        out = jnp.where(lane == g, moved, out)
    return out


def fill_lanes(v):
    v = v + pltpu.roll(v, C, 1)
    return v + pltpu.roll(v, 2 * C, 1)


def own_mode(m):
    row = lax.broadcasted_iota(jnp.int32, (2 * KX, LANES), 0) % KX
    lane = lax.broadcasted_iota(jnp.int32, (2 * KX, LANES), 1) // C
    return row == m * (LANES // C) + lane


def diagonal(spread):
    turned = jnp.concatenate([-spread[KX:], spread[:KX]], axis=0)
    blocks = [jnp.where(own_mode(m), v, 0.0) for v in (spread, turned) for m in range(KX * C // LANES)]
    return jnp.concatenate(blocks, axis=1)


def put_channels(parts, k, v):
    lane = lax.broadcasted_iota(jnp.int32, (2 * KX, LANES), 1) // OCT
    for g in range(GROUPS):
        shift = (k * OCT - g * OCT) % LANES
        moved = pltpu.roll(v, shift, 1) if shift else v
        parts[g] = jnp.where(lane == k, moved, parts[g])


def lines_out(parts, gx2, src, n):
    for g in range(GROUPS):
        both = sharp(gx2[...], parts[g])
        for r in range(2):
            src[g, :, :, r * HALF : (r + 1) * HALF] = both[r * NX : (r + 1) * NX].reshape(
                n, NX // n, HALF
            )


def widen_with(weight, turn):
    n = C * TILE
    row = lax.broadcasted_iota(jnp.int32, (n, C), 0) // TILE
    up = jnp.where(row == lax.broadcasted_iota(jnp.int32, (n, C), 1), 1.0, 0.0).astype(BF)
    dims = (((1,), (1 if turn else 0,)), ((), ()))
    left = lax.dot_general(up, weight, dims, preferred_element_type=F32).astype(BF)
    full = lax.dot_general(left, up, (((1,), (1,)), ((), ())), preferred_element_type=F32)
    ri = lax.broadcasted_iota(jnp.int32, (n, n), 0)
    ci = lax.broadcasted_iota(jnp.int32, (n, n), 1)
    return jnp.where(ri % TILE == ci % TILE, full, 0.0).astype(BF)


def slope(x):
    x2 = x * x
    th = jnp.tanh(x * (ROOT + (ROOT * 0.044715) * x2))
    return (1.0 + th) * (0.5 + (1.0 - th) * (x * (0.5 * ROOT + (1.5 * ROOT * 0.044715) * x2)))


def unfold(lhs, gz, ub):
    lines = lhs.shape[0]
    u = dot(lhs, gz[...]).astype(BF)
    for q in range(OCT):
        for r in range(2):
            at = (2 * q + r) * NZ
            ub[r * lines : (r + 1) * lines, q * NZ : (q + 1) * NZ] = u[:, at : at + NZ]


def heart_kernel(
    rows, n, feat_hbm, cot_hbm, w_hbm, fy_hbm, fz_hbm, gy_hbm, gz_hbm, weight, bias, fx2, gx2,
    mix_hbm, back, vout, dout, total,
    feat, cot, pg, field, ring, wb, fy, fz, gy, gz, kron, acc, ub, stage, src_a, src_b,
    dst_1, dst_2, dst_3, dst_4, sums, every, fsem, csem, tsem, wsem, send, recv, ssem, rsem, osem,
):
    me = lax.axis_index("mp")
    cells = rows * NY
    lines = KY * rows
    steps = cells // (STEP * TILE)
    greet(n)
    early = [pltpu.make_async_copy(a, b, tsem.at[i]) for i, (a, b) in enumerate(((fy_hbm, fy), (fz_hbm, fz)))]
    late = [pltpu.make_async_copy(a, b, tsem.at[2 + i]) for i, (a, b) in enumerate(((gy_hbm, gy), (gz_hbm, gz)))]

    def feat_copy(g):
        part = pl.ds(g * OCT, OCT)
        return pltpu.make_async_copy(feat_hbm.at[part], feat.at[part], fsem.at[g])

    def cot_copy(g):
        part = pl.ds(g * OCT, OCT)
        return pltpu.make_async_copy(cot_hbm.at[part], cot.at[part], csem.at[g])

    def ring_copy(k, slot):
        return pltpu.make_async_copy(w_hbm.at[k], ring.at[slot], wsem.at[slot])

    for copy in early:
        copy.start()
    for g in range(GROUPS):
        feat_copy(g).start()
    for copy in early:
        copy.wait()

    @pl.loop(0, GROUPS)
    def _(g):
        feat_copy(g).wait()
        res = forward_group(feat, g, fy, fz, lines)
        src_a[g] = res.reshape(n, rows, GLANES)

        @pl.when(g == 0)
        def _():
            pl.semaphore_wait(pltpu.get_barrier_semaphore(), n - 1)

        send_group(n, 0, g, src_a, dst_1, send, recv)

    for k in range(RING):
        ring_copy(k, k).start()
    for copy in late:
        copy.start()
    for g in range(GROUPS):
        cot_copy(g).start()

    kron[...] = widen_with(weight[...], False)
    size = C * TILE
    row = lax.broadcasted_iota(jnp.int32, (size, C), 0) // TILE
    column = jnp.where(row == lax.broadcasted_iota(jnp.int32, (size, C), 1), bias[...], 0.0)
    shift = jnp.sum(column, axis=1, keepdims=True)

    @pl.loop(0, steps)
    def _(s):
        f = jnp.concatenate([tile_of(feat, STEP * s + h) for h in range(STEP)], axis=1)
        mix = dot(kron[...], f)
        for h in range(STEP):
            put_tile(field, STEP * s + h, mix[:, h * NZ : (h + 1) * NZ] + shift)

    @pl.loop(0, KZ // RING)
    def _(i):
        for slot in range(RING):
            k = i * RING + slot
            ring_copy(k, slot).wait()
            wb[k] = ring[slot].astype(BF)

            @pl.when(k + RING < KZ)
            def _():
                ring_copy(k + RING, slot).start()

    for g in range(GROUPS):
        wait_bytes(dst_1.at[g], recv.at[0, g])
        vout[g] = spectrum(dst_1, g, fx2)
    parts = [vout[g] for g in range(GROUPS)]
    mixed = [jnp.zeros((2 * KX, LANES), F32) for _ in range(GROUPS)]
    for k in range(KZ):
        left = diagonal(fill_lanes(gather_channels(parts, k))).astype(BF)
        stage[k, :, :C] = dot(left, wb[k])
    for k in range(KZ):
        put_channels(mixed, k, stage[k])
    lines_out(mixed, gx2, src_b, n)
    for g in range(GROUPS):
        send_group(n, 1, g, src_b, dst_2, send, recv)
    for copy in late:
        copy.wait()
    for g in range(GROUPS):
        wait_sent(n, 0, g, src_a, send)
        cot_copy(g).wait()

    @pl.loop(0, GROUPS)
    def _(g):
        wait_bytes(dst_2.at[g], recv.at[1, g])
        lhs = (dst_2[g].reshape(lines, GLANES) * lane_weight()).astype(BF)
        unfold(lhs, gz, ub)

        @pl.loop(0, OCT // 2)
        def _(p):
            uv = ub[:, pl.ds(pl.multiple_of(p * PAIR, PAIR), PAIR)]
            for r in range(0, cells, CHUNK):
                res = dot(gy[r : r + CHUNK, :], uv)
                for h in range(2):
                    c = g * OCT + 2 * p + h
                    for t in range(0, CHUNK, SUB):
                        at = slice(r + t, r + t + SUB)
                        x = res[t : t + SUB, h * NZ : (h + 1) * NZ] + field[c, at]
                        pg[c, at] = (cot[c, at].astype(F32) * slope(x)).astype(BF)

        out = forward_group(pg, g, fy, fz, lines) * lane_weight()
        src_a[g] = out.reshape(n, rows, GLANES)
        send_group(n, 2, g, src_a, dst_3, send, recv)

    acc[...] = jnp.zeros_like(acc)

    @pl.loop(0, steps)
    def _(s):
        f = jnp.concatenate([tile_of(feat, STEP * s + h) for h in range(STEP)], axis=1)
        g = jnp.concatenate([tile_of(pg, STEP * s + h) for h in range(STEP)], axis=1)
        acc[...] += lax.dot_general(g, f, (((1,), (1,)), ((), ())), preferred_element_type=F32)

    ri = lax.broadcasted_iota(jnp.int32, (size, size), 0)
    ci = lax.broadcasted_iota(jnp.int32, (size, size), 1)
    masked = jnp.where(ri % TILE == ci % TILE, acc[...], 0.0)
    rows_sum = jnp.sum(masked.reshape(C, TILE, size), axis=1)
    fold = jnp.where(
        lax.broadcasted_iota(jnp.int32, (size, LANES), 0) // TILE
        == lax.broadcasted_iota(jnp.int32, (size, LANES), 1),
        1.0,
        0.0,
    ).astype(F32)
    pw = sharp(rows_sum, fold)
    packed = pw[:8]
    for i in range(1, C // 8):
        packed = packed + pltpu.roll(pw[8 * i : 8 * i + 8], i * C, 1)
    sums[:8] = packed
    kron[...] = widen_with(weight[...], True)

    for g in range(GROUPS):
        wait_bytes(dst_3.at[g], recv.at[2, g])
        dout[g] = spectrum(dst_3, g, fx2)
    parts = [dout[g] for g in range(GROUPS)]
    dc = jnp.zeros((1, LANES), F32)
    lane = lax.broadcasted_iota(jnp.int32, (1, LANES), 1)
    for g in range(GROUPS):
        v = parts[g][KX // 2 : KX // 2 + 1]
        v = pltpu.roll(v, g * OCT, 1) if g else v
        dc = jnp.where(lane // OCT == g, v * ONE, dc)
    owner = jnp.where(me == KY // 2, 1.0, 0.0)
    first = lax.broadcasted_iota(jnp.int32, (8, LANES), 0) == 0
    sums[8:] = jnp.where(first, dc * owner, 0.0)
    mixed = [jnp.zeros((2 * KX, LANES), F32) for _ in range(GROUPS)]
    half = KX * C
    for k in range(KZ):
        d = gather_channels(parts, k)[:, :C].astype(BF)
        full = lax.dot_general(d, wb[k], (((1,), (1,)), ((), ())), preferred_element_type=F32)
        a0 = jnp.zeros((2 * KX, LANES), F32)
        a1 = a0
        for m in range(half // LANES):
            own = own_mode(m)
            a0 = a0 + jnp.where(own, full[:, m * LANES : (m + 1) * LANES], 0.0)
            a1 = a1 + jnp.where(own, full[:, half + m * LANES : half + (m + 1) * LANES], 0.0)
        both = a0 + jnp.concatenate([a1[KX:], -a1[:KX]], axis=0)
        put_channels(mixed, k, fill_lanes(both))
    for g in range(GROUPS):
        wait_sent(n, 1, g, src_b, send)
    lines_out(mixed, gx2, src_b, n)
    for g in range(GROUPS):
        send_group(n, 3, g, src_b, dst_4, send, recv)

    @pl.loop(1, n)
    def _(s):
        peer = lax.rem(me + s, n)
        remote(sums, every.at[me], ssem, rsem, peer).start()

    pltpu.make_async_copy(sums, every.at[me], rsem).start()

    @pl.loop(0, steps)
    def _(s):
        f = jnp.concatenate([tile_of(pg, STEP * s + h) for h in range(STEP)], axis=1)
        mix = dot(kron[...], f)
        for h in range(STEP):
            put_tile(cot, STEP * s + h, mix[:, h * NZ : (h + 1) * NZ].astype(BF))

    save = pltpu.make_async_copy(cot, mix_hbm, osem)
    save.start()
    for g in range(GROUPS):
        wait_bytes(dst_4.at[g], recv.at[3, g])
        back[g] = dst_4[g].reshape(lines, GLANES).astype(BF)
    wait_bytes(every, rsem)
    total[...] = jnp.sum(every[...], axis=0) * float(NX * NY * NZ) ** (-0.5)
    wait_bytes(every.at[pl.ds(0, n - 1)], ssem)
    for g in range(GROUPS):
        wait_sent(n, 2, g, src_a, send)
        wait_sent(n, 3, g, src_b, send)
    save.wait()


def tail_kernel(
    rows, mix_hbm, gz_hbm, gy_hbm, back, v, d, total, grad_hbm, sg_hbm, pwg, bg,
    mix, out, gz, gy, ub, sg, msem, tsem, osem, ssem,
):
    cells = rows * NY
    tables_in = [pltpu.make_async_copy(a, b, tsem.at[i]) for i, (a, b) in enumerate(((gz_hbm, gz), (gy_hbm, gy)))]
    for copy in tables_in:
        copy.start()
    loads = load_groups(mix_hbm, mix, msem)
    t = total[...]
    for i in range(C // 8):
        part = pltpu.roll(t[:8], LANES - i * C, 1) if i else t[:8]
        pwg[8 * i : 8 * i + 8, :] = part[:, :C]
    bg[...] = t[8:9, :C]
    vs = [v[g] for g in range(GROUPS)]
    ds = [d[g] for g in range(GROUPS)]
    for k in range(KZ):
        full = diagonal(fill_lanes(gather_channels(vs, k)))
        right = gather_channels(ds, k)[:, :C]
        high, top = full.astype(BF), right.astype(BF)
        rest, low_part = (full - high.astype(F32)).astype(BF), (right - top.astype(F32)).astype(BF)
        left = jnp.concatenate([high, rest, high], axis=0)
        side = jnp.concatenate([top, top, low_part], axis=0)
        sg[k] = lax.dot_general(left, side, (((0,), (0,)), ((), ())), preferred_element_type=F32)
        pltpu.make_async_copy(sg.at[k], sg_hbm.at[k], ssem.at[k]).start()
    for copy in tables_in:
        copy.wait()
    for g in range(GROUPS):
        loads[g].wait()
        unfold(back[g], gz, ub)

        @pl.loop(0, OCT // 2)
        def _(p):
            uv = ub[:, pl.ds(pl.multiple_of(p * PAIR, PAIR), PAIR)]
            for r in range(0, cells, CHUNK):
                res = dot(gy[r : r + CHUNK, :], uv)
                for h in range(2):
                    c = g * OCT + 2 * p + h
                    at = slice(r, r + CHUNK)
                    out[c, at] = (res[:, h * NZ : (h + 1) * NZ] + mix[c, at].astype(F32)).astype(BF)

        part = pl.ds(g * OCT, OCT)
        pltpu.make_async_copy(out.at[part], grad_hbm.at[part], osem.at[g]).start()
    for g in range(GROUPS):
        part = pl.ds(g * OCT, OCT)
        pltpu.make_async_copy(out.at[part], grad_hbm.at[part], osem.at[g]).wait()
    for k in range(KZ):
        pltpu.make_async_copy(sg.at[k], sg_hbm.at[k], ssem.at[k]).wait()


def fused_shards(n, rows, features, cotangent, spectral_weight, pointwise_weight, biases):
    known = tables(rows)
    fy, gy, fx2, gx2, fz, gz = [jnp.asarray(known[i]) for i in (0, 1, 8, 9, 10, 11)]
    cells = rows * NY
    lines = KY * rows
    dma = pltpu.SemaphoreType.DMA
    block = pltpu.VMEM((C, cells, NZ), BF)
    shape = jax.ShapeDtypeStruct
    wide = C * TILE
    swap = pltpu.VMEM((GROUPS, n, rows, GLANES), F32)
    spec = shape((GROUPS, 2 * KX, LANES), F32)
    mix, back, v, d, total = pl.pallas_call(
        functools.partial(heart_kernel, rows, n),
        out_shape=[
            shape((C, cells, NZ), BF), shape((GROUPS, lines, GLANES), BF), spec, spec,
            shape((16, LANES), F32),
        ],
        in_specs=[HBM] * 7 + [VMEM] * 4,
        out_specs=[HBM] + [VMEM] * 4,
        scratch_shapes=[
            block, block, block, pltpu.VMEM((C, cells, NZ), F32),
            pltpu.VMEM((RING, FULL, C), F32), pltpu.VMEM((KZ, FULL, C), BF),
            pltpu.VMEM(fy.shape, BF), pltpu.VMEM(fz.shape, BF),
            pltpu.VMEM(gy.shape, BF), pltpu.VMEM(gz.shape, BF),
            pltpu.VMEM((wide, wide), BF), pltpu.VMEM((wide, wide), F32),
            pltpu.VMEM((2 * lines, OCT * NZ), BF), pltpu.VMEM((KZ, 2 * KX, LANES), F32),
            swap, swap, swap, swap, swap, swap,
            pltpu.VMEM((16, LANES), F32), pltpu.VMEM((n, 16, LANES), F32),
            dma((GROUPS,)), dma((GROUPS,)), dma((4,)), dma((RING,)),
            dma((4, GROUPS)), dma((4, GROUPS)), dma, dma, dma,
        ],
        compiler_params=pltpu.CompilerParams(
            collective_id=1, has_side_effects=True, vmem_limit_bytes=62 << 20
        ),
        name="heart",
    )(
        features.reshape(C, cells, NZ), cotangent.reshape(C, cells, NZ),
        spectral_weight.reshape(KZ, FULL, C), fy, fz, gy, gz, pointwise_weight,
        biases.reshape(1, C), fx2, gx2,
    )
    grad, sg, pwg, bg = pl.pallas_call(
        functools.partial(tail_kernel, rows),
        out_shape=[
            shape((C, cells, NZ), BF), shape((KZ, FULL, C), F32), shape((C, C), F32),
            shape((1, C), F32),
        ],
        in_specs=[HBM] * 3 + [VMEM] * 4,
        out_specs=[HBM, HBM, VMEM, VMEM],
        scratch_shapes=[
            block, block, pltpu.VMEM(gz.shape, BF), pltpu.VMEM(gy.shape, BF),
            pltpu.VMEM((2 * lines, OCT * NZ), BF), pltpu.VMEM((KZ, FULL, C), F32),
            dma((GROUPS,)), dma((2,)), dma((GROUPS,)), dma((KZ,)),
        ],
        compiler_params=pltpu.CompilerParams(vmem_limit_bytes=56 << 20),
        name="tail",
    )(mix, gz, gy, back, v, d, total)
    return (
        grad.reshape(features.shape), sg.reshape(spectral_weight.shape), pwg, bg.reshape(C),
    )


def shards(features, cotangent, spectral_weight, pointwise_weight, biases):
    n = lax.axis_size("mp")
    rows = NX // n
    if n == KY:
        return fused_shards(
            n, rows, features, cotangent, spectral_weight, pointwise_weight, biases
        )
    fy, gy, fz, fz_w, gz, gz_w, fx, gx = [jnp.asarray(t) for t in tables(rows)[:8]]
    cells = rows * NY
    feat = features.reshape(C, cells, NZ)
    cot = cotangent.reshape(C, cells, NZ)
    bias = jnp.repeat(biases, TILE)[:, None]
    spread = jax.ShapeDtypeStruct((KY * rows, 2 * C * KZ), F32)
    whole = jax.ShapeDtypeStruct((C, cells, NZ), BF)
    field = pltpu.VMEM((C, cells, NZ), F32)
    block = pltpu.VMEM((C, cells, NZ), BF)
    wide = C * TILE
    dma = pltpu.SemaphoreType.DMA
    sems = dma((GROUPS,))
    part = call(forward_kernel, rows, [spread], [], (feat, fy, fz), "analysis")[0]
    v_r, v_i = lines_forward(exchange([owner_blocks(part, n, rows)], n, 1)[0], fx)
    w_r, w_i = spectral_weight[:, 0], spectral_weight[:, 1]
    s_r, s_i = v_r[..., None], v_i[..., None]
    u_r = jnp.sum(s_r * w_r - s_i * w_i, axis=2)
    u_i = jnp.sum(s_r * w_i + s_i * w_r, axis=2)
    modes = exchange([lines_back(u_r, u_i, gx, n, rows)], n, 2)[0]
    pg, dpart, sums = call(
        middle_kernel,
        rows,
        [whole, spread, jax.ShapeDtypeStruct((C, LANES), F32)],
        [
            field,
            pltpu.VMEM((wide, wide), F32),
            pltpu.VMEM((wide, NZ), F32),
            pltpu.VMEM((wide, wide), BF),
            block,
            block,
            block,
            sems,
            sems,
            dma,
        ],
        (feat, cot, plane_blocks(modes, n, rows), pointwise_weight, bias, gz_w, gy, fy, fz_w),
        "middle",
        far=(0, 1),
        far_out=(0,),
    )
    d_r, d_i = lines_forward(exchange([owner_blocks(dpart, n, rows)], n, 3)[0], fx)
    e_r, e_i = d_r[:, :, None, :], d_i[:, :, None, :]
    m_r = jnp.sum(e_r * w_r + e_i * w_i, axis=3)
    m_i = jnp.sum(e_i * w_r - e_r * w_i, axis=3)
    packed = jnp.concatenate(
        [sums[:, :C].reshape(-1, LANES), jnp.pad(sums[:, C], (0, LANES - C))[None]], axis=0
    )
    mine = jnp.broadcast_to(packed, (n, *packed.shape))
    back, every = exchange([lines_back(m_r, m_i, gx, n, rows), mine], n, 4)
    total = jnp.sum(every, axis=0)
    first = jnp.stack([v_r, -v_i], axis=1)[..., None]
    second = jnp.stack([v_i, v_r], axis=1)[..., None]
    spectral_grad = first * e_r[:, None] + second * e_i[:, None]
    grad = call(
        last_kernel,
        rows,
        [whole],
        [field, pltpu.VMEM((wide, wide), BF), block, block, sems, dma((SAVES,))],
        (pg, plane_blocks(back, n, rows), pointwise_weight.T, gz, gy),
        "synthesis",
        far=(0,),
        far_out=(0,),
    )[0]
    factor = float(NX * NY * NZ) ** (-0.5)
    total = total * factor
    return (grad.reshape(features.shape), spectral_grad, total[:-1].reshape(C, C), total[-1, :C])


def solution(mesh):
    return jax.shard_map(
        shards,
        mesh=mesh,
        in_specs=(
            P(None, ("groups", "mp"), None, None),
            P(None, ("groups", "mp"), None, None),
            P("mp", None, None, None, None),
            P(),
            P(),
        ),
        out_specs=(
            P(None, ("groups", "mp"), None, None),
            P(("groups", "mp"), None, None, None, None),
            P("groups", None),
            P("groups"),
        ),
        check_vma=False,
    )
```

```python
import functools
import math

import jax
import jax.numpy as jnp
import ml_dtypes
import numpy as np
from jax import lax
from jax.experimental import pallas as pl
from jax.experimental.pallas import tpu as pltpu
from jax.sharding import PartitionSpec as P

C = 32
NX = 128
NY = 128
NZ = 128
KX = 16
KY = 16
KZ = 16
SCALE = 1.0 / (NX * NY * NZ)
OCT = 8
GROUPS = C // OCT
GLANES = 2 * OCT * KZ
LANES = 128
SAVES = 4
BF = jnp.bfloat16
F32 = jnp.float32
precise = lax.Precision.HIGHEST
VMEM = pl.BlockSpec(memory_space=pltpu.VMEM)
HBM = pl.BlockSpec(memory_space=pl.ANY)


def trig(length, mode_count, signed):
    freqs = np.arange(mode_count) - (mode_count // 2 if signed else 0)
    spots = np.arange(length)
    phases = (spots[:, None] * freqs[None, :] % length) * (2.0 * math.pi / length)
    return np.cos(phases), np.sin(phases)


def low(table):
    return np.asarray(table, np.float32).astype(ml_dtypes.bfloat16)


def tables(rows):
    zc, zs = trig(NZ, KZ, False)
    yc, ys = trig(NY, KY, True)
    xc, xs = trig(NX, KX, True)
    wz = np.where(np.arange(KZ) == 0, 1.0, 2.0) * SCALE
    eye = np.eye(rows)
    fy = np.einsum("syj,xw->sjxwy", np.stack([yc, ys]), eye).reshape(2 * KY * rows, rows * NY)
    gy = np.einsum("syj,xw->xysjw", np.stack([yc, -ys]), eye).reshape(rows * NY, 2 * KY * rows)
    zc_low = low(zc).astype(np.float64)
    zs_low = low(zs).astype(np.float64)
    oct_eye = np.eye(OCT)
    block = np.stack([np.stack([zc_low, -zs_low]), np.stack([-zs_low, -zc_low])])
    fz = np.einsum("srzk,ab->aszrbk", block, oct_eye).reshape(OCT * 2 * NZ, 2 * OCT * KZ)
    fz_w = (fz.reshape(-1, KZ) * wz).reshape(fz.shape)
    fy_k = np.einsum("syj,xw->sxjwy", np.stack([yc, ys]), np.eye(2)).reshape(4 * KY, 2 * NY)
    fz_k = np.einsum("srzk,ab->aszrkb", block, oct_eye).reshape(fz.shape)
    back = np.stack([np.stack([zc, zs]), np.stack([-zs, zc])])
    gz = np.einsum("rqzk,ab->rakbqz", back, oct_eye).reshape(2 * OCT * KZ, OCT * 2 * NZ)
    gz_w = (np.einsum("rqzk,ab,k->rakbqz", back, oct_eye, wz)).reshape(gz.shape)
    gz_k = np.einsum("rqzk,ab->rkabqz", back, oct_eye).reshape(gz.shape)
    fx = np.concatenate([xc.T, xs.T], 0).astype(np.float32)
    gx = np.concatenate([xc, xs], 0).astype(np.float32)
    fx2 = np.block([[xc.T, xs.T], [-xs.T, xc.T]]).astype(np.float32)
    gx2 = np.block([[xc, -xs], [xs, xc]]).astype(np.float32)
    return low(fy), low(gy), low(fz), low(fz_w), low(gz), low(gz_w), fx, gx, fx2, gx2, low(fz_k), low(gz_k), low(fy_k)


def dot(a, b):
    return jnp.dot(a, b, preferred_element_type=F32)


def forward_group(src, g, fy, fz, lines):
    parts = []
    for q in range(0, OCT, 2):
        pair = jnp.concatenate([src[g * OCT + q], src[g * OCT + q + 1]], axis=1)
        both = dot(fy[...], pair).astype(BF)
        for h in range(2):
            piece = both[:, h * NZ : (h + 1) * NZ]
            parts += [piece[:lines], piece[lines:]]
    return dot(jnp.concatenate(parts, axis=1), fz[...])


def plane_back(src, gz, gy, out):
    @pl.loop(0, GROUPS)
    def _(g):
        lhs = src[:, pl.ds(pl.multiple_of(g * GLANES, GLANES), GLANES)].astype(BF)
        u = dot(lhs, gz[...]).astype(BF)
        for q in range(0, OCT, 2):
            cols = []
            for h in range(2):
                o = q + h
                cols.append(
                    jnp.concatenate(
                        [u[:, (2 * o + r) * NZ : (2 * o + r + 1) * NZ] for r in range(2)], axis=0
                    )
                )
            res = dot(gy[...], jnp.concatenate(cols, axis=1))
            out[g * OCT + q] = res[:, :NZ]
            out[g * OCT + q + 1] = res[:, NZ:]


def plain_forward(src, fy, fz, out, lines):
    @pl.loop(0, GROUPS)
    def _(g):
        at = pl.multiple_of(g * GLANES, GLANES)
        out[:, pl.ds(at, GLANES)] = forward_group(src, g, fy, fz, lines)


def load_groups(hbm, buf, sems):
    copies = []
    for g in range(GROUPS):
        part = pl.ds(g * OCT, OCT)
        copies.append(pltpu.make_async_copy(hbm.at[part], buf.at[part], sems.at[g]))
        copies[-1].start()
    return copies


def greet(n):
    me = lax.axis_index("mp")

    @pl.loop(1, n)
    def _(s):
        pl.semaphore_signal(
            pltpu.get_barrier_semaphore(),
            inc=1,
            device_id={"mp": lax.rem(me + s, n)},
            device_id_type=pl.DeviceIdType.MESH,
        )


def remote(src, dst, send, recv, peer):
    return pltpu.make_async_remote_copy(
        src_ref=src,
        dst_ref=dst,
        send_sem=send,
        recv_sem=recv,
        device_id={"mp": peer},
        device_id_type=pl.DeviceIdType.MESH,
    )


def forward_kernel(rows, feat, fy, fz, out):
    plain_forward(feat, fy, fz, out, KY * rows)


TILE = 16
STEP = 4


def tile_of(ref, t):
    at = pl.multiple_of(t * TILE, TILE)
    return ref[:, pl.ds(at, TILE), :].reshape(C * TILE, NZ)


def put_tile(ref, t, value):
    at = pl.multiple_of(t * TILE, TILE)
    ref[:, pl.ds(at, TILE), :] = value.reshape(C, TILE, NZ)


def widen(weight):
    n = C * TILE
    row = lax.broadcasted_iota(jnp.int32, (n, C), 0) // TILE
    up = jnp.where(row == lax.broadcasted_iota(jnp.int32, (n, C), 1), 1.0, 0.0).astype(BF)
    left = dot(up, weight).astype(BF)
    full = lax.dot_general(left, up, (((1,), (1,)), ((), ())), preferred_element_type=F32)
    ri = lax.broadcasted_iota(jnp.int32, (n, n), 0)
    ci = lax.broadcasted_iota(jnp.int32, (n, n), 1)
    return jnp.where(ri % TILE == ci % TILE, full, 0.0).astype(BF)


def middle_kernel(
    rows, feat_hbm, cot_hbm, modes, weight, bias, gz, gy, fy, fz, pg_hbm, part, sums,
    field, acc, bacc, kron, feat, cot, pg, fsem, csem, psem,
):
    loads = load_groups(feat_hbm, feat, fsem) + load_groups(cot_hbm, cot, csem)
    kron[...] = widen(weight[...])
    acc[...] = jnp.zeros_like(acc)
    bacc[...] = jnp.zeros_like(bacc)
    plane_back(modes, gz, gy, field)
    for copy in loads:
        copy.wait()

    @pl.loop(0, rows * NY // (STEP * TILE))
    def _(s):
        f = jnp.concatenate([tile_of(feat, STEP * s + h) for h in range(STEP)], axis=1)
        mix = dot(kron[...], f)
        gs = []
        for h in range(STEP):
            t = STEP * s + h
            x = mix[:, h * NZ : (h + 1) * NZ] + tile_of(field, t) + bias[...]
            x2 = x * x
            a = math.sqrt(2.0 / math.pi)
            th = jnp.tanh(x * (a + (a * 0.044715) * x2))
            d = (0.5 + 0.5 * th) * (1.0 + (x * (1.0 - th)) * (a + (3.0 * a * 0.044715) * x2))
            g = (tile_of(cot, t).astype(F32) * d).astype(BF)
            put_tile(pg, t, g)
            gs.append(g)
        bacc[...] += sum(g.astype(F32) for g in gs)
        g = jnp.concatenate(gs, axis=1)
        acc[...] += lax.dot_general(g, f, (((1,), (1,)), ((), ())), preferred_element_type=F32)

    save = pltpu.make_async_copy(pg, pg_hbm, psem)
    save.start()
    size = C * TILE
    ri = lax.broadcasted_iota(jnp.int32, (size, size), 0)
    ci = lax.broadcasted_iota(jnp.int32, (size, size), 1)
    masked = jnp.where(ri % TILE == ci % TILE, acc[...], 0.0)
    rows_sum = jnp.sum(masked.reshape(C, TILE, size), axis=1)
    fold = jnp.where(
        lax.broadcasted_iota(jnp.int32, (size, LANES), 0) // TILE
        == lax.broadcasted_iota(jnp.int32, (size, LANES), 1),
        1.0,
        0.0,
    ).astype(F32)
    pw = jnp.dot(rows_sum, fold, precision=precise, preferred_element_type=F32)
    by_row = jnp.sum(bacc[...].reshape(C, TILE, NZ), axis=1)
    lane = lax.broadcasted_iota(jnp.int32, (C, LANES), 1)
    sums[...] = pw + jnp.where(lane == C, jnp.sum(by_row, axis=1, keepdims=True), 0.0)
    plain_forward(pg, fy, fz, part, KY * rows)
    save.wait()


def last_kernel(rows, pg_hbm, modes, weight, gz, gy, out_hbm, field, kron, pg, out, fsem, osem):
    loads = load_groups(pg_hbm, pg, fsem)
    kron[...] = widen(weight[...])
    plane_back(modes, gz, gy, field)
    for copy in loads:
        copy.wait()
    saves = []
    cells = rows * NY // SAVES
    for piece in range(SAVES):

        @pl.loop(0, cells // (STEP * TILE))
        def _(i):
            s = piece * (cells // (STEP * TILE)) + i
            f = jnp.concatenate([tile_of(pg, STEP * s + h) for h in range(STEP)], axis=1)
            mix = dot(kron[...], f)
            for h in range(STEP):
                t = STEP * s + h
                r = mix[:, h * NZ : (h + 1) * NZ] + tile_of(field, t)
                put_tile(out, t, r.astype(BF))

        at = pl.ds(piece * cells, cells)
        saves.append(pltpu.make_async_copy(out.at[:, at], out_hbm.at[:, at], osem.at[piece]))
        saves[-1].start()
    for copy in saves:
        copy.wait()


def exchange_kernel(n, arrays, *refs):
    me = lax.axis_index("mp")
    greet(n)
    srcs = refs[:arrays]
    dsts = refs[arrays : 2 * arrays]
    send, recv, own = refs[2 * arrays :]
    pl.semaphore_wait(pltpu.get_barrier_semaphore(), n - 1)

    @pl.loop(1, n)
    def _(s):
        peer = lax.rem(me + s, n)
        for i in range(arrays):
            remote(
                srcs[i].at[peer], dsts[i].at[me], send.at[i, peer], recv.at[i, me], peer
            ).start()

    for i in range(arrays):
        mine = pltpu.make_async_copy(srcs[i].at[me], dsts[i].at[me], own.at[i])
        mine.start()
        mine.wait()

    @pl.loop(1, n)
    def _(s):
        peer = lax.rem(me + s, n)
        for i in range(arrays):
            both = remote(
                srcs[i].at[peer], dsts[i].at[peer], send.at[i, peer], recv.at[i, peer], peer
            )
            both.wait_recv()
            both.wait_send()


def exchange(xs, n, cid):
    shapes = [jax.ShapeDtypeStruct(x.shape, x.dtype) for x in xs]
    return pl.pallas_call(
        functools.partial(exchange_kernel, n, len(xs)),
        out_shape=shapes,
        in_specs=[VMEM] * len(xs),
        out_specs=[VMEM] * len(xs),
        scratch_shapes=[
            pltpu.SemaphoreType.DMA((len(xs), n)),
            pltpu.SemaphoreType.DMA((len(xs), n)),
            pltpu.SemaphoreType.DMA((len(xs),)),
        ],
        compiler_params=pltpu.CompilerParams(
            collective_id=cid, has_side_effects=True, vmem_limit_bytes=16 << 20
        ),
        name=f"exchange{cid}",
    )(*xs)


def call(kernel, rows, outs, scratch, args, name, far=(), far_out=(), cid=None):
    outs = list(outs)
    params = {} if cid is None else {"collective_id": cid, "has_side_effects": True}
    return pl.pallas_call(
        functools.partial(kernel, rows),
        out_shape=outs,
        in_specs=[HBM if i in far else VMEM for i in range(len(args))],
        out_specs=[HBM if i in far_out else VMEM for i in range(len(outs))],
        scratch_shapes=scratch,
        compiler_params=pltpu.CompilerParams(vmem_limit_bytes=60 << 20, **params),
        name=name,
    )(*args)


def owner_blocks(part, n, rows):
    subs = n // KY
    if subs > 1:
        v = part.reshape(KY, rows, 2 * C, subs, KZ // subs)
        part = jnp.transpose(v, (0, 3, 1, 2, 4))
    return part.reshape(n, rows, 2 * C * KZ // subs)


def plane_blocks(got, n, rows):
    subs = n // KY
    if subs > 1:
        v = got.reshape(KY, subs, rows, 2 * C, KZ // subs)
        got = jnp.transpose(v, (0, 2, 3, 1, 4))
    return got.reshape(KY * rows, 2 * C * KZ)


def lines_forward(g, fx):
    g = g.reshape(NX, -1)
    t = jnp.einsum("qx,xl->ql", fx, g, precision=precise).reshape(2, KX, GROUPS, 2, OCT, -1)
    real = t[0, :, :, 0] + t[1, :, :, 1]
    imag = t[0, :, :, 1] - t[1, :, :, 0]
    real, imag = (jnp.transpose(v.reshape(KX, C, -1), (2, 0, 1)) for v in (real, imag))
    return real, imag


def lines_back(real, imag, gx, n, rows):
    u = jnp.stack([real, imag]).reshape(2, real.shape[0], KX, GROUPS, OCT)
    u = jnp.transpose(u, (2, 3, 0, 4, 1)).reshape(KX, -1)
    b = jnp.einsum("qa,al->ql", gx, u, precision=precise).reshape(2, NX, GROUPS, 2, -1)
    lines = jnp.stack([b[0, :, :, 0] - b[1, :, :, 1], b[0, :, :, 1] + b[1, :, :, 0]], 2)
    return lines.reshape(n, rows, -1)


HALF = OCT * KZ
FULL = 2 * KX * C
ONE = 1.0 / SCALE
RING = 8
EIGHT = 8
BATCH = 16
PAIR = 2 * NZ
DUO = 2 * NY
SUB = 128
ROOT = math.sqrt(2.0 / math.pi)


def sharp(a, b):
    return jnp.dot(a, b, precision=precise, preferred_element_type=F32)


def lane_weight():
    k = lax.broadcasted_iota(jnp.int32, (1, GLANES), 1) % HALF // OCT
    return jnp.where(k == 0, SCALE, 2.0 * SCALE)


def send_group(n, turn, g, src, dst, send, recv):
    me = lax.axis_index("mp")

    @pl.loop(1, n)
    def _(s):
        peer = lax.rem(me + s, n)
        remote(src.at[g, peer], dst.at[g, me], send.at[turn, g], recv.at[turn, g], peer).start()

    pltpu.make_async_copy(src.at[g, me], dst.at[g, me], recv.at[turn, g]).start()


def wait_bytes(ref, sem):
    pltpu.make_async_copy(ref, ref, sem).wait()


def wait_sent(n, turn, g, src, send):
    wait_bytes(src.at[g, pl.ds(0, n - 1)], send.at[turn, g])


def spectrum(dst, g, fx2):
    pair = [dst[g, :, :, r * HALF : (r + 1) * HALF].reshape(NX, HALF) for r in range(2)]
    return sharp(fx2[...], jnp.concatenate(pair, axis=0))


def gather_channels(parts, k):
    lane = lax.broadcasted_iota(jnp.int32, (2 * KX, LANES), 1) // OCT
    out = jnp.zeros((2 * KX, LANES), F32)
    for g in range(GROUPS):
        shift = (g * OCT - k * OCT) % LANES
        moved = pltpu.roll(parts[g], shift, 1) if shift else parts[g]
        out = jnp.where(lane == g, moved, out)
    return out


def fill_lanes(v):
    v = v + pltpu.roll(v, C, 1)
    return v + pltpu.roll(v, 2 * C, 1)


def own_mode(m):
    row = lax.broadcasted_iota(jnp.int32, (2 * KX, LANES), 0) % KX
    lane = lax.broadcasted_iota(jnp.int32, (2 * KX, LANES), 1) // C
    return row == m * (LANES // C) + lane


def diagonal(spread):
    turned = jnp.concatenate([-spread[KX:], spread[:KX]], axis=0)
    blocks = [jnp.where(own_mode(m), v, 0.0) for v in (spread, turned) for m in range(KX * C // LANES)]
    return jnp.concatenate(blocks, axis=1)


def put_channels(parts, k, v):
    lane = lax.broadcasted_iota(jnp.int32, (2 * KX, LANES), 1) // OCT
    for g in range(GROUPS):
        shift = (k * OCT - g * OCT) % LANES
        moved = pltpu.roll(v, shift, 1) if shift else v
        parts[g] = jnp.where(lane == k, moved, parts[g])


def lines_out(parts, gx2, src, n):
    for g in range(GROUPS):
        both = sharp(gx2[...], parts[g])
        for r in range(2):
            src[g, :, :, r * HALF : (r + 1) * HALF] = both[r * NX : (r + 1) * NX].reshape(
                n, NX // n, HALF
            )


def halves(ref, t):
    v = tile_of(ref, t).reshape(C, TILE, NZ).astype(F32)
    return [
        v[:, w * EIGHT : (w + 1) * EIGHT].reshape(C * EIGHT, NZ).astype(BF)
        for w in range(TILE // EIGHT)
    ]


def batch_of(ref, s):
    return jnp.concatenate([v for h in range(BATCH) for v in halves(ref, BATCH * s + h)], axis=1)


def unbatch(mix, h):
    return [
        mix[:, (2 * h + w) * NZ : (2 * h + w + 1) * NZ].reshape(C, EIGHT, NZ) for w in range(2)
    ]


def widen_with(weight, turn):
    n = C * EIGHT
    row = lax.broadcasted_iota(jnp.int32, (n, C), 0) // EIGHT
    up = jnp.where(row == lax.broadcasted_iota(jnp.int32, (n, C), 1), 1.0, 0.0).astype(BF)
    dims = (((1,), (1 if turn else 0,)), ((), ()))
    left = lax.dot_general(up, weight, dims, preferred_element_type=F32).astype(BF)
    full = lax.dot_general(left, up, (((1,), (1,)), ((), ())), preferred_element_type=F32)
    ri = lax.broadcasted_iota(jnp.int32, (n, n), 0)
    ci = lax.broadcasted_iota(jnp.int32, (n, n), 1)
    return jnp.where(ri % EIGHT == ci % EIGHT, full, 0.0).astype(BF)


def slope(x):
    x2 = x * x
    th = jnp.tanh(x * (ROOT + (ROOT * 0.044715) * x2))
    return (1.0 + th) * (0.5 + (1.0 - th) * (x * (0.5 * ROOT + (1.5 * ROOT * 0.044715) * x2)))


def fold_pair(outs):
    parts = []
    for h in range(2):
        for s in range(2):
            rows = [
                o[s * 2 * KY : (s + 1) * 2 * KY, h * NZ : (h + 1) * NZ] for o in outs
            ]
            parts.append(jnp.concatenate(rows, axis=0))
    return parts


def put_plane(parts, fz, weight, tmp, src, g, rows):
    res = dot(jnp.concatenate(parts, axis=1), fz[...])
    if weight is not None:
        res = res * weight
    for r in range(2):
        tmp[r] = res[:, r * HALF : (r + 1) * HALF]
    for j in range(KY):
        for r in range(2):
            src[g, j, :, r * HALF : (r + 1) * HALF] = tmp[r, pl.ds(j, rows, stride=KY), :]


def unfold(lhs, gz, ub):
    lines = lhs.shape[0]
    u = dot(lhs, gz[...]).astype(BF)
    for q in range(OCT):
        for r in range(2):
            at = (2 * q + r) * NZ
            ub[r * lines : (r + 1) * lines, q * NZ : (q + 1) * NZ] = u[:, at : at + NZ]


def heart_kernel(
    rows, n, feat_hbm, cot_hbm, w_hbm, fy_hbm, fz_hbm, gy_hbm, gz_hbm, weight, bias, fx2, gx2,
    mix_hbm, back, vout, dout, total,
    feat, cot, pg, field, ring, wb, fy, fz, gy, gz, kron, acc, ub, stage, src_a, src_b,
    dst_1, dst_2, dst_3, dst_4, sums, every, tmp, fsem, csem, tsem, wsem, send, recv, ssem, rsem, osem,
):
    me = lax.axis_index("mp")
    cells = rows * NY
    lines = KY * rows
    steps = cells // (BATCH * TILE)
    duos = cells // DUO
    greet(n)
    early = [pltpu.make_async_copy(a, b, tsem.at[i]) for i, (a, b) in enumerate(((fy_hbm, fy), (fz_hbm, fz)))]
    late = [pltpu.make_async_copy(a, b, tsem.at[2 + i]) for i, (a, b) in enumerate(((gy_hbm, gy), (gz_hbm, gz)))]

    def feat_copy(g):
        part = pl.ds(g * OCT, OCT)
        return pltpu.make_async_copy(feat_hbm.at[part], feat.at[part], fsem.at[g])

    def cot_copy(g):
        part = pl.ds(g * OCT, OCT)
        return pltpu.make_async_copy(cot_hbm.at[part], cot.at[part], csem.at[g])

    def ring_copy(k, slot):
        return pltpu.make_async_copy(w_hbm.at[k], ring.at[slot], wsem.at[slot])

    for copy in early:
        copy.start()
    for g in range(GROUPS):
        feat_copy(g).start()
    for copy in early:
        copy.wait()

    @pl.loop(0, GROUPS)
    def _(g):
        feat_copy(g).wait()
        parts = []
        for q in range(0, OCT, 2):
            c = g * OCT + q
            outs = []
            for x in range(duos):
                at = slice(x * DUO, (x + 1) * DUO)
                both = jnp.concatenate([feat[c, at], feat[c + 1, at]], axis=1)
                outs.append(dot(fy[...], both).astype(BF))
            parts += fold_pair(outs)
        put_plane(parts, fz, None, tmp, src_a, g, rows)

        @pl.when(g == 0)
        def _():
            pl.semaphore_wait(pltpu.get_barrier_semaphore(), n - 1)

        send_group(n, 0, g, src_a, dst_1, send, recv)

    for k in range(RING):
        ring_copy(k, k).start()
    for copy in late:
        copy.start()
    for g in range(GROUPS):
        cot_copy(g).start()

    kron[...] = widen_with(weight[...], False)
    size = C * EIGHT
    row = lax.broadcasted_iota(jnp.int32, (size, C), 0) // EIGHT
    column = jnp.where(row == lax.broadcasted_iota(jnp.int32, (size, C), 1), bias[...], 0.0)
    shift = jnp.sum(column, axis=1, keepdims=True)

    @pl.loop(0, steps)
    def _(s):
        mix = dot(kron[...], batch_of(feat, s)) + shift
        for h in range(BATCH):
            at = pl.multiple_of((BATCH * s + h) * TILE, TILE)
            for w, v in enumerate(unbatch(mix, h)):
                field[:, pl.ds(at + w * EIGHT, EIGHT), :] = v

    @pl.loop(0, KZ // RING)
    def _(i):
        for slot in range(RING):
            k = i * RING + slot
            ring_copy(k, slot).wait()
            wb[k] = ring[slot].astype(BF)

            @pl.when(k + RING < KZ)
            def _():
                ring_copy(k + RING, slot).start()

    for g in range(GROUPS):
        wait_bytes(dst_1.at[g], recv.at[0, g])
        vout[g] = spectrum(dst_1, g, fx2)
    parts = [vout[g] for g in range(GROUPS)]
    mixed = [jnp.zeros((2 * KX, LANES), F32) for _ in range(GROUPS)]
    for k in range(KZ):
        left = diagonal(fill_lanes(gather_channels(parts, k))).astype(BF)
        stage[k, :, :C] = dot(left, wb[k])
    for k in range(KZ):
        put_channels(mixed, k, stage[k])
    lines_out(mixed, gx2, src_b, n)
    for g in range(GROUPS):
        send_group(n, 1, g, src_b, dst_2, send, recv)
    for copy in late:
        copy.wait()
    for g in range(GROUPS):
        wait_sent(n, 0, g, src_a, send)
        cot_copy(g).wait()

    @pl.loop(0, GROUPS)
    def _(g):
        wait_bytes(dst_2.at[g], recv.at[1, g])
        lhs = (dst_2[g].reshape(lines, GLANES) * lane_weight()).astype(BF)
        unfold(lhs, gz, ub)

        parts = []
        for p in range(OCT // 2):
            uv = ub[:, p * PAIR : (p + 1) * PAIR]
            outs = []
            for d in range(duos):
                res = dot(gy[d * DUO : (d + 1) * DUO, :], uv)
                new = []
                for h in range(2):
                    c = g * OCT + 2 * p + h
                    pieces = []
                    for t in range(0, DUO, SUB):
                        at = slice(d * DUO + t, d * DUO + t + SUB)
                        x = res[t : t + SUB, h * NZ : (h + 1) * NZ] + field[c, at]
                        v = (cot[c, at].astype(F32) * slope(x)).astype(BF)
                        pg[c, at] = v
                        pieces.append(v)
                    new.append(jnp.concatenate(pieces, axis=0))
                outs.append(dot(fy[...], jnp.concatenate(new, axis=1)).astype(BF))
            parts += fold_pair(outs)
        put_plane(parts, fz, lane_weight(), tmp, src_a, g, rows)
        send_group(n, 2, g, src_a, dst_3, send, recv)

    acc[...] = jnp.zeros_like(acc)

    @pl.loop(0, steps)
    def _(s):
        acc[...] += lax.dot_general(
            batch_of(pg, s), batch_of(feat, s), (((1,), (1,)), ((), ())),
            preferred_element_type=F32,
        )

    ri = lax.broadcasted_iota(jnp.int32, (size, size), 0)
    ci = lax.broadcasted_iota(jnp.int32, (size, size), 1)
    masked = jnp.where(ri % EIGHT == ci % EIGHT, acc[...], 0.0)
    rows_sum = jnp.sum(masked.reshape(C, EIGHT, size), axis=1)
    fold = jnp.where(
        lax.broadcasted_iota(jnp.int32, (size, LANES), 0) // EIGHT
        == lax.broadcasted_iota(jnp.int32, (size, LANES), 1),
        1.0,
        0.0,
    ).astype(F32)
    pw = sharp(rows_sum, fold)
    packed = pw[:8]
    for i in range(1, C // 8):
        packed = packed + pltpu.roll(pw[8 * i : 8 * i + 8], i * C, 1)
    sums[:8] = packed
    kron[...] = widen_with(weight[...], True)

    for g in range(GROUPS):
        wait_bytes(dst_3.at[g], recv.at[2, g])
        dout[g] = spectrum(dst_3, g, fx2)
    parts = [dout[g] for g in range(GROUPS)]
    dc = jnp.zeros((1, LANES), F32)
    lane = lax.broadcasted_iota(jnp.int32, (1, LANES), 1)
    for g in range(GROUPS):
        v = parts[g][KX // 2 : KX // 2 + 1]
        v = pltpu.roll(v, g * OCT, 1) if g else v
        dc = jnp.where(lane // OCT == g, v * ONE, dc)
    owner = jnp.where(me == KY // 2, 1.0, 0.0)
    first = lax.broadcasted_iota(jnp.int32, (8, LANES), 0) == 0
    sums[8:] = jnp.where(first, dc * owner, 0.0)
    mixed = [jnp.zeros((2 * KX, LANES), F32) for _ in range(GROUPS)]
    half = KX * C
    for k in range(KZ):
        d = gather_channels(parts, k)[:, :C].astype(BF)
        full = lax.dot_general(d, wb[k], (((1,), (1,)), ((), ())), preferred_element_type=F32)
        a0 = jnp.zeros((2 * KX, LANES), F32)
        a1 = a0
        for m in range(half // LANES):
            own = own_mode(m)
            a0 = a0 + jnp.where(own, full[:, m * LANES : (m + 1) * LANES], 0.0)
            a1 = a1 + jnp.where(own, full[:, half + m * LANES : half + (m + 1) * LANES], 0.0)
        both = a0 + jnp.concatenate([a1[KX:], -a1[:KX]], axis=0)
        put_channels(mixed, k, fill_lanes(both))
    for g in range(GROUPS):
        wait_sent(n, 1, g, src_b, send)
    lines_out(mixed, gx2, src_b, n)
    for g in range(GROUPS):
        send_group(n, 3, g, src_b, dst_4, send, recv)

    @pl.loop(1, n)
    def _(s):
        peer = lax.rem(me + s, n)
        remote(sums, every.at[me], ssem, rsem, peer).start()

    pltpu.make_async_copy(sums, every.at[me], rsem).start()

    @pl.loop(0, steps)
    def _(s):
        mix = dot(kron[...], batch_of(pg, s))
        for h in range(BATCH):
            both = jnp.concatenate(unbatch(mix, h), axis=1).astype(BF)
            put_tile(cot, BATCH * s + h, both.reshape(C * TILE, NZ))

    save = pltpu.make_async_copy(cot, mix_hbm, osem)
    save.start()
    for g in range(GROUPS):
        wait_bytes(dst_4.at[g], recv.at[3, g])
        back[g] = dst_4[g].reshape(lines, GLANES).astype(BF)
    wait_bytes(every, rsem)
    total[...] = jnp.sum(every[...], axis=0) * float(NX * NY * NZ) ** (-0.5)
    wait_bytes(every.at[pl.ds(0, n - 1)], ssem)
    for g in range(GROUPS):
        wait_sent(n, 2, g, src_a, send)
        wait_sent(n, 3, g, src_b, send)
    save.wait()


def tail_kernel(
    rows, mix_hbm, gz_hbm, gy_hbm, back, v, d, total, grad_hbm, sg_hbm, pwg, bg,
    mix, out, gz, gy, ub, sg, msem, tsem, osem, ssem,
):
    cells = rows * NY
    tables_in = [pltpu.make_async_copy(a, b, tsem.at[i]) for i, (a, b) in enumerate(((gz_hbm, gz), (gy_hbm, gy)))]
    for copy in tables_in:
        copy.start()
    loads = load_groups(mix_hbm, mix, msem)
    t = total[...]
    for i in range(C // 8):
        part = pltpu.roll(t[:8], LANES - i * C, 1) if i else t[:8]
        pwg[8 * i : 8 * i + 8, :] = part[:, :C]
    bg[...] = t[8:9, :C]
    vs = [v[g] for g in range(GROUPS)]
    ds = [d[g] for g in range(GROUPS)]
    for k in range(KZ):
        left = diagonal(fill_lanes(gather_channels(vs, k))).astype(BF)
        side = gather_channels(ds, k)[:, :C].astype(BF)
        sg[k] = lax.dot_general(left, side, (((0,), (0,)), ((), ())), preferred_element_type=F32)
        pltpu.make_async_copy(sg.at[k], sg_hbm.at[k], ssem.at[k]).start()
    for copy in tables_in:
        copy.wait()
    for g in range(GROUPS):
        loads[g].wait()
        unfold(back[g], gz, ub)

        for p in range(OCT // 2):
            uv = ub[:, p * PAIR : (p + 1) * PAIR]
            for r in range(0, cells, DUO):
                res = dot(gy[r : r + DUO, :], uv)
                for h in range(2):
                    c = g * OCT + 2 * p + h
                    at = slice(r, r + DUO)
                    out[c, at] = (res[:, h * NZ : (h + 1) * NZ] + mix[c, at].astype(F32)).astype(BF)

        part = pl.ds(g * OCT, OCT)
        pltpu.make_async_copy(out.at[part], grad_hbm.at[part], osem.at[g]).start()
    for g in range(GROUPS):
        part = pl.ds(g * OCT, OCT)
        pltpu.make_async_copy(out.at[part], grad_hbm.at[part], osem.at[g]).wait()
    for k in range(KZ):
        pltpu.make_async_copy(sg.at[k], sg_hbm.at[k], ssem.at[k]).wait()


def fused_shards(n, rows, features, cotangent, spectral_weight, pointwise_weight, biases):
    known = tables(rows)
    gy, fx2, gx2, fz, gz, fy = [jnp.asarray(known[i]) for i in (1, 8, 9, 10, 11, 12)]
    cells = rows * NY
    lines = KY * rows
    dma = pltpu.SemaphoreType.DMA
    block = pltpu.VMEM((C, cells, NZ), BF)
    shape = jax.ShapeDtypeStruct
    wide = C * EIGHT
    swap = pltpu.VMEM((GROUPS, n, rows, GLANES), F32)
    spec = shape((GROUPS, 2 * KX, LANES), F32)
    mix, back, v, d, total = pl.pallas_call(
        functools.partial(heart_kernel, rows, n),
        out_shape=[
            shape((C, cells, NZ), BF), shape((GROUPS, lines, GLANES), BF), spec, spec,
            shape((16, LANES), F32),
        ],
        in_specs=[HBM] * 7 + [VMEM] * 4,
        out_specs=[HBM] + [VMEM] * 4,
        scratch_shapes=[
            block, block, block, pltpu.VMEM((C, cells, NZ), F32),
            pltpu.VMEM((RING, FULL, C), F32), pltpu.VMEM((KZ, FULL, C), BF),
            pltpu.VMEM(fy.shape, BF), pltpu.VMEM(fz.shape, BF),
            pltpu.VMEM(gy.shape, BF), pltpu.VMEM(gz.shape, BF),
            pltpu.VMEM((wide, wide), BF), pltpu.VMEM((wide, wide), F32),
            pltpu.VMEM((2 * lines, OCT * NZ), BF), pltpu.VMEM((KZ, 2 * KX, LANES), F32),
            swap, swap, swap, swap, swap, swap,
            pltpu.VMEM((16, LANES), F32), pltpu.VMEM((n, 16, LANES), F32),
            pltpu.VMEM((2, lines, LANES), F32),
            dma((GROUPS,)), dma((GROUPS,)), dma((4,)), dma((RING,)),
            dma((4, GROUPS)), dma((4, GROUPS)), dma, dma, dma,
        ],
        compiler_params=pltpu.CompilerParams(
            collective_id=1, has_side_effects=True, vmem_limit_bytes=62 << 20
        ),
        name="heart",
    )(
        features.reshape(C, cells, NZ), cotangent.reshape(C, cells, NZ),
        spectral_weight.reshape(KZ, FULL, C), fy, fz, gy, gz, pointwise_weight,
        biases.reshape(1, C), fx2, gx2,
    )
    grad, sg, pwg, bg = pl.pallas_call(
        functools.partial(tail_kernel, rows),
        out_shape=[
            shape((C, cells, NZ), BF), shape((KZ, FULL, C), F32), shape((C, C), F32),
            shape((1, C), F32),
        ],
        in_specs=[HBM] * 3 + [VMEM] * 4,
        out_specs=[HBM, HBM, VMEM, VMEM],
        scratch_shapes=[
            block, block, pltpu.VMEM(gz.shape, BF), pltpu.VMEM(gy.shape, BF),
            pltpu.VMEM((2 * lines, OCT * NZ), BF), pltpu.VMEM((KZ, FULL, C), F32),
            dma((GROUPS,)), dma((2,)), dma((GROUPS,)), dma((KZ,)),
        ],
        compiler_params=pltpu.CompilerParams(vmem_limit_bytes=56 << 20),
        name="tail",
    )(mix, gz, gy, back, v, d, total)
    return (
        grad.reshape(features.shape), sg.reshape(spectral_weight.shape), pwg, bg.reshape(C),
    )


def shards(features, cotangent, spectral_weight, pointwise_weight, biases):
    n = lax.axis_size("mp")
    rows = NX // n
    if n == KY:
        return fused_shards(
            n, rows, features, cotangent, spectral_weight, pointwise_weight, biases
        )
    fy, gy, fz, fz_w, gz, gz_w, fx, gx = [jnp.asarray(t) for t in tables(rows)[:8]]
    cells = rows * NY
    feat = features.reshape(C, cells, NZ)
    cot = cotangent.reshape(C, cells, NZ)
    bias = jnp.repeat(biases, TILE)[:, None]
    spread = jax.ShapeDtypeStruct((KY * rows, 2 * C * KZ), F32)
    whole = jax.ShapeDtypeStruct((C, cells, NZ), BF)
    field = pltpu.VMEM((C, cells, NZ), F32)
    block = pltpu.VMEM((C, cells, NZ), BF)
    wide = C * TILE
    dma = pltpu.SemaphoreType.DMA
    sems = dma((GROUPS,))
    part = call(forward_kernel, rows, [spread], [], (feat, fy, fz), "analysis")[0]
    v_r, v_i = lines_forward(exchange([owner_blocks(part, n, rows)], n, 1)[0], fx)
    w_r, w_i = spectral_weight[:, 0], spectral_weight[:, 1]
    s_r, s_i = v_r[..., None], v_i[..., None]
    u_r = jnp.sum(s_r * w_r - s_i * w_i, axis=2)
    u_i = jnp.sum(s_r * w_i + s_i * w_r, axis=2)
    modes = exchange([lines_back(u_r, u_i, gx, n, rows)], n, 2)[0]
    pg, dpart, sums = call(
        middle_kernel,
        rows,
        [whole, spread, jax.ShapeDtypeStruct((C, LANES), F32)],
        [
            field,
            pltpu.VMEM((wide, wide), F32),
            pltpu.VMEM((wide, NZ), F32),
            pltpu.VMEM((wide, wide), BF),
            block,
            block,
            block,
            sems,
            sems,
            dma,
        ],
        (feat, cot, plane_blocks(modes, n, rows), pointwise_weight, bias, gz_w, gy, fy, fz_w),
        "middle",
        far=(0, 1),
        far_out=(0,),
    )
    d_r, d_i = lines_forward(exchange([owner_blocks(dpart, n, rows)], n, 3)[0], fx)
    e_r, e_i = d_r[:, :, None, :], d_i[:, :, None, :]
    m_r = jnp.sum(e_r * w_r + e_i * w_i, axis=3)
    m_i = jnp.sum(e_i * w_r - e_r * w_i, axis=3)
    packed = jnp.concatenate(
        [sums[:, :C].reshape(-1, LANES), jnp.pad(sums[:, C], (0, LANES - C))[None]], axis=0
    )
    mine = jnp.broadcast_to(packed, (n, *packed.shape))
    back, every = exchange([lines_back(m_r, m_i, gx, n, rows), mine], n, 4)
    total = jnp.sum(every, axis=0)
    first = jnp.stack([v_r, -v_i], axis=1)[..., None]
    second = jnp.stack([v_i, v_r], axis=1)[..., None]
    spectral_grad = first * e_r[:, None] + second * e_i[:, None]
    grad = call(
        last_kernel,
        rows,
        [whole],
        [field, pltpu.VMEM((wide, wide), BF), block, block, sems, dma((SAVES,))],
        (pg, plane_blocks(back, n, rows), pointwise_weight.T, gz, gy),
        "synthesis",
        far=(0,),
        far_out=(0,),
    )[0]
    factor = float(NX * NY * NZ) ** (-0.5)
    total = total * factor
    return (grad.reshape(features.shape), spectral_grad, total[:-1].reshape(C, C), total[-1, :C])


def solution(mesh):
    return jax.shard_map(
        shards,
        mesh=mesh,
        in_specs=(
            P(None, ("groups", "mp"), None, None),
            P(None, ("groups", "mp"), None, None),
            P("mp", None, None, None, None),
            P(),
            P(),
        ),
        out_specs=(
            P(None, ("groups", "mp"), None, None),
            P(("groups", "mp"), None, None, None, None),
            P("groups", None),
            P("groups"),
        ),
        check_vma=False,
    )
```

```python
import functools
import math

import jax
import jax.numpy as jnp
import ml_dtypes
import numpy as np
from jax import lax
from jax.experimental import pallas as pl
from jax.experimental.pallas import tpu as pltpu
from jax.sharding import PartitionSpec as P

C = 32
NX = 128
NY = 128
NZ = 128
KX = 16
KY = 16
KZ = 16
SCALE = 1.0 / (NX * NY * NZ)
OCT = 8
GROUPS = C // OCT
GLANES = 2 * OCT * KZ
LANES = 128
SAVES = 4
BF = jnp.bfloat16
F32 = jnp.float32
precise = lax.Precision.HIGHEST
VMEM = pl.BlockSpec(memory_space=pltpu.VMEM)
HBM = pl.BlockSpec(memory_space=pl.ANY)


def trig(length, mode_count, signed):
    freqs = np.arange(mode_count) - (mode_count // 2 if signed else 0)
    spots = np.arange(length)
    phases = (spots[:, None] * freqs[None, :] % length) * (2.0 * math.pi / length)
    return np.cos(phases), np.sin(phases)


def low(table):
    return np.asarray(table, np.float32).astype(ml_dtypes.bfloat16)


def tables(rows):
    zc, zs = trig(NZ, KZ, False)
    yc, ys = trig(NY, KY, True)
    xc, xs = trig(NX, KX, True)
    wz = np.where(np.arange(KZ) == 0, 1.0, 2.0) * SCALE
    eye = np.eye(rows)
    fy = np.einsum("syj,xw->sjxwy", np.stack([yc, ys]), eye).reshape(2 * KY * rows, rows * NY)
    gy = np.einsum("syj,xw->xysjw", np.stack([yc, -ys]), eye).reshape(rows * NY, 2 * KY * rows)
    zc_low = low(zc).astype(np.float64)
    zs_low = low(zs).astype(np.float64)
    oct_eye = np.eye(OCT)
    block = np.stack([np.stack([zc_low, -zs_low]), np.stack([-zs_low, -zc_low])])
    fz = np.einsum("srzk,ab->aszrbk", block, oct_eye).reshape(OCT * 2 * NZ, 2 * OCT * KZ)
    fz_w = (fz.reshape(-1, KZ) * wz).reshape(fz.shape)
    fy_k = np.einsum("syj,xw->sxjwy", np.stack([yc, ys]), np.eye(2)).reshape(4 * KY, 2 * NY)
    fz_k = np.einsum("srzk,ab->aszrkb", block, oct_eye).reshape(fz.shape)
    back = np.stack([np.stack([zc, zs]), np.stack([-zs, zc])])
    gz = np.einsum("rqzk,ab->rakbqz", back, oct_eye).reshape(2 * OCT * KZ, OCT * 2 * NZ)
    gz_w = (np.einsum("rqzk,ab,k->rakbqz", back, oct_eye, wz)).reshape(gz.shape)
    gz_k = np.einsum("rqzk,ab->rkabqz", back, oct_eye).reshape(gz.shape)
    fx = np.concatenate([xc.T, xs.T], 0).astype(np.float32)
    gx = np.concatenate([xc, xs], 0).astype(np.float32)
    fx2 = np.block([[xc.T, xs.T], [-xs.T, xc.T]]).astype(np.float32)
    gx2 = np.block([[xc, -xs], [xs, xc]]).astype(np.float32)
    return low(fy), low(gy), low(fz), low(fz_w), low(gz), low(gz_w), fx, gx, fx2, gx2, low(fz_k), low(gz_k), low(fy_k)


def dot(a, b):
    return jnp.dot(a, b, preferred_element_type=F32)


def forward_group(src, g, fy, fz, lines):
    parts = []
    for q in range(0, OCT, 2):
        pair = jnp.concatenate([src[g * OCT + q], src[g * OCT + q + 1]], axis=1)
        both = dot(fy[...], pair).astype(BF)
        for h in range(2):
            piece = both[:, h * NZ : (h + 1) * NZ]
            parts += [piece[:lines], piece[lines:]]
    return dot(jnp.concatenate(parts, axis=1), fz[...])


def plane_back(src, gz, gy, out):
    @pl.loop(0, GROUPS)
    def _(g):
        lhs = src[:, pl.ds(pl.multiple_of(g * GLANES, GLANES), GLANES)].astype(BF)
        u = dot(lhs, gz[...]).astype(BF)
        for q in range(0, OCT, 2):
            cols = []
            for h in range(2):
                o = q + h
                cols.append(
                    jnp.concatenate(
                        [u[:, (2 * o + r) * NZ : (2 * o + r + 1) * NZ] for r in range(2)], axis=0
                    )
                )
            res = dot(gy[...], jnp.concatenate(cols, axis=1))
            out[g * OCT + q] = res[:, :NZ]
            out[g * OCT + q + 1] = res[:, NZ:]


def plain_forward(src, fy, fz, out, lines):
    @pl.loop(0, GROUPS)
    def _(g):
        at = pl.multiple_of(g * GLANES, GLANES)
        out[:, pl.ds(at, GLANES)] = forward_group(src, g, fy, fz, lines)


def load_groups(hbm, buf, sems):
    copies = []
    for g in range(GROUPS):
        part = pl.ds(g * OCT, OCT)
        copies.append(pltpu.make_async_copy(hbm.at[part], buf.at[part], sems.at[g]))
        copies[-1].start()
    return copies


def greet(n):
    me = lax.axis_index("mp")

    @pl.loop(1, n)
    def _(s):
        pl.semaphore_signal(
            pltpu.get_barrier_semaphore(),
            inc=1,
            device_id={"mp": lax.rem(me + s, n)},
            device_id_type=pl.DeviceIdType.MESH,
        )


def remote(src, dst, send, recv, peer):
    return pltpu.make_async_remote_copy(
        src_ref=src,
        dst_ref=dst,
        send_sem=send,
        recv_sem=recv,
        device_id={"mp": peer},
        device_id_type=pl.DeviceIdType.MESH,
    )


def forward_kernel(rows, feat, fy, fz, out):
    plain_forward(feat, fy, fz, out, KY * rows)


TILE = 16
STEP = 4


def tile_of(ref, t):
    at = pl.multiple_of(t * TILE, TILE)
    return ref[:, pl.ds(at, TILE), :].reshape(C * TILE, NZ)


def put_tile(ref, t, value):
    at = pl.multiple_of(t * TILE, TILE)
    ref[:, pl.ds(at, TILE), :] = value.reshape(C, TILE, NZ)


def widen(weight):
    n = C * TILE
    row = lax.broadcasted_iota(jnp.int32, (n, C), 0) // TILE
    up = jnp.where(row == lax.broadcasted_iota(jnp.int32, (n, C), 1), 1.0, 0.0).astype(BF)
    left = dot(up, weight).astype(BF)
    full = lax.dot_general(left, up, (((1,), (1,)), ((), ())), preferred_element_type=F32)
    ri = lax.broadcasted_iota(jnp.int32, (n, n), 0)
    ci = lax.broadcasted_iota(jnp.int32, (n, n), 1)
    return jnp.where(ri % TILE == ci % TILE, full, 0.0).astype(BF)


def middle_kernel(
    rows, feat_hbm, cot_hbm, modes, weight, bias, gz, gy, fy, fz, pg_hbm, part, sums,
    field, acc, bacc, kron, feat, cot, pg, fsem, csem, psem,
):
    loads = load_groups(feat_hbm, feat, fsem) + load_groups(cot_hbm, cot, csem)
    kron[...] = widen(weight[...])
    acc[...] = jnp.zeros_like(acc)
    bacc[...] = jnp.zeros_like(bacc)
    plane_back(modes, gz, gy, field)
    for copy in loads:
        copy.wait()

    @pl.loop(0, rows * NY // (STEP * TILE))
    def _(s):
        f = jnp.concatenate([tile_of(feat, STEP * s + h) for h in range(STEP)], axis=1)
        mix = dot(kron[...], f)
        gs = []
        for h in range(STEP):
            t = STEP * s + h
            x = mix[:, h * NZ : (h + 1) * NZ] + tile_of(field, t) + bias[...]
            x2 = x * x
            a = math.sqrt(2.0 / math.pi)
            th = jnp.tanh(x * (a + (a * 0.044715) * x2))
            d = (0.5 + 0.5 * th) * (1.0 + (x * (1.0 - th)) * (a + (3.0 * a * 0.044715) * x2))
            g = (tile_of(cot, t).astype(F32) * d).astype(BF)
            put_tile(pg, t, g)
            gs.append(g)
        bacc[...] += sum(g.astype(F32) for g in gs)
        g = jnp.concatenate(gs, axis=1)
        acc[...] += lax.dot_general(g, f, (((1,), (1,)), ((), ())), preferred_element_type=F32)

    save = pltpu.make_async_copy(pg, pg_hbm, psem)
    save.start()
    size = C * TILE
    ri = lax.broadcasted_iota(jnp.int32, (size, size), 0)
    ci = lax.broadcasted_iota(jnp.int32, (size, size), 1)
    masked = jnp.where(ri % TILE == ci % TILE, acc[...], 0.0)
    rows_sum = jnp.sum(masked.reshape(C, TILE, size), axis=1)
    fold = jnp.where(
        lax.broadcasted_iota(jnp.int32, (size, LANES), 0) // TILE
        == lax.broadcasted_iota(jnp.int32, (size, LANES), 1),
        1.0,
        0.0,
    ).astype(F32)
    pw = jnp.dot(rows_sum, fold, precision=precise, preferred_element_type=F32)
    by_row = jnp.sum(bacc[...].reshape(C, TILE, NZ), axis=1)
    lane = lax.broadcasted_iota(jnp.int32, (C, LANES), 1)
    sums[...] = pw + jnp.where(lane == C, jnp.sum(by_row, axis=1, keepdims=True), 0.0)
    plain_forward(pg, fy, fz, part, KY * rows)
    save.wait()


def last_kernel(rows, pg_hbm, modes, weight, gz, gy, out_hbm, field, kron, pg, out, fsem, osem):
    loads = load_groups(pg_hbm, pg, fsem)
    kron[...] = widen(weight[...])
    plane_back(modes, gz, gy, field)
    for copy in loads:
        copy.wait()
    saves = []
    cells = rows * NY // SAVES
    for piece in range(SAVES):

        @pl.loop(0, cells // (STEP * TILE))
        def _(i):
            s = piece * (cells // (STEP * TILE)) + i
            f = jnp.concatenate([tile_of(pg, STEP * s + h) for h in range(STEP)], axis=1)
            mix = dot(kron[...], f)
            for h in range(STEP):
                t = STEP * s + h
                r = mix[:, h * NZ : (h + 1) * NZ] + tile_of(field, t)
                put_tile(out, t, r.astype(BF))

        at = pl.ds(piece * cells, cells)
        saves.append(pltpu.make_async_copy(out.at[:, at], out_hbm.at[:, at], osem.at[piece]))
        saves[-1].start()
    for copy in saves:
        copy.wait()


def exchange_kernel(n, arrays, *refs):
    me = lax.axis_index("mp")
    greet(n)
    srcs = refs[:arrays]
    dsts = refs[arrays : 2 * arrays]
    send, recv, own = refs[2 * arrays :]
    pl.semaphore_wait(pltpu.get_barrier_semaphore(), n - 1)

    @pl.loop(1, n)
    def _(s):
        peer = lax.rem(me + s, n)
        for i in range(arrays):
            remote(
                srcs[i].at[peer], dsts[i].at[me], send.at[i, peer], recv.at[i, me], peer
            ).start()

    for i in range(arrays):
        mine = pltpu.make_async_copy(srcs[i].at[me], dsts[i].at[me], own.at[i])
        mine.start()
        mine.wait()

    @pl.loop(1, n)
    def _(s):
        peer = lax.rem(me + s, n)
        for i in range(arrays):
            both = remote(
                srcs[i].at[peer], dsts[i].at[peer], send.at[i, peer], recv.at[i, peer], peer
            )
            both.wait_recv()
            both.wait_send()


def exchange(xs, n, cid):
    shapes = [jax.ShapeDtypeStruct(x.shape, x.dtype) for x in xs]
    return pl.pallas_call(
        functools.partial(exchange_kernel, n, len(xs)),
        out_shape=shapes,
        in_specs=[VMEM] * len(xs),
        out_specs=[VMEM] * len(xs),
        scratch_shapes=[
            pltpu.SemaphoreType.DMA((len(xs), n)),
            pltpu.SemaphoreType.DMA((len(xs), n)),
            pltpu.SemaphoreType.DMA((len(xs),)),
        ],
        compiler_params=pltpu.CompilerParams(
            collective_id=cid, has_side_effects=True, vmem_limit_bytes=16 << 20
        ),
        name=f"exchange{cid}",
    )(*xs)


def call(kernel, rows, outs, scratch, args, name, far=(), far_out=(), cid=None):
    outs = list(outs)
    params = {} if cid is None else {"collective_id": cid, "has_side_effects": True}
    return pl.pallas_call(
        functools.partial(kernel, rows),
        out_shape=outs,
        in_specs=[HBM if i in far else VMEM for i in range(len(args))],
        out_specs=[HBM if i in far_out else VMEM for i in range(len(outs))],
        scratch_shapes=scratch,
        compiler_params=pltpu.CompilerParams(vmem_limit_bytes=60 << 20, **params),
        name=name,
    )(*args)


def owner_blocks(part, n, rows):
    subs = n // KY
    if subs > 1:
        v = part.reshape(KY, rows, 2 * C, subs, KZ // subs)
        part = jnp.transpose(v, (0, 3, 1, 2, 4))
    return part.reshape(n, rows, 2 * C * KZ // subs)


def plane_blocks(got, n, rows):
    subs = n // KY
    if subs > 1:
        v = got.reshape(KY, subs, rows, 2 * C, KZ // subs)
        got = jnp.transpose(v, (0, 2, 3, 1, 4))
    return got.reshape(KY * rows, 2 * C * KZ)


def lines_forward(g, fx):
    g = g.reshape(NX, -1)
    t = jnp.einsum("qx,xl->ql", fx, g, precision=precise).reshape(2, KX, GROUPS, 2, OCT, -1)
    real = t[0, :, :, 0] + t[1, :, :, 1]
    imag = t[0, :, :, 1] - t[1, :, :, 0]
    real, imag = (jnp.transpose(v.reshape(KX, C, -1), (2, 0, 1)) for v in (real, imag))
    return real, imag


def lines_back(real, imag, gx, n, rows):
    u = jnp.stack([real, imag]).reshape(2, real.shape[0], KX, GROUPS, OCT)
    u = jnp.transpose(u, (2, 3, 0, 4, 1)).reshape(KX, -1)
    b = jnp.einsum("qa,al->ql", gx, u, precision=precise).reshape(2, NX, GROUPS, 2, -1)
    lines = jnp.stack([b[0, :, :, 0] - b[1, :, :, 1], b[0, :, :, 1] + b[1, :, :, 0]], 2)
    return lines.reshape(n, rows, -1)


HALF = OCT * KZ
FULL = 2 * KX * C
ONE = 1.0 / SCALE
RING = 8
QUAD = 4
EIGHT = 8
BATCH = 16
PAIR = 2 * NZ
DUO = 2 * NY
SUB = 128
ROOT = math.sqrt(2.0 / math.pi)


def sharp(a, b):
    return jnp.dot(a, b, precision=precise, preferred_element_type=F32)


def lane_weight():
    k = lax.broadcasted_iota(jnp.int32, (1, GLANES), 1) % HALF // OCT
    return jnp.where(k == 0, SCALE, 2.0 * SCALE)


def place():
    me = lax.axis_index("mp")
    return me // QUAD, lax.rem(me, QUAD)


def near_peers():
    slab, spot = place()
    mates = [lax.rem(spot + s, QUAD) for s in range(1, QUAD)]
    return [(mate, slab * QUAD + mate) for mate in mates]


def far_peers(slabs):
    slab, spot = place()
    others = [lax.rem(slab + s, slabs) for s in range(1, slabs)]
    return [(other, other * QUAD + spot) for other in others]


def meet(slabs):
    barrier = pltpu.get_barrier_semaphore()
    for _, peer in near_peers() + far_peers(slabs):
        pl.semaphore_signal(
            barrier, inc=1, device_id={"mp": peer}, device_id_type=pl.DeviceIdType.MESH
        )


def send_near(turn, g, src, dst, send, recv):
    _, spot = place()
    for mate, peer in near_peers():
        remote(src.at[g, mate], dst.at[g, spot], send.at[turn, g], recv.at[turn, g], peer).start()
    pltpu.make_async_copy(src.at[g, spot], dst.at[g, spot], recv.at[turn, g]).start()


def send_far(turn, g, pick, dst, send, recv, slabs):
    slab, _ = place()
    for other, peer in far_peers(slabs):
        remote(pick(other), dst.at[g, slab], send.at[turn, g], recv.at[turn, g], peer).start()
    pltpu.make_async_copy(pick(slab), dst.at[g, slab], recv.at[turn, g]).start()


def wait_bytes(ref, sem):
    pltpu.make_async_copy(ref, ref, sem).wait()


def wait_sent(turn, g, like, send):
    wait_bytes(like.at[g, pl.ds(0, like.shape[1] - 1)], send.at[turn, g])


def part_lines(near, g, fxs, far):
    slab, _ = place()
    columns = []
    for t in range(near.shape[2]):
        pair = [
            near[g, :, t, :, r * HALF : (r + 1) * HALF].reshape(fxs.shape[2] // 2, HALF)
            for r in range(2)
        ]
        columns.append(jnp.concatenate(pair, axis=0))
    res = sharp(fxs[slab], jnp.concatenate(columns, axis=1))
    for t in range(near.shape[2]):
        far[g, t] = res[:, t * HALF : (t + 1) * HALF]


def sum_lines(far, g):
    return sum(far[g, t] for t in range(1, far.shape[1])) + far[g, 0]


def spread_lines(far, g, gxs, src):
    slab, _ = place()
    rows = src.shape[3]
    both = sharp(gxs[slab], jnp.concatenate([far[g, z] for z in range(far.shape[1])], axis=1))
    for r in range(2):
        for q in range(QUAD):
            top = (r * QUAD + q) * rows
            for z in range(far.shape[1]):
                src[g, q, z, :, r * HALF : (r + 1) * HALF] = both[
                    top : top + rows, z * HALF : (z + 1) * HALF
                ]


def gather_channels(parts, k):
    lane = lax.broadcasted_iota(jnp.int32, (2 * KX, LANES), 1) // OCT
    out = jnp.zeros((2 * KX, LANES), F32)
    for g in range(GROUPS):
        shift = (g * OCT - k * OCT) % LANES
        moved = pltpu.roll(parts[g], shift, 1) if shift else parts[g]
        out = jnp.where(lane == g, moved, out)
    return out


def fill_lanes(v):
    v = v + pltpu.roll(v, C, 1)
    return v + pltpu.roll(v, 2 * C, 1)


def own_mode(m):
    row = lax.broadcasted_iota(jnp.int32, (2 * KX, LANES), 0) % KX
    lane = lax.broadcasted_iota(jnp.int32, (2 * KX, LANES), 1) // C
    return row == m * (LANES // C) + lane


def diagonal(spread):
    turned = jnp.concatenate([-spread[KX:], spread[:KX]], axis=0)
    blocks = [jnp.where(own_mode(m), v, 0.0) for v in (spread, turned) for m in range(KX * C // LANES)]
    return jnp.concatenate(blocks, axis=1)


def put_channels(parts, k, v):
    lane = lax.broadcasted_iota(jnp.int32, (2 * KX, LANES), 1) // OCT
    for g in range(GROUPS):
        shift = (k * OCT - g * OCT) % LANES
        moved = pltpu.roll(v, shift, 1) if shift else v
        parts[g] = jnp.where(lane == k, moved, parts[g])


def halves(ref, t):
    v = tile_of(ref, t).reshape(C, TILE, NZ).astype(F32)
    return [
        v[:, w * EIGHT : (w + 1) * EIGHT].reshape(C * EIGHT, NZ).astype(BF)
        for w in range(TILE // EIGHT)
    ]


def batch_of(ref, s):
    return jnp.concatenate([v for h in range(BATCH) for v in halves(ref, BATCH * s + h)], axis=1)


def unbatch(mix, h):
    return [
        mix[:, (2 * h + w) * NZ : (2 * h + w + 1) * NZ].reshape(C, EIGHT, NZ) for w in range(2)
    ]


def widen_with(weight, turn):
    n = C * EIGHT
    row = lax.broadcasted_iota(jnp.int32, (n, C), 0) // EIGHT
    up = jnp.where(row == lax.broadcasted_iota(jnp.int32, (n, C), 1), 1.0, 0.0).astype(BF)
    dims = (((1,), (1 if turn else 0,)), ((), ()))
    left = lax.dot_general(up, weight, dims, preferred_element_type=F32).astype(BF)
    full = lax.dot_general(left, up, (((1,), (1,)), ((), ())), preferred_element_type=F32)
    ri = lax.broadcasted_iota(jnp.int32, (n, n), 0)
    ci = lax.broadcasted_iota(jnp.int32, (n, n), 1)
    return jnp.where(ri % EIGHT == ci % EIGHT, full, 0.0).astype(BF)


def slope(x):
    x2 = x * x
    th = jnp.tanh(x * (ROOT + (ROOT * 0.044715) * x2))
    return (1.0 + th) * (0.5 + (1.0 - th) * (x * (0.5 * ROOT + (1.5 * ROOT * 0.044715) * x2)))


def fold_pair(outs):
    parts = []
    for h in range(2):
        for s in range(2):
            rows = [
                o[s * 2 * KY : (s + 1) * 2 * KY, h * NZ : (h + 1) * NZ] for o in outs
            ]
            parts.append(jnp.concatenate(rows, axis=0))
    return parts


def put_plane(parts, fz, weight, tmp, src, g, rows):
    res = dot(jnp.concatenate(parts, axis=1), fz[...])
    if weight is not None:
        res = res * weight
    for r in range(2):
        tmp[r] = res[:, r * HALF : (r + 1) * HALF]
    for j in range(KY):
        for r in range(2):
            src[g, j % QUAD, j // QUAD, :, r * HALF : (r + 1) * HALF] = tmp[
                r, pl.ds(j, rows, stride=KY), :
            ]


def unfold(lhs, gz, ub):
    lines = lhs.shape[0]
    u = dot(lhs, gz[...]).astype(BF)
    for q in range(OCT):
        for r in range(2):
            at = (2 * q + r) * NZ
            ub[r * lines : (r + 1) * lines, q * NZ : (q + 1) * NZ] = u[:, at : at + NZ]


def heart_kernel(
    rows, n, feat_hbm, cot_hbm, w_hbm, fy_hbm, fz_hbm, gy_hbm, gz_hbm, weight, bias, fxs, gxs,
    mix_hbm, back, vout, dout, total,
    feat, cot, pg, field, ring, wb, fy, fz, gy, gz, kron, acc, ub, stage, src_a, src_b,
    near_1, near_2, near_3, near_4, out_f, out_m, far_1, far_2, far_3, far_4,
    sums, sums_near, sums_mid, sums_far, tmp, fsem, csem, tsem, wsem, send, recv, ssem, rsem, osem,
):
    me = lax.axis_index("mp")
    cells = rows * NY
    lines = KY * rows
    steps = cells // (BATCH * TILE)
    duos = cells // DUO
    slabs = n // QUAD
    slab, spot = place()
    meet(slabs)
    early = [pltpu.make_async_copy(a, b, tsem.at[i]) for i, (a, b) in enumerate(((fy_hbm, fy), (fz_hbm, fz)))]
    late = [pltpu.make_async_copy(a, b, tsem.at[2 + i]) for i, (a, b) in enumerate(((gy_hbm, gy), (gz_hbm, gz)))]

    def feat_copy(g):
        part = pl.ds(g * OCT, OCT)
        return pltpu.make_async_copy(feat_hbm.at[part], feat.at[part], fsem.at[g])

    def cot_copy(g):
        part = pl.ds(g * OCT, OCT)
        return pltpu.make_async_copy(cot_hbm.at[part], cot.at[part], csem.at[g])

    def ring_copy(k, slot):
        return pltpu.make_async_copy(w_hbm.at[k], ring.at[slot], wsem.at[slot])

    for copy in early:
        copy.start()
    for g in range(GROUPS):
        feat_copy(g).start()
    for copy in early:
        copy.wait()

    @pl.loop(0, GROUPS)
    def _(g):
        feat_copy(g).wait()
        parts = []
        for q in range(0, OCT, 2):
            c = g * OCT + q
            outs = []
            for x in range(duos):
                at = slice(x * DUO, (x + 1) * DUO)
                both = jnp.concatenate([feat[c, at], feat[c + 1, at]], axis=1)
                outs.append(dot(fy[...], both).astype(BF))
            parts += fold_pair(outs)
        put_plane(parts, fz, None, tmp, src_a, g, rows)

        @pl.when(g == 0)
        def _():
            pl.semaphore_wait(pltpu.get_barrier_semaphore(), QUAD + slabs - 2)

        send_near(0, g, src_a, near_1, send, recv)

    def reduce_group(turn, g, near, far):
        wait_bytes(near.at[g], recv.at[turn, g])
        part_lines(near, g, fxs, out_f)
        send_far(turn + 1, g, lambda t: out_f.at[g, t], far, send, recv, slabs)

    def give_group(turn, g, far):
        send_far(turn, g, lambda t: out_m.at[g], far, send, recv, slabs)

    def open_group(turn, g, far, near):
        wait_bytes(far.at[g], recv.at[turn, g])
        spread_lines(far, g, gxs, src_b)
        send_near(turn + 1, g, src_b, near, send, recv)

    for k in range(RING):
        ring_copy(k, k).start()
    for copy in late:
        copy.start()
    for g in range(GROUPS):
        cot_copy(g).start()

    kron[...] = widen_with(weight[...], False)
    size = C * EIGHT
    row = lax.broadcasted_iota(jnp.int32, (size, C), 0) // EIGHT
    column = jnp.where(row == lax.broadcasted_iota(jnp.int32, (size, C), 1), bias[...], 0.0)
    shift = jnp.sum(column, axis=1, keepdims=True)

    @pl.loop(0, steps)
    def _(s):
        mix = dot(kron[...], batch_of(feat, s)) + shift
        for h in range(BATCH):
            at = pl.multiple_of((BATCH * s + h) * TILE, TILE)
            for w, v in enumerate(unbatch(mix, h)):
                field[:, pl.ds(at + w * EIGHT, EIGHT), :] = v
        reduce_group(0, s, near_1, far_1)

    @pl.loop(0, KZ // RING)
    def _(i):
        for slot in range(RING):
            k = i * RING + slot
            ring_copy(k, slot).wait()
            wb[k] = ring[slot].astype(BF)

            @pl.when(k + RING < KZ)
            def _():
                ring_copy(k + RING, slot).start()

    for g in range(GROUPS):
        wait_bytes(far_1.at[g], recv.at[1, g])
        vout[g] = sum_lines(far_1, g)
    parts = [vout[g] for g in range(GROUPS)]
    mixed = [jnp.zeros((2 * KX, LANES), F32) for _ in range(GROUPS)]
    for k in range(KZ):
        left = diagonal(fill_lanes(gather_channels(parts, k))).astype(BF)
        stage[k, :, :C] = dot(left, wb[k])
    for k in range(KZ):
        put_channels(mixed, k, stage[k])
    for g in range(GROUPS):
        out_m[g] = mixed[g]
        give_group(2, g, far_2)
    for copy in late:
        copy.wait()
    for g in range(GROUPS):
        wait_sent(0, g, src_a, send)
        wait_sent(1, g, out_f, send)
        cot_copy(g).wait()
    open_group(2, 0, far_2, near_2)

    @pl.loop(0, GROUPS)
    def _(g):
        @pl.when(g + 1 < GROUPS)
        def _():
            open_group(2, g + 1, far_2, near_2)

        wait_bytes(near_2.at[g], recv.at[3, g])
        lhs = (near_2[g].reshape(lines, GLANES) * lane_weight()).astype(BF)
        unfold(lhs, gz, ub)

        parts = []
        for p in range(OCT // 2):
            uv = ub[:, p * PAIR : (p + 1) * PAIR]
            outs = []
            for d in range(duos):
                res = dot(gy[d * DUO : (d + 1) * DUO, :], uv)
                new = []
                for h in range(2):
                    c = g * OCT + 2 * p + h
                    pieces = []
                    for t in range(0, DUO, SUB):
                        at = slice(d * DUO + t, d * DUO + t + SUB)
                        x = res[t : t + SUB, h * NZ : (h + 1) * NZ] + field[c, at]
                        v = (cot[c, at].astype(F32) * slope(x)).astype(BF)
                        pg[c, at] = v
                        pieces.append(v)
                    new.append(jnp.concatenate(pieces, axis=0))
                outs.append(dot(fy[...], jnp.concatenate(new, axis=1)).astype(BF))
            parts += fold_pair(outs)
        put_plane(parts, fz, lane_weight(), tmp, src_a, g, rows)
        send_near(4, g, src_a, near_3, send, recv)

        @pl.when(g > 0)
        def _():
            reduce_group(4, g - 1, near_3, far_3)

    acc[...] = jnp.zeros_like(acc)

    @pl.loop(0, steps)
    def _(s):
        acc[...] += lax.dot_general(
            batch_of(pg, s), batch_of(feat, s), (((1,), (1,)), ((), ())),
            preferred_element_type=F32,
        )

        @pl.when(s == steps - 2)
        def _():
            reduce_group(4, GROUPS - 1, near_3, far_3)

    ri = lax.broadcasted_iota(jnp.int32, (size, size), 0)
    ci = lax.broadcasted_iota(jnp.int32, (size, size), 1)
    masked = jnp.where(ri % EIGHT == ci % EIGHT, acc[...], 0.0)
    rows_sum = jnp.sum(masked.reshape(C, EIGHT, size), axis=1)
    fold = jnp.where(
        lax.broadcasted_iota(jnp.int32, (size, LANES), 0) // EIGHT
        == lax.broadcasted_iota(jnp.int32, (size, LANES), 1),
        1.0,
        0.0,
    ).astype(F32)
    pw = sharp(rows_sum, fold)
    packed = pw[:8]
    for i in range(1, C // 8):
        packed = packed + pltpu.roll(pw[8 * i : 8 * i + 8], i * C, 1)
    sums[:8] = packed
    kron[...] = widen_with(weight[...], True)

    for g in range(GROUPS):
        wait_bytes(far_3.at[g], recv.at[5, g])
        dout[g] = sum_lines(far_3, g)
    parts = [dout[g] for g in range(GROUPS)]
    dc = jnp.zeros((1, LANES), F32)
    lane = lax.broadcasted_iota(jnp.int32, (1, LANES), 1)
    for g in range(GROUPS):
        v = parts[g][KX // 2 : KX // 2 + 1]
        v = pltpu.roll(v, g * OCT, 1) if g else v
        dc = jnp.where(lane // OCT == g, v * ONE, dc)
    owner = jnp.where(me == KY // 2, 1.0, 0.0)
    first = lax.broadcasted_iota(jnp.int32, (8, LANES), 0) == 0
    sums[8:] = jnp.where(first, dc * owner, 0.0)
    mixed = [jnp.zeros((2 * KX, LANES), F32) for _ in range(GROUPS)]
    half = KX * C
    for k in range(KZ):
        d = gather_channels(parts, k)[:, :C].astype(BF)
        full = lax.dot_general(d, wb[k], (((1,), (1,)), ((), ())), preferred_element_type=F32)
        a0 = jnp.zeros((2 * KX, LANES), F32)
        a1 = a0
        for m in range(half // LANES):
            own = own_mode(m)
            a0 = a0 + jnp.where(own, full[:, m * LANES : (m + 1) * LANES], 0.0)
            a1 = a1 + jnp.where(own, full[:, half + m * LANES : half + (m + 1) * LANES], 0.0)
        both = a0 + jnp.concatenate([a1[KX:], -a1[:KX]], axis=0)
        put_channels(mixed, k, fill_lanes(both))
    for g in range(GROUPS):
        wait_sent(2, g, far_2, send)
        wait_sent(3, g, src_b, send)
    for g in range(GROUPS):
        out_m[g] = mixed[g]
        give_group(6, g, far_4)
    for _, peer in near_peers():
        remote(sums, sums_near.at[spot], ssem.at[0], rsem.at[0], peer).start()
    pltpu.make_async_copy(sums, sums_near.at[spot], rsem.at[0]).start()

    @pl.loop(0, steps)
    def _(s):
        mix = dot(kron[...], batch_of(pg, s))
        for h in range(BATCH):
            both = jnp.concatenate(unbatch(mix, h), axis=1).astype(BF)
            put_tile(cot, BATCH * s + h, both.reshape(C * TILE, NZ))
        open_group(6, s, far_4, near_4)

    save = pltpu.make_async_copy(cot, mix_hbm, osem)
    save.start()
    wait_bytes(sums_near, rsem.at[0])
    sums_mid[...] = jnp.sum(sums_near[...], axis=0)
    for _, peer in far_peers(slabs):
        remote(sums_mid, sums_far.at[slab], ssem.at[1], rsem.at[1], peer).start()
    pltpu.make_async_copy(sums_mid, sums_far.at[slab], rsem.at[1]).start()
    for g in range(GROUPS):
        wait_bytes(near_4.at[g], recv.at[7, g])
        back[g] = near_4[g].reshape(lines, GLANES).astype(BF)
    wait_bytes(sums_far, rsem.at[1])
    total[...] = jnp.sum(sums_far[...], axis=0) * float(NX * NY * NZ) ** (-0.5)
    wait_bytes(sums_near.at[pl.ds(0, QUAD - 1)], ssem.at[0])
    wait_bytes(sums_far.at[pl.ds(0, slabs - 1)], ssem.at[1])
    for g in range(GROUPS):
        wait_sent(4, g, src_a, send)
        wait_sent(5, g, out_f, send)
        wait_sent(6, g, far_4, send)
        wait_sent(7, g, src_b, send)
    save.wait()


def tail_kernel(
    rows, mix_hbm, gz_hbm, gy_hbm, back, v, d, total, grad_hbm, sg_hbm, pwg, bg,
    mix, out, gz, gy, ub, sg, msem, tsem, osem, ssem,
):
    cells = rows * NY
    tables_in = [pltpu.make_async_copy(a, b, tsem.at[i]) for i, (a, b) in enumerate(((gz_hbm, gz), (gy_hbm, gy)))]
    for copy in tables_in:
        copy.start()
    loads = load_groups(mix_hbm, mix, msem)
    t = total[...]
    for i in range(C // 8):
        part = pltpu.roll(t[:8], LANES - i * C, 1) if i else t[:8]
        pwg[8 * i : 8 * i + 8, :] = part[:, :C]
    bg[...] = t[8:9, :C]
    vs = [v[g] for g in range(GROUPS)]
    ds = [d[g] for g in range(GROUPS)]
    for k in range(KZ):
        left = diagonal(fill_lanes(gather_channels(vs, k))).astype(BF)
        side = gather_channels(ds, k)[:, :C].astype(BF)
        sg[k] = lax.dot_general(left, side, (((0,), (0,)), ((), ())), preferred_element_type=F32)
        pltpu.make_async_copy(sg.at[k], sg_hbm.at[k], ssem.at[k]).start()
    for copy in tables_in:
        copy.wait()
    for g in range(GROUPS):
        loads[g].wait()
        unfold(back[g], gz, ub)

        for p in range(OCT // 2):
            uv = ub[:, p * PAIR : (p + 1) * PAIR]
            for r in range(0, cells, DUO):
                res = dot(gy[r : r + DUO, :], uv)
                for h in range(2):
                    c = g * OCT + 2 * p + h
                    at = slice(r, r + DUO)
                    out[c, at] = (res[:, h * NZ : (h + 1) * NZ] + mix[c, at].astype(F32)).astype(BF)

        part = pl.ds(g * OCT, OCT)
        pltpu.make_async_copy(out.at[part], grad_hbm.at[part], osem.at[g]).start()
    for g in range(GROUPS):
        part = pl.ds(g * OCT, OCT)
        pltpu.make_async_copy(out.at[part], grad_hbm.at[part], osem.at[g]).wait()
    for k in range(KZ):
        pltpu.make_async_copy(sg.at[k], sg_hbm.at[k], ssem.at[k]).wait()


def fused_shards(n, rows, features, cotangent, spectral_weight, pointwise_weight, biases):
    known = tables(rows)
    fz, gz, fy = [jnp.asarray(known[i]) for i in (10, 11, 12)]
    cells = rows * NY
    lines = KY * rows
    slabs = n // QUAD
    tall = QUAD * rows
    gy = known[1].reshape(cells, 2, slabs, QUAD, rows).transpose(0, 1, 3, 2, 4)
    gy = jnp.asarray(gy.reshape(known[1].shape))
    fxs = known[8].reshape(2 * KX, 2, slabs, tall).transpose(2, 0, 1, 3)
    fxs = jnp.asarray(fxs.reshape(slabs, 2 * KX, 2 * tall))
    gxs = known[9].reshape(2, slabs, tall, 2 * KX).transpose(1, 0, 2, 3)
    gxs = jnp.asarray(gxs.reshape(slabs, 2 * tall, 2 * KX))
    dma = pltpu.SemaphoreType.DMA
    block = pltpu.VMEM((C, cells, NZ), BF)
    shape = jax.ShapeDtypeStruct
    wide = C * EIGHT
    swap = pltpu.VMEM((GROUPS, QUAD, slabs, rows, GLANES), F32)
    far = pltpu.VMEM((GROUPS, slabs, 2 * KX, LANES), F32)
    few = pltpu.VMEM((16, LANES), F32)
    spec = shape((GROUPS, 2 * KX, LANES), F32)
    mix, back, v, d, total = pl.pallas_call(
        functools.partial(heart_kernel, rows, n),
        out_shape=[
            shape((C, cells, NZ), BF), shape((GROUPS, lines, GLANES), BF), spec, spec,
            shape((16, LANES), F32),
        ],
        in_specs=[HBM] * 7 + [VMEM] * 4,
        out_specs=[HBM] + [VMEM] * 4,
        scratch_shapes=[
            block, block, block, pltpu.VMEM((C, cells, NZ), F32),
            pltpu.VMEM((RING, FULL, C), F32), pltpu.VMEM((KZ, FULL, C), BF),
            pltpu.VMEM(fy.shape, BF), pltpu.VMEM(fz.shape, BF),
            pltpu.VMEM(gy.shape, BF), pltpu.VMEM(gz.shape, BF),
            pltpu.VMEM((wide, wide), BF), pltpu.VMEM((wide, wide), F32),
            pltpu.VMEM((2 * lines, OCT * NZ), BF), pltpu.VMEM((KZ, 2 * KX, LANES), F32),
            swap, swap, swap, swap, swap, swap, far,
            pltpu.VMEM((GROUPS, 2 * KX, LANES), F32), far, far, far, far,
            few, pltpu.VMEM((QUAD, 16, LANES), F32), few, pltpu.VMEM((slabs, 16, LANES), F32),
            pltpu.VMEM((2, lines, LANES), F32),
            dma((GROUPS,)), dma((GROUPS,)), dma((4,)), dma((RING,)),
            dma((8, GROUPS)), dma((8, GROUPS)), dma((2,)), dma((2,)), dma,
        ],
        compiler_params=pltpu.CompilerParams(
            collective_id=1, has_side_effects=True, vmem_limit_bytes=62 << 20
        ),
        name="heart",
    )(
        features.reshape(C, cells, NZ), cotangent.reshape(C, cells, NZ),
        spectral_weight.reshape(KZ, FULL, C), fy, fz, gy, gz, pointwise_weight,
        biases.reshape(1, C), fxs, gxs,
    )
    grad, sg, pwg, bg = pl.pallas_call(
        functools.partial(tail_kernel, rows),
        out_shape=[
            shape((C, cells, NZ), BF), shape((KZ, FULL, C), F32), shape((C, C), F32),
            shape((1, C), F32),
        ],
        in_specs=[HBM] * 3 + [VMEM] * 4,
        out_specs=[HBM, HBM, VMEM, VMEM],
        scratch_shapes=[
            block, block, pltpu.VMEM(gz.shape, BF), pltpu.VMEM(gy.shape, BF),
            pltpu.VMEM((2 * lines, OCT * NZ), BF), pltpu.VMEM((KZ, FULL, C), F32),
            dma((GROUPS,)), dma((2,)), dma((GROUPS,)), dma((KZ,)),
        ],
        compiler_params=pltpu.CompilerParams(vmem_limit_bytes=56 << 20),
        name="tail",
    )(mix, gz, gy, back, v, d, total)
    return (
        grad.reshape(features.shape), sg.reshape(spectral_weight.shape), pwg, bg.reshape(C),
    )


def shards(features, cotangent, spectral_weight, pointwise_weight, biases):
    n = lax.axis_size("mp")
    rows = NX // n
    if n == KY:
        return fused_shards(
            n, rows, features, cotangent, spectral_weight, pointwise_weight, biases
        )
    fy, gy, fz, fz_w, gz, gz_w, fx, gx = [jnp.asarray(t) for t in tables(rows)[:8]]
    cells = rows * NY
    feat = features.reshape(C, cells, NZ)
    cot = cotangent.reshape(C, cells, NZ)
    bias = jnp.repeat(biases, TILE)[:, None]
    spread = jax.ShapeDtypeStruct((KY * rows, 2 * C * KZ), F32)
    whole = jax.ShapeDtypeStruct((C, cells, NZ), BF)
    field = pltpu.VMEM((C, cells, NZ), F32)
    block = pltpu.VMEM((C, cells, NZ), BF)
    wide = C * TILE
    dma = pltpu.SemaphoreType.DMA
    sems = dma((GROUPS,))
    part = call(forward_kernel, rows, [spread], [], (feat, fy, fz), "analysis")[0]
    v_r, v_i = lines_forward(exchange([owner_blocks(part, n, rows)], n, 1)[0], fx)
    w_r, w_i = spectral_weight[:, 0], spectral_weight[:, 1]
    s_r, s_i = v_r[..., None], v_i[..., None]
    u_r = jnp.sum(s_r * w_r - s_i * w_i, axis=2)
    u_i = jnp.sum(s_r * w_i + s_i * w_r, axis=2)
    modes = exchange([lines_back(u_r, u_i, gx, n, rows)], n, 2)[0]
    pg, dpart, sums = call(
        middle_kernel,
        rows,
        [whole, spread, jax.ShapeDtypeStruct((C, LANES), F32)],
        [
            field,
            pltpu.VMEM((wide, wide), F32),
            pltpu.VMEM((wide, NZ), F32),
            pltpu.VMEM((wide, wide), BF),
            block,
            block,
            block,
            sems,
            sems,
            dma,
        ],
        (feat, cot, plane_blocks(modes, n, rows), pointwise_weight, bias, gz_w, gy, fy, fz_w),
        "middle",
        far=(0, 1),
        far_out=(0,),
    )
    d_r, d_i = lines_forward(exchange([owner_blocks(dpart, n, rows)], n, 3)[0], fx)
    e_r, e_i = d_r[:, :, None, :], d_i[:, :, None, :]
    m_r = jnp.sum(e_r * w_r + e_i * w_i, axis=3)
    m_i = jnp.sum(e_i * w_r - e_r * w_i, axis=3)
    packed = jnp.concatenate(
        [sums[:, :C].reshape(-1, LANES), jnp.pad(sums[:, C], (0, LANES - C))[None]], axis=0
    )
    mine = jnp.broadcast_to(packed, (n, *packed.shape))
    back, every = exchange([lines_back(m_r, m_i, gx, n, rows), mine], n, 4)
    total = jnp.sum(every, axis=0)
    first = jnp.stack([v_r, -v_i], axis=1)[..., None]
    second = jnp.stack([v_i, v_r], axis=1)[..., None]
    spectral_grad = first * e_r[:, None] + second * e_i[:, None]
    grad = call(
        last_kernel,
        rows,
        [whole],
        [field, pltpu.VMEM((wide, wide), BF), block, block, sems, dma((SAVES,))],
        (pg, plane_blocks(back, n, rows), pointwise_weight.T, gz, gy),
        "synthesis",
        far=(0,),
        far_out=(0,),
    )[0]
    factor = float(NX * NY * NZ) ** (-0.5)
    total = total * factor
    return (grad.reshape(features.shape), spectral_grad, total[:-1].reshape(C, C), total[-1, :C])


def solution(mesh):
    return jax.shard_map(
        shards,
        mesh=mesh,
        in_specs=(
            P(None, ("groups", "mp"), None, None),
            P(None, ("groups", "mp"), None, None),
            P("mp", None, None, None, None),
            P(),
            P(),
        ),
        out_specs=(
            P(None, ("groups", "mp"), None, None),
            P(("groups", "mp"), None, None, None, None),
            P("groups", None),
            P("groups"),
        ),
        check_vma=False,
    )
```

```python
import functools
import math

import jax
import jax.numpy as jnp
import ml_dtypes
import numpy as np
from jax import lax
from jax.experimental import pallas as pl
from jax.experimental.pallas import tpu as pltpu
from jax.sharding import PartitionSpec as P

C = 32
NX = 128
NY = 128
NZ = 128
KX = 16
KY = 16
KZ = 16
SCALE = 1.0 / (NX * NY * NZ)
OCT = 8
GROUPS = C // OCT
GLANES = 2 * OCT * KZ
LANES = 128
SAVES = 4
BF = jnp.bfloat16
F32 = jnp.float32
precise = lax.Precision.HIGHEST
VMEM = pl.BlockSpec(memory_space=pltpu.VMEM)
HBM = pl.BlockSpec(memory_space=pl.ANY)


def trig(length, mode_count, signed):
    freqs = np.arange(mode_count) - (mode_count // 2 if signed else 0)
    spots = np.arange(length)
    phases = (spots[:, None] * freqs[None, :] % length) * (2.0 * math.pi / length)
    return np.cos(phases), np.sin(phases)


def low(table):
    return np.asarray(table, np.float32).astype(ml_dtypes.bfloat16)


def tables(rows):
    zc, zs = trig(NZ, KZ, False)
    yc, ys = trig(NY, KY, True)
    xc, xs = trig(NX, KX, True)
    wz = np.where(np.arange(KZ) == 0, 1.0, 2.0) * SCALE
    eye = np.eye(rows)
    fy = np.einsum("syj,xw->sjxwy", np.stack([yc, ys]), eye).reshape(2 * KY * rows, rows * NY)
    gy = np.einsum("syj,xw->xysjw", np.stack([yc, -ys]), eye).reshape(rows * NY, 2 * KY * rows)
    zc_low = low(zc).astype(np.float64)
    zs_low = low(zs).astype(np.float64)
    oct_eye = np.eye(OCT)
    block = np.stack([np.stack([zc_low, -zs_low]), np.stack([-zs_low, -zc_low])])
    fz = np.einsum("srzk,ab->aszrbk", block, oct_eye).reshape(OCT * 2 * NZ, 2 * OCT * KZ)
    fz_w = (fz.reshape(-1, KZ) * wz).reshape(fz.shape)
    fy_k = np.einsum("syj,xw->sxjwy", np.stack([yc, ys]), np.eye(2)).reshape(4 * KY, 2 * NY)
    fz_k = np.einsum("srzk,ab->aszrkb", block, oct_eye).reshape(fz.shape)
    back = np.stack([np.stack([zc, zs]), np.stack([-zs, zc])])
    gz = np.einsum("rqzk,ab->rakbqz", back, oct_eye).reshape(2 * OCT * KZ, OCT * 2 * NZ)
    gz_w = (np.einsum("rqzk,ab,k->rakbqz", back, oct_eye, wz)).reshape(gz.shape)
    gz_k = np.einsum("rqzk,ab->rkabqz", back, oct_eye).reshape(gz.shape)
    fx = np.concatenate([xc.T, xs.T], 0).astype(np.float32)
    gx = np.concatenate([xc, xs], 0).astype(np.float32)
    fx2 = np.block([[xc.T, xs.T], [-xs.T, xc.T]]).astype(np.float32)
    gx2 = np.block([[xc, -xs], [xs, xc]]).astype(np.float32)
    return low(fy), low(gy), low(fz), low(fz_w), low(gz), low(gz_w), fx, gx, fx2, gx2, low(fz_k), low(gz_k), low(fy_k)


def dot(a, b):
    return jnp.dot(a, b, preferred_element_type=F32)


def forward_group(src, g, fy, fz, lines):
    parts = []
    for q in range(0, OCT, 2):
        pair = jnp.concatenate([src[g * OCT + q], src[g * OCT + q + 1]], axis=1)
        both = dot(fy[...], pair).astype(BF)
        for h in range(2):
            piece = both[:, h * NZ : (h + 1) * NZ]
            parts += [piece[:lines], piece[lines:]]
    return dot(jnp.concatenate(parts, axis=1), fz[...])


def plane_back(src, gz, gy, out):
    @pl.loop(0, GROUPS)
    def _(g):
        lhs = src[:, pl.ds(pl.multiple_of(g * GLANES, GLANES), GLANES)].astype(BF)
        u = dot(lhs, gz[...]).astype(BF)
        for q in range(0, OCT, 2):
            cols = []
            for h in range(2):
                o = q + h
                cols.append(
                    jnp.concatenate(
                        [u[:, (2 * o + r) * NZ : (2 * o + r + 1) * NZ] for r in range(2)], axis=0
                    )
                )
            res = dot(gy[...], jnp.concatenate(cols, axis=1))
            out[g * OCT + q] = res[:, :NZ]
            out[g * OCT + q + 1] = res[:, NZ:]


def plain_forward(src, fy, fz, out, lines):
    @pl.loop(0, GROUPS)
    def _(g):
        at = pl.multiple_of(g * GLANES, GLANES)
        out[:, pl.ds(at, GLANES)] = forward_group(src, g, fy, fz, lines)


def load_groups(hbm, buf, sems):
    copies = []
    for g in range(GROUPS):
        part = pl.ds(g * OCT, OCT)
        copies.append(pltpu.make_async_copy(hbm.at[part], buf.at[part], sems.at[g]))
        copies[-1].start()
    return copies


def greet(n):
    me = lax.axis_index("mp")

    @pl.loop(1, n)
    def _(s):
        pl.semaphore_signal(
            pltpu.get_barrier_semaphore(),
            inc=1,
            device_id={"mp": lax.rem(me + s, n)},
            device_id_type=pl.DeviceIdType.MESH,
        )


def remote(src, dst, send, recv, peer):
    return pltpu.make_async_remote_copy(
        src_ref=src,
        dst_ref=dst,
        send_sem=send,
        recv_sem=recv,
        device_id={"mp": peer},
        device_id_type=pl.DeviceIdType.MESH,
    )


def forward_kernel(rows, feat, fy, fz, out):
    plain_forward(feat, fy, fz, out, KY * rows)


TILE = 16
STEP = 4


def tile_of(ref, t):
    at = pl.multiple_of(t * TILE, TILE)
    return ref[:, pl.ds(at, TILE), :].reshape(C * TILE, NZ)


def put_tile(ref, t, value):
    at = pl.multiple_of(t * TILE, TILE)
    ref[:, pl.ds(at, TILE), :] = value.reshape(C, TILE, NZ)


def widen(weight):
    n = C * TILE
    row = lax.broadcasted_iota(jnp.int32, (n, C), 0) // TILE
    up = jnp.where(row == lax.broadcasted_iota(jnp.int32, (n, C), 1), 1.0, 0.0).astype(BF)
    left = dot(up, weight).astype(BF)
    full = lax.dot_general(left, up, (((1,), (1,)), ((), ())), preferred_element_type=F32)
    ri = lax.broadcasted_iota(jnp.int32, (n, n), 0)
    ci = lax.broadcasted_iota(jnp.int32, (n, n), 1)
    return jnp.where(ri % TILE == ci % TILE, full, 0.0).astype(BF)


def middle_kernel(
    rows, feat_hbm, cot_hbm, modes, weight, bias, gz, gy, fy, fz, pg_hbm, part, sums,
    field, acc, bacc, kron, feat, cot, pg, fsem, csem, psem,
):
    loads = load_groups(feat_hbm, feat, fsem) + load_groups(cot_hbm, cot, csem)
    kron[...] = widen(weight[...])
    acc[...] = jnp.zeros_like(acc)
    bacc[...] = jnp.zeros_like(bacc)
    plane_back(modes, gz, gy, field)
    for copy in loads:
        copy.wait()

    @pl.loop(0, rows * NY // (STEP * TILE))
    def _(s):
        f = jnp.concatenate([tile_of(feat, STEP * s + h) for h in range(STEP)], axis=1)
        mix = dot(kron[...], f)
        gs = []
        for h in range(STEP):
            t = STEP * s + h
            x = mix[:, h * NZ : (h + 1) * NZ] + tile_of(field, t) + bias[...]
            x2 = x * x
            a = math.sqrt(2.0 / math.pi)
            th = jnp.tanh(x * (a + (a * 0.044715) * x2))
            d = (0.5 + 0.5 * th) * (1.0 + (x * (1.0 - th)) * (a + (3.0 * a * 0.044715) * x2))
            g = (tile_of(cot, t).astype(F32) * d).astype(BF)
            put_tile(pg, t, g)
            gs.append(g)
        bacc[...] += sum(g.astype(F32) for g in gs)
        g = jnp.concatenate(gs, axis=1)
        acc[...] += lax.dot_general(g, f, (((1,), (1,)), ((), ())), preferred_element_type=F32)

    save = pltpu.make_async_copy(pg, pg_hbm, psem)
    save.start()
    size = C * TILE
    ri = lax.broadcasted_iota(jnp.int32, (size, size), 0)
    ci = lax.broadcasted_iota(jnp.int32, (size, size), 1)
    masked = jnp.where(ri % TILE == ci % TILE, acc[...], 0.0)
    rows_sum = jnp.sum(masked.reshape(C, TILE, size), axis=1)
    fold = jnp.where(
        lax.broadcasted_iota(jnp.int32, (size, LANES), 0) // TILE
        == lax.broadcasted_iota(jnp.int32, (size, LANES), 1),
        1.0,
        0.0,
    ).astype(F32)
    pw = jnp.dot(rows_sum, fold, precision=precise, preferred_element_type=F32)
    by_row = jnp.sum(bacc[...].reshape(C, TILE, NZ), axis=1)
    lane = lax.broadcasted_iota(jnp.int32, (C, LANES), 1)
    sums[...] = pw + jnp.where(lane == C, jnp.sum(by_row, axis=1, keepdims=True), 0.0)
    plain_forward(pg, fy, fz, part, KY * rows)
    save.wait()


def last_kernel(rows, pg_hbm, modes, weight, gz, gy, out_hbm, field, kron, pg, out, fsem, osem):
    loads = load_groups(pg_hbm, pg, fsem)
    kron[...] = widen(weight[...])
    plane_back(modes, gz, gy, field)
    for copy in loads:
        copy.wait()
    saves = []
    cells = rows * NY // SAVES
    for piece in range(SAVES):

        @pl.loop(0, cells // (STEP * TILE))
        def _(i):
            s = piece * (cells // (STEP * TILE)) + i
            f = jnp.concatenate([tile_of(pg, STEP * s + h) for h in range(STEP)], axis=1)
            mix = dot(kron[...], f)
            for h in range(STEP):
                t = STEP * s + h
                r = mix[:, h * NZ : (h + 1) * NZ] + tile_of(field, t)
                put_tile(out, t, r.astype(BF))

        at = pl.ds(piece * cells, cells)
        saves.append(pltpu.make_async_copy(out.at[:, at], out_hbm.at[:, at], osem.at[piece]))
        saves[-1].start()
    for copy in saves:
        copy.wait()


def exchange_kernel(n, arrays, *refs):
    me = lax.axis_index("mp")
    greet(n)
    srcs = refs[:arrays]
    dsts = refs[arrays : 2 * arrays]
    send, recv, own = refs[2 * arrays :]
    pl.semaphore_wait(pltpu.get_barrier_semaphore(), n - 1)

    @pl.loop(1, n)
    def _(s):
        peer = lax.rem(me + s, n)
        for i in range(arrays):
            remote(
                srcs[i].at[peer], dsts[i].at[me], send.at[i, peer], recv.at[i, me], peer
            ).start()

    for i in range(arrays):
        mine = pltpu.make_async_copy(srcs[i].at[me], dsts[i].at[me], own.at[i])
        mine.start()
        mine.wait()

    @pl.loop(1, n)
    def _(s):
        peer = lax.rem(me + s, n)
        for i in range(arrays):
            both = remote(
                srcs[i].at[peer], dsts[i].at[peer], send.at[i, peer], recv.at[i, peer], peer
            )
            both.wait_recv()
            both.wait_send()


def exchange(xs, n, cid):
    shapes = [jax.ShapeDtypeStruct(x.shape, x.dtype) for x in xs]
    return pl.pallas_call(
        functools.partial(exchange_kernel, n, len(xs)),
        out_shape=shapes,
        in_specs=[VMEM] * len(xs),
        out_specs=[VMEM] * len(xs),
        scratch_shapes=[
            pltpu.SemaphoreType.DMA((len(xs), n)),
            pltpu.SemaphoreType.DMA((len(xs), n)),
            pltpu.SemaphoreType.DMA((len(xs),)),
        ],
        compiler_params=pltpu.CompilerParams(
            collective_id=cid, has_side_effects=True, vmem_limit_bytes=16 << 20
        ),
        name=f"exchange{cid}",
    )(*xs)


def call(kernel, rows, outs, scratch, args, name, far=(), far_out=(), cid=None):
    outs = list(outs)
    params = {} if cid is None else {"collective_id": cid, "has_side_effects": True}
    return pl.pallas_call(
        functools.partial(kernel, rows),
        out_shape=outs,
        in_specs=[HBM if i in far else VMEM for i in range(len(args))],
        out_specs=[HBM if i in far_out else VMEM for i in range(len(outs))],
        scratch_shapes=scratch,
        compiler_params=pltpu.CompilerParams(vmem_limit_bytes=60 << 20, **params),
        name=name,
    )(*args)


def owner_blocks(part, n, rows):
    subs = n // KY
    if subs > 1:
        v = part.reshape(KY, rows, 2 * C, subs, KZ // subs)
        part = jnp.transpose(v, (0, 3, 1, 2, 4))
    return part.reshape(n, rows, 2 * C * KZ // subs)


def plane_blocks(got, n, rows):
    subs = n // KY
    if subs > 1:
        v = got.reshape(KY, subs, rows, 2 * C, KZ // subs)
        got = jnp.transpose(v, (0, 2, 3, 1, 4))
    return got.reshape(KY * rows, 2 * C * KZ)


def lines_forward(g, fx):
    g = g.reshape(NX, -1)
    t = jnp.einsum("qx,xl->ql", fx, g, precision=precise).reshape(2, KX, GROUPS, 2, OCT, -1)
    real = t[0, :, :, 0] + t[1, :, :, 1]
    imag = t[0, :, :, 1] - t[1, :, :, 0]
    real, imag = (jnp.transpose(v.reshape(KX, C, -1), (2, 0, 1)) for v in (real, imag))
    return real, imag


def lines_back(real, imag, gx, n, rows):
    u = jnp.stack([real, imag]).reshape(2, real.shape[0], KX, GROUPS, OCT)
    u = jnp.transpose(u, (2, 3, 0, 4, 1)).reshape(KX, -1)
    b = jnp.einsum("qa,al->ql", gx, u, precision=precise).reshape(2, NX, GROUPS, 2, -1)
    lines = jnp.stack([b[0, :, :, 0] - b[1, :, :, 1], b[0, :, :, 1] + b[1, :, :, 0]], 2)
    return lines.reshape(n, rows, -1)


HALF = OCT * KZ
FULL = 2 * KX * C
ONE = 1.0 / SCALE
RING = 8
QUAD = 4
EIGHT = 8
BATCH = 16
PAIR = 2 * NZ
DUO = 2 * NY
SUB = 128
ROOT = math.sqrt(2.0 / math.pi)


def sharp(a, b):
    return jnp.dot(a, b, precision=precise, preferred_element_type=F32)


def lane_weight():
    k = lax.broadcasted_iota(jnp.int32, (1, GLANES), 1) % HALF // OCT
    return jnp.where(k == 0, SCALE, 2.0 * SCALE)


def place():
    me = lax.axis_index("mp")
    return me // QUAD, lax.rem(me, QUAD)


def near_peers():
    slab, spot = place()
    mates = [lax.rem(spot + s, QUAD) for s in range(1, QUAD)]
    return [(mate, slab * QUAD + mate) for mate in mates]


def far_peers(slabs):
    slab, spot = place()
    others = [lax.rem(slab + s, slabs) for s in range(1, slabs)]
    return [(other, other * QUAD + spot) for other in others]


def meet(slabs):
    barrier = pltpu.get_barrier_semaphore()
    for _, peer in near_peers() + far_peers(slabs):
        pl.semaphore_signal(
            barrier, inc=1, device_id={"mp": peer}, device_id_type=pl.DeviceIdType.MESH
        )


def send_near(turn, g, src, dst, send, recv):
    _, spot = place()
    for mate, peer in near_peers():
        remote(src.at[g, mate], dst.at[g, spot], send.at[turn, g], recv.at[turn, g], peer).start()
    pltpu.make_async_copy(src.at[g, spot], dst.at[g, spot], recv.at[turn, g]).start()


def send_far(turn, g, pick, dst, send, recv, slabs):
    slab, _ = place()
    for other, peer in far_peers(slabs):
        remote(pick(other), dst.at[g, slab], send.at[turn, g], recv.at[turn, g], peer).start()
    pltpu.make_async_copy(pick(slab), dst.at[g, slab], recv.at[turn, g]).start()


def wait_bytes(ref, sem):
    pltpu.make_async_copy(ref, ref, sem).wait()


def wait_sent(turn, g, like, send):
    wait_bytes(like.at[g, pl.ds(0, like.shape[1] - 1)], send.at[turn, g])


def part_lines(near, g, fxs, far):
    slab, _ = place()
    columns = []
    for t in range(near.shape[2]):
        pair = [
            near[g, :, t, :, r * HALF : (r + 1) * HALF].reshape(fxs.shape[2] // 2, HALF)
            for r in range(2)
        ]
        columns.append(jnp.concatenate(pair, axis=0))
    res = sharp(fxs[slab], jnp.concatenate(columns, axis=1))
    for t in range(near.shape[2]):
        far[g, t] = res[:, t * HALF : (t + 1) * HALF]


def sum_lines(far, g):
    return sum(far[g, t] for t in range(1, far.shape[1])) + far[g, 0]


def spread_lines(far, g, gxs, src):
    slab, _ = place()
    rows = src.shape[3]
    both = sharp(gxs[slab], jnp.concatenate([far[g, z] for z in range(far.shape[1])], axis=1))
    for r in range(2):
        for q in range(QUAD):
            top = (r * QUAD + q) * rows
            for z in range(far.shape[1]):
                src[g, q, z, :, r * HALF : (r + 1) * HALF] = both[
                    top : top + rows, z * HALF : (z + 1) * HALF
                ]


def gather_channels(parts, k):
    lane = lax.broadcasted_iota(jnp.int32, (2 * KX, LANES), 1) // OCT
    out = jnp.zeros((2 * KX, LANES), F32)
    for g in range(GROUPS):
        shift = (g * OCT - k * OCT) % LANES
        moved = pltpu.roll(parts[g], shift, 1) if shift else parts[g]
        out = jnp.where(lane == g, moved, out)
    return out


def fill_lanes(v):
    v = v + pltpu.roll(v, C, 1)
    return v + pltpu.roll(v, 2 * C, 1)


def own_mode(m):
    row = lax.broadcasted_iota(jnp.int32, (2 * KX, LANES), 0) % KX
    lane = lax.broadcasted_iota(jnp.int32, (2 * KX, LANES), 1) // C
    return row == m * (LANES // C) + lane


def diagonal(spread):
    turned = jnp.concatenate([-spread[KX:], spread[:KX]], axis=0)
    blocks = [jnp.where(own_mode(m), v, 0.0) for v in (spread, turned) for m in range(KX * C // LANES)]
    return jnp.concatenate(blocks, axis=1)


def put_channels(parts, k, v):
    lane = lax.broadcasted_iota(jnp.int32, (2 * KX, LANES), 1) // OCT
    for g in range(GROUPS):
        shift = (k * OCT - g * OCT) % LANES
        moved = pltpu.roll(v, shift, 1) if shift else v
        parts[g] = jnp.where(lane == k, moved, parts[g])


def halves(ref, t):
    v = tile_of(ref, t).reshape(C, TILE, NZ).astype(F32)
    return [
        v[:, w * EIGHT : (w + 1) * EIGHT].reshape(C * EIGHT, NZ).astype(BF)
        for w in range(TILE // EIGHT)
    ]


def batch_of(ref, s):
    return jnp.concatenate([v for h in range(BATCH) for v in halves(ref, BATCH * s + h)], axis=1)


def unbatch(mix, h):
    return [
        mix[:, (2 * h + w) * NZ : (2 * h + w + 1) * NZ].reshape(C, EIGHT, NZ) for w in range(2)
    ]


def widen_with(weight, turn):
    n = C * EIGHT
    row = lax.broadcasted_iota(jnp.int32, (n, C), 0) // EIGHT
    up = jnp.where(row == lax.broadcasted_iota(jnp.int32, (n, C), 1), 1.0, 0.0).astype(BF)
    dims = (((1,), (1 if turn else 0,)), ((), ()))
    left = lax.dot_general(up, weight, dims, preferred_element_type=F32).astype(BF)
    full = lax.dot_general(left, up, (((1,), (1,)), ((), ())), preferred_element_type=F32)
    ri = lax.broadcasted_iota(jnp.int32, (n, n), 0)
    ci = lax.broadcasted_iota(jnp.int32, (n, n), 1)
    return jnp.where(ri % EIGHT == ci % EIGHT, full, 0.0).astype(BF)


def slope(x):
    x2 = x * x
    th = jnp.tanh(x * (ROOT + (ROOT * 0.044715) * x2))
    return (1.0 + th) * (0.5 + (1.0 - th) * (x * (0.5 * ROOT + (1.5 * ROOT * 0.044715) * x2)))


def fold_pair(outs):
    parts = []
    for h in range(2):
        for s in range(2):
            rows = [
                o[s * 2 * KY : (s + 1) * 2 * KY, h * NZ : (h + 1) * NZ] for o in outs
            ]
            parts.append(jnp.concatenate(rows, axis=0))
    return parts


def put_plane(parts, fz, weight, tmp, src, g, rows):
    res = dot(jnp.concatenate(parts, axis=1), fz[...])
    if weight is not None:
        res = res * weight
    for r in range(2):
        tmp[r] = res[:, r * HALF : (r + 1) * HALF]
    for j in range(KY):
        for r in range(2):
            src[g, j % QUAD, j // QUAD, :, r * HALF : (r + 1) * HALF] = tmp[
                r, pl.ds(j, rows, stride=KY), :
            ]


def unfold(lhs, gz, ub):
    lines = lhs.shape[0]
    u = dot(lhs, gz[...]).astype(BF)
    for q in range(OCT):
        for r in range(2):
            at = (2 * q + r) * NZ
            ub[r * lines : (r + 1) * lines, q * NZ : (q + 1) * NZ] = u[:, at : at + NZ]


def heart_kernel(
    rows, n, feat_hbm, cot_hbm, w_hbm, fy_hbm, fz_hbm, gy_hbm, gz_hbm, weight, bias, fxs, gxs,
    mix_hbm, back, vout, dout, total,
    feat, cot, pg, field, ring, wb, fy, fz, gy, gz, kron, acc, ub, stage, src_a, src_b,
    near_1, near_2, near_3, near_4, out_f, out_m, far_1, far_2, far_3, far_4,
    sums, sums_near, sums_mid, sums_far, tmp, fsem, csem, tsem, wsem, send, recv, ssem, rsem, osem,
):
    me = lax.axis_index("mp")
    cells = rows * NY
    lines = KY * rows
    steps = cells // (BATCH * TILE)
    duos = cells // DUO
    slabs = n // QUAD
    slab, spot = place()
    meet(slabs)
    early = [pltpu.make_async_copy(a, b, tsem.at[i]) for i, (a, b) in enumerate(((fy_hbm, fy), (fz_hbm, fz)))]
    late = [pltpu.make_async_copy(a, b, tsem.at[2 + i]) for i, (a, b) in enumerate(((gy_hbm, gy), (gz_hbm, gz)))]

    def feat_copy(g):
        part = pl.ds(g * OCT, OCT)
        return pltpu.make_async_copy(feat_hbm.at[part], feat.at[part], fsem.at[g])

    def cot_copy(g):
        part = pl.ds(g * OCT, OCT)
        return pltpu.make_async_copy(cot_hbm.at[part], cot.at[part], csem.at[g])

    def ring_copy(k, slot):
        return pltpu.make_async_copy(w_hbm.at[k], ring.at[slot], wsem.at[slot])

    for copy in early:
        copy.start()
    for g in range(GROUPS):
        feat_copy(g).start()
    for copy in early:
        copy.wait()

    @pl.loop(0, GROUPS)
    def _(g):
        feat_copy(g).wait()
        parts = []
        for q in range(0, OCT, 2):
            c = g * OCT + q
            outs = []
            for x in range(duos):
                at = slice(x * DUO, (x + 1) * DUO)
                both = jnp.concatenate([feat[c, at], feat[c + 1, at]], axis=1)
                outs.append(dot(fy[...], both).astype(BF))
            parts += fold_pair(outs)
        put_plane(parts, fz, None, tmp, src_a, g, rows)

        @pl.when(g == 0)
        def _():
            pl.semaphore_wait(pltpu.get_barrier_semaphore(), QUAD + slabs - 2)

        send_near(0, g, src_a, near_1, send, recv)

    def reduce_group(turn, g, near, far):
        wait_bytes(near.at[g], recv.at[turn, g])
        part_lines(near, g, fxs, out_f)
        send_far(turn + 1, g, lambda t: out_f.at[g, t], far, send, recv, slabs)

    def give_group(turn, g, far):
        send_far(turn, g, lambda t: out_m.at[g], far, send, recv, slabs)

    def open_group(turn, g, far, near):
        wait_bytes(far.at[g], recv.at[turn, g])
        spread_lines(far, g, gxs, src_b)
        send_near(turn + 1, g, src_b, near, send, recv)

    for k in range(RING):
        ring_copy(k, k).start()
    for copy in late:
        copy.start()
    for g in range(GROUPS):
        cot_copy(g).start()

    kron[...] = widen_with(weight[...], False)
    size = C * EIGHT
    row = lax.broadcasted_iota(jnp.int32, (size, C), 0) // EIGHT
    column = jnp.where(row == lax.broadcasted_iota(jnp.int32, (size, C), 1), bias[...], 0.0)
    shift = jnp.sum(column, axis=1, keepdims=True)

    @pl.loop(0, steps)
    def _(s):
        mix = dot(kron[...], batch_of(feat, s)) + shift
        for h in range(BATCH):
            at = pl.multiple_of((BATCH * s + h) * TILE, TILE)
            for w, v in enumerate(unbatch(mix, h)):
                field[:, pl.ds(at + w * EIGHT, EIGHT), :] = v
        reduce_group(0, s, near_1, far_1)

    @pl.loop(0, KZ // RING)
    def _(i):
        for slot in range(RING):
            k = i * RING + slot
            ring_copy(k, slot).wait()
            wb[k] = ring[slot].astype(BF)

            @pl.when(k + RING < KZ)
            def _():
                ring_copy(k + RING, slot).start()

    for g in range(GROUPS):
        wait_bytes(far_1.at[g], recv.at[1, g])
        vout[g] = sum_lines(far_1, g)
    parts = [vout[g] for g in range(GROUPS)]
    mixed = [jnp.zeros((2 * KX, LANES), F32) for _ in range(GROUPS)]
    for k in range(KZ):
        left = diagonal(fill_lanes(gather_channels(parts, k))).astype(BF)
        stage[k, :, :C] = dot(left, wb[k])
    for k in range(KZ):
        put_channels(mixed, k, stage[k])
    for g in range(GROUPS):
        out_m[g] = mixed[g]
        give_group(2, g, far_2)
    for copy in late:
        copy.wait()
    for g in range(GROUPS):
        wait_sent(0, g, src_a, send)
        wait_sent(1, g, out_f, send)
        cot_copy(g).wait()
    open_group(2, 0, far_2, near_2)

    @pl.loop(0, GROUPS)
    def _(g):
        @pl.when(g + 1 < GROUPS)
        def _():
            open_group(2, g + 1, far_2, near_2)

        wait_bytes(near_2.at[g], recv.at[3, g])
        lhs = (near_2[g].reshape(lines, GLANES) * lane_weight()).astype(BF)
        unfold(lhs, gz, ub)

        parts = []
        for p in range(OCT // 2):
            uv = ub[:, p * PAIR : (p + 1) * PAIR]
            outs = []
            for d in range(duos):
                res = dot(gy[d * DUO : (d + 1) * DUO, :], uv)
                new = []
                for h in range(2):
                    c = g * OCT + 2 * p + h
                    pieces = []
                    for t in range(0, DUO, SUB):
                        at = slice(d * DUO + t, d * DUO + t + SUB)
                        x = res[t : t + SUB, h * NZ : (h + 1) * NZ] + field[c, at]
                        v = (cot[c, at].astype(F32) * slope(x)).astype(BF)
                        pg[c, at] = v
                        pieces.append(v)
                    new.append(jnp.concatenate(pieces, axis=0))
                outs.append(dot(fy[...], jnp.concatenate(new, axis=1)).astype(BF))
            parts += fold_pair(outs)
        put_plane(parts, fz, lane_weight(), tmp, src_a, g, rows)
        send_near(4, g, src_a, near_3, send, recv)

        @pl.when(g > 0)
        def _():
            reduce_group(4, g - 1, near_3, far_3)

    acc[...] = jnp.zeros_like(acc)

    @pl.loop(0, steps)
    def _(s):
        acc[...] += lax.dot_general(
            batch_of(pg, s), batch_of(feat, s), (((1,), (1,)), ((), ())),
            preferred_element_type=F32,
        )

        @pl.when(s == steps - 2)
        def _():
            reduce_group(4, GROUPS - 1, near_3, far_3)

    ri = lax.broadcasted_iota(jnp.int32, (size, size), 0)
    ci = lax.broadcasted_iota(jnp.int32, (size, size), 1)
    masked = jnp.where(ri % EIGHT == ci % EIGHT, acc[...], 0.0)
    rows_sum = jnp.sum(masked.reshape(C, EIGHT, size), axis=1)
    fold = jnp.where(
        lax.broadcasted_iota(jnp.int32, (size, LANES), 0) // EIGHT
        == lax.broadcasted_iota(jnp.int32, (size, LANES), 1),
        1.0,
        0.0,
    ).astype(F32)
    pw = sharp(rows_sum, fold)
    packed = pw[:8]
    for i in range(1, C // 8):
        packed = packed + pltpu.roll(pw[8 * i : 8 * i + 8], i * C, 1)
    sums[:8] = packed
    kron[...] = widen_with(weight[...], True)

    for g in range(GROUPS):
        wait_bytes(far_3.at[g], recv.at[5, g])
        dout[g] = sum_lines(far_3, g)
    parts = [dout[g] for g in range(GROUPS)]
    dc = jnp.zeros((1, LANES), F32)
    lane = lax.broadcasted_iota(jnp.int32, (1, LANES), 1)
    for g in range(GROUPS):
        v = parts[g][KX // 2 : KX // 2 + 1]
        v = pltpu.roll(v, g * OCT, 1) if g else v
        dc = jnp.where(lane // OCT == g, v * ONE, dc)
    owner = jnp.where(me == KY // 2, 1.0, 0.0)
    first = lax.broadcasted_iota(jnp.int32, (8, LANES), 0) == 0
    sums[8:] = jnp.where(first, dc * owner, 0.0)
    mixed = [jnp.zeros((2 * KX, LANES), F32) for _ in range(GROUPS)]
    half = KX * C
    for k in range(KZ):
        d = gather_channels(parts, k)[:, :C].astype(BF)
        full = lax.dot_general(d, wb[k], (((1,), (1,)), ((), ())), preferred_element_type=F32)
        a0 = jnp.zeros((2 * KX, LANES), F32)
        a1 = a0
        for m in range(half // LANES):
            own = own_mode(m)
            a0 = a0 + jnp.where(own, full[:, m * LANES : (m + 1) * LANES], 0.0)
            a1 = a1 + jnp.where(own, full[:, half + m * LANES : half + (m + 1) * LANES], 0.0)
        both = a0 + jnp.concatenate([a1[KX:], -a1[:KX]], axis=0)
        put_channels(mixed, k, fill_lanes(both))
    for g in range(GROUPS):
        wait_sent(2, g, far_2, send)
        wait_sent(3, g, src_b, send)
    for g in range(GROUPS):
        out_m[g] = mixed[g]
        give_group(6, g, far_4)
    for _, peer in near_peers():
        remote(sums, sums_near.at[spot], ssem.at[0], rsem.at[0], peer).start()
    pltpu.make_async_copy(sums, sums_near.at[spot], rsem.at[0]).start()

    @pl.loop(0, steps)
    def _(s):
        mix = dot(kron[...], batch_of(pg, s))
        for h in range(BATCH):
            both = jnp.concatenate(unbatch(mix, h), axis=1).astype(BF)
            put_tile(cot, BATCH * s + h, both.reshape(C * TILE, NZ))
        open_group(6, s, far_4, near_4)

    save = pltpu.make_async_copy(cot, mix_hbm, osem)
    save.start()
    wait_bytes(sums_near, rsem.at[0])
    sums_mid[...] = jnp.sum(sums_near[...], axis=0)
    for _, peer in far_peers(slabs):
        remote(sums_mid, sums_far.at[slab], ssem.at[1], rsem.at[1], peer).start()
    pltpu.make_async_copy(sums_mid, sums_far.at[slab], rsem.at[1]).start()
    for g in range(GROUPS):
        wait_bytes(near_4.at[g], recv.at[7, g])
        back[g] = near_4[g].reshape(lines, GLANES).astype(BF)
    wait_bytes(sums_far, rsem.at[1])
    total[...] = jnp.sum(sums_far[...], axis=0) * float(NX * NY * NZ) ** (-0.5)
    wait_bytes(sums_near.at[pl.ds(0, QUAD - 1)], ssem.at[0])
    wait_bytes(sums_far.at[pl.ds(0, slabs - 1)], ssem.at[1])
    for g in range(GROUPS):
        wait_sent(4, g, src_a, send)
        wait_sent(5, g, out_f, send)
        wait_sent(6, g, far_4, send)
        wait_sent(7, g, src_b, send)
    save.wait()


def tail_kernel(
    rows, mix_hbm, gz_hbm, gy_hbm, back, v, d, total, grad_hbm, sg_hbm, pwg, bg,
    mix, out, gz, gy, ub, sg, msem, tsem, osem, ssem,
):
    cells = rows * NY
    tables_in = [pltpu.make_async_copy(a, b, tsem.at[i]) for i, (a, b) in enumerate(((gz_hbm, gz), (gy_hbm, gy)))]
    for copy in tables_in:
        copy.start()
    loads = [
        pltpu.make_async_copy(
            mix_hbm.at[pl.ds(g * OCT, OCT)], mix.at[pl.ds(g * OCT, OCT)], msem.at[g]
        )
        for g in range(GROUPS)
    ]
    for copy in loads[:2]:
        copy.start()
    t = total[...]
    for i in range(C // 8):
        part = pltpu.roll(t[:8], LANES - i * C, 1) if i else t[:8]
        pwg[8 * i : 8 * i + 8, :] = part[:, :C]
    bg[...] = t[8:9, :C]
    vs = [v[g] for g in range(GROUPS)]
    ds = [d[g] for g in range(GROUPS)]
    each = KZ // GROUPS
    for g in range(GROUPS):
        for k in range(g * each, (g + 1) * each):
            left = diagonal(fill_lanes(gather_channels(vs, k))).astype(BF)
            side = gather_channels(ds, k)[:, :C].astype(BF)
            sg[k] = lax.dot_general(
                left, side, (((0,), (0,)), ((), ())), preferred_element_type=F32
            )
            pltpu.make_async_copy(sg.at[k], sg_hbm.at[k], ssem.at[k]).start()
        if g == 0:
            for copy in tables_in:
                copy.wait()
        loads[g].wait()
        if g + 2 < GROUPS:
            loads[g + 2].start()
        unfold(back[g], gz, ub)

        for p in range(OCT // 2):
            uv = ub[:, p * PAIR : (p + 1) * PAIR]
            for r in range(0, cells, DUO):
                res = dot(gy[r : r + DUO, :], uv)
                for h in range(2):
                    c = g * OCT + 2 * p + h
                    at = slice(r, r + DUO)
                    out[c, at] = (res[:, h * NZ : (h + 1) * NZ] + mix[c, at].astype(F32)).astype(BF)

        part = pl.ds(g * OCT, OCT)
        pltpu.make_async_copy(out.at[part], grad_hbm.at[part], osem.at[g]).start()
    for g in range(GROUPS):
        part = pl.ds(g * OCT, OCT)
        pltpu.make_async_copy(out.at[part], grad_hbm.at[part], osem.at[g]).wait()
    for k in range(KZ):
        pltpu.make_async_copy(sg.at[k], sg_hbm.at[k], ssem.at[k]).wait()


def fused_shards(n, rows, features, cotangent, spectral_weight, pointwise_weight, biases):
    known = tables(rows)
    fz, gz, fy = [jnp.asarray(known[i]) for i in (10, 11, 12)]
    cells = rows * NY
    lines = KY * rows
    slabs = n // QUAD
    tall = QUAD * rows
    gy = known[1].reshape(cells, 2, slabs, QUAD, rows).transpose(0, 1, 3, 2, 4)
    gy = jnp.asarray(gy.reshape(known[1].shape))
    fxs = known[8].reshape(2 * KX, 2, slabs, tall).transpose(2, 0, 1, 3)
    fxs = jnp.asarray(fxs.reshape(slabs, 2 * KX, 2 * tall))
    gxs = known[9].reshape(2, slabs, tall, 2 * KX).transpose(1, 0, 2, 3)
    gxs = jnp.asarray(gxs.reshape(slabs, 2 * tall, 2 * KX))
    dma = pltpu.SemaphoreType.DMA
    block = pltpu.VMEM((C, cells, NZ), BF)
    shape = jax.ShapeDtypeStruct
    wide = C * EIGHT
    swap = pltpu.VMEM((GROUPS, QUAD, slabs, rows, GLANES), F32)
    far = pltpu.VMEM((GROUPS, slabs, 2 * KX, LANES), F32)
    few = pltpu.VMEM((16, LANES), F32)
    spec = shape((GROUPS, 2 * KX, LANES), F32)
    mix, back, v, d, total = pl.pallas_call(
        functools.partial(heart_kernel, rows, n),
        out_shape=[
            shape((C, cells, NZ), BF), shape((GROUPS, lines, GLANES), BF), spec, spec,
            shape((16, LANES), F32),
        ],
        in_specs=[HBM] * 7 + [VMEM] * 4,
        out_specs=[HBM] + [VMEM] * 4,
        scratch_shapes=[
            block, block, block, pltpu.VMEM((C, cells, NZ), F32),
            pltpu.VMEM((RING, FULL, C), F32), pltpu.VMEM((KZ, FULL, C), BF),
            pltpu.VMEM(fy.shape, BF), pltpu.VMEM(fz.shape, BF),
            pltpu.VMEM(gy.shape, BF), pltpu.VMEM(gz.shape, BF),
            pltpu.VMEM((wide, wide), BF), pltpu.VMEM((wide, wide), F32),
            pltpu.VMEM((2 * lines, OCT * NZ), BF), pltpu.VMEM((KZ, 2 * KX, LANES), F32),
            swap, swap, swap, swap, swap, swap, far,
            pltpu.VMEM((GROUPS, 2 * KX, LANES), F32), far, far, far, far,
            few, pltpu.VMEM((QUAD, 16, LANES), F32), few, pltpu.VMEM((slabs, 16, LANES), F32),
            pltpu.VMEM((2, lines, LANES), F32),
            dma((GROUPS,)), dma((GROUPS,)), dma((4,)), dma((RING,)),
            dma((8, GROUPS)), dma((8, GROUPS)), dma((2,)), dma((2,)), dma,
        ],
        compiler_params=pltpu.CompilerParams(
            collective_id=1, has_side_effects=True, vmem_limit_bytes=62 << 20
        ),
        name="heart",
    )(
        features.reshape(C, cells, NZ), cotangent.reshape(C, cells, NZ),
        spectral_weight.reshape(KZ, FULL, C), fy, fz, gy, gz, pointwise_weight,
        biases.reshape(1, C), fxs, gxs,
    )
    grad, sg, pwg, bg = pl.pallas_call(
        functools.partial(tail_kernel, rows),
        out_shape=[
            shape((C, cells, NZ), BF), shape((KZ, FULL, C), F32), shape((C, C), F32),
            shape((1, C), F32),
        ],
        in_specs=[HBM] * 3 + [VMEM] * 4,
        out_specs=[HBM, HBM, VMEM, VMEM],
        scratch_shapes=[
            block, block, pltpu.VMEM(gz.shape, BF), pltpu.VMEM(gy.shape, BF),
            pltpu.VMEM((2 * lines, OCT * NZ), BF), pltpu.VMEM((KZ, FULL, C), F32),
            dma((GROUPS,)), dma((2,)), dma((GROUPS,)), dma((KZ,)),
        ],
        compiler_params=pltpu.CompilerParams(vmem_limit_bytes=56 << 20),
        name="tail",
    )(mix, gz, gy, back, v, d, total)
    return (
        grad.reshape(features.shape), sg.reshape(spectral_weight.shape), pwg, bg.reshape(C),
    )


def shards(features, cotangent, spectral_weight, pointwise_weight, biases):
    n = lax.axis_size("mp")
    rows = NX // n
    if n == KY:
        return fused_shards(
            n, rows, features, cotangent, spectral_weight, pointwise_weight, biases
        )
    fy, gy, fz, fz_w, gz, gz_w, fx, gx = [jnp.asarray(t) for t in tables(rows)[:8]]
    cells = rows * NY
    feat = features.reshape(C, cells, NZ)
    cot = cotangent.reshape(C, cells, NZ)
    bias = jnp.repeat(biases, TILE)[:, None]
    spread = jax.ShapeDtypeStruct((KY * rows, 2 * C * KZ), F32)
    whole = jax.ShapeDtypeStruct((C, cells, NZ), BF)
    field = pltpu.VMEM((C, cells, NZ), F32)
    block = pltpu.VMEM((C, cells, NZ), BF)
    wide = C * TILE
    dma = pltpu.SemaphoreType.DMA
    sems = dma((GROUPS,))
    part = call(forward_kernel, rows, [spread], [], (feat, fy, fz), "analysis")[0]
    v_r, v_i = lines_forward(exchange([owner_blocks(part, n, rows)], n, 1)[0], fx)
    w_r, w_i = spectral_weight[:, 0], spectral_weight[:, 1]
    s_r, s_i = v_r[..., None], v_i[..., None]
    u_r = jnp.sum(s_r * w_r - s_i * w_i, axis=2)
    u_i = jnp.sum(s_r * w_i + s_i * w_r, axis=2)
    modes = exchange([lines_back(u_r, u_i, gx, n, rows)], n, 2)[0]
    pg, dpart, sums = call(
        middle_kernel,
        rows,
        [whole, spread, jax.ShapeDtypeStruct((C, LANES), F32)],
        [
            field,
            pltpu.VMEM((wide, wide), F32),
            pltpu.VMEM((wide, NZ), F32),
            pltpu.VMEM((wide, wide), BF),
            block,
            block,
            block,
            sems,
            sems,
            dma,
        ],
        (feat, cot, plane_blocks(modes, n, rows), pointwise_weight, bias, gz_w, gy, fy, fz_w),
        "middle",
        far=(0, 1),
        far_out=(0,),
    )
    d_r, d_i = lines_forward(exchange([owner_blocks(dpart, n, rows)], n, 3)[0], fx)
    e_r, e_i = d_r[:, :, None, :], d_i[:, :, None, :]
    m_r = jnp.sum(e_r * w_r + e_i * w_i, axis=3)
    m_i = jnp.sum(e_i * w_r - e_r * w_i, axis=3)
    packed = jnp.concatenate(
        [sums[:, :C].reshape(-1, LANES), jnp.pad(sums[:, C], (0, LANES - C))[None]], axis=0
    )
    mine = jnp.broadcast_to(packed, (n, *packed.shape))
    back, every = exchange([lines_back(m_r, m_i, gx, n, rows), mine], n, 4)
    total = jnp.sum(every, axis=0)
    first = jnp.stack([v_r, -v_i], axis=1)[..., None]
    second = jnp.stack([v_i, v_r], axis=1)[..., None]
    spectral_grad = first * e_r[:, None] + second * e_i[:, None]
    grad = call(
        last_kernel,
        rows,
        [whole],
        [field, pltpu.VMEM((wide, wide), BF), block, block, sems, dma((SAVES,))],
        (pg, plane_blocks(back, n, rows), pointwise_weight.T, gz, gy),
        "synthesis",
        far=(0,),
        far_out=(0,),
    )[0]
    factor = float(NX * NY * NZ) ** (-0.5)
    total = total * factor
    return (grad.reshape(features.shape), spectral_grad, total[:-1].reshape(C, C), total[-1, :C])


def solution(mesh):
    return jax.shard_map(
        shards,
        mesh=mesh,
        in_specs=(
            P(None, ("groups", "mp"), None, None),
            P(None, ("groups", "mp"), None, None),
            P("mp", None, None, None, None),
            P(),
            P(),
        ),
        out_specs=(
            P(None, ("groups", "mp"), None, None),
            P(("groups", "mp"), None, None, None, None),
            P("groups", None),
            P("groups"),
        ),
        check_vma=False,
    )
```

```python
import functools
import math

import jax
import jax.numpy as jnp
import ml_dtypes
import numpy as np
from jax import lax
from jax.experimental import pallas as pl
from jax.experimental.pallas import tpu as pltpu
from jax.sharding import PartitionSpec as P

C = 32
NX = 128
NY = 128
NZ = 128
KX = 16
KY = 16
KZ = 16
SCALE = 1.0 / (NX * NY * NZ)
OCT = 8
GROUPS = C // OCT
GLANES = 2 * OCT * KZ
LANES = 128
SAVES = 4
BF = jnp.bfloat16
F32 = jnp.float32
precise = lax.Precision.HIGHEST
VMEM = pl.BlockSpec(memory_space=pltpu.VMEM)
HBM = pl.BlockSpec(memory_space=pl.ANY)


def trig(length, mode_count, signed):
    freqs = np.arange(mode_count) - (mode_count // 2 if signed else 0)
    spots = np.arange(length)
    phases = (spots[:, None] * freqs[None, :] % length) * (2.0 * math.pi / length)
    return np.cos(phases), np.sin(phases)


def low(table):
    return np.asarray(table, np.float32).astype(ml_dtypes.bfloat16)


def tables(rows):
    zc, zs = trig(NZ, KZ, False)
    yc, ys = trig(NY, KY, True)
    xc, xs = trig(NX, KX, True)
    wz = np.where(np.arange(KZ) == 0, 1.0, 2.0) * SCALE
    eye = np.eye(rows)
    fy = np.einsum("syj,xw->sjxwy", np.stack([yc, ys]), eye).reshape(2 * KY * rows, rows * NY)
    gy = np.einsum("syj,xw->xysjw", np.stack([yc, -ys]), eye).reshape(rows * NY, 2 * KY * rows)
    zc_low = low(zc).astype(np.float64)
    zs_low = low(zs).astype(np.float64)
    oct_eye = np.eye(OCT)
    block = np.stack([np.stack([zc_low, -zs_low]), np.stack([-zs_low, -zc_low])])
    fz = np.einsum("srzk,ab->aszrbk", block, oct_eye).reshape(OCT * 2 * NZ, 2 * OCT * KZ)
    fz_w = (fz.reshape(-1, KZ) * wz).reshape(fz.shape)
    fy_k = np.einsum("syj,xw->sxjwy", np.stack([yc, ys]), np.eye(2)).reshape(4 * KY, 2 * NY)
    fz_k = np.einsum("srzk,ab->aszrkb", block, oct_eye).reshape(fz.shape)
    back = np.stack([np.stack([zc, zs]), np.stack([-zs, zc])])
    gz = np.einsum("rqzk,ab->rakbqz", back, oct_eye).reshape(2 * OCT * KZ, OCT * 2 * NZ)
    gz_w = (np.einsum("rqzk,ab,k->rakbqz", back, oct_eye, wz)).reshape(gz.shape)
    gz_k = np.einsum("rqzk,ab->rkabqz", back, oct_eye).reshape(gz.shape)
    fx = np.concatenate([xc.T, xs.T], 0).astype(np.float32)
    gx = np.concatenate([xc, xs], 0).astype(np.float32)
    fx2 = np.block([[xc.T, xs.T], [-xs.T, xc.T]]).astype(np.float32)
    gx2 = np.block([[xc, -xs], [xs, xc]]).astype(np.float32)
    return low(fy), low(gy), low(fz), low(fz_w), low(gz), low(gz_w), fx, gx, fx2, gx2, low(fz_k), low(gz_k), low(fy_k)


def dot(a, b):
    return jnp.dot(a, b, preferred_element_type=F32)


def forward_group(src, g, fy, fz, lines):
    parts = []
    for q in range(0, OCT, 2):
        pair = jnp.concatenate([src[g * OCT + q], src[g * OCT + q + 1]], axis=1)
        both = dot(fy[...], pair).astype(BF)
        for h in range(2):
            piece = both[:, h * NZ : (h + 1) * NZ]
            parts += [piece[:lines], piece[lines:]]
    return dot(jnp.concatenate(parts, axis=1), fz[...])


def plane_back(src, gz, gy, out):
    @pl.loop(0, GROUPS)
    def _(g):
        lhs = src[:, pl.ds(pl.multiple_of(g * GLANES, GLANES), GLANES)].astype(BF)
        u = dot(lhs, gz[...]).astype(BF)
        for q in range(0, OCT, 2):
            cols = []
            for h in range(2):
                o = q + h
                cols.append(
                    jnp.concatenate(
                        [u[:, (2 * o + r) * NZ : (2 * o + r + 1) * NZ] for r in range(2)], axis=0
                    )
                )
            res = dot(gy[...], jnp.concatenate(cols, axis=1))
            out[g * OCT + q] = res[:, :NZ]
            out[g * OCT + q + 1] = res[:, NZ:]


def plain_forward(src, fy, fz, out, lines):
    @pl.loop(0, GROUPS)
    def _(g):
        at = pl.multiple_of(g * GLANES, GLANES)
        out[:, pl.ds(at, GLANES)] = forward_group(src, g, fy, fz, lines)


def load_groups(hbm, buf, sems):
    copies = []
    for g in range(GROUPS):
        part = pl.ds(g * OCT, OCT)
        copies.append(pltpu.make_async_copy(hbm.at[part], buf.at[part], sems.at[g]))
        copies[-1].start()
    return copies


def greet(n):
    me = lax.axis_index("mp")

    @pl.loop(1, n)
    def _(s):
        pl.semaphore_signal(
            pltpu.get_barrier_semaphore(),
            inc=1,
            device_id={"mp": lax.rem(me + s, n)},
            device_id_type=pl.DeviceIdType.MESH,
        )


def remote(src, dst, send, recv, peer):
    return pltpu.make_async_remote_copy(
        src_ref=src,
        dst_ref=dst,
        send_sem=send,
        recv_sem=recv,
        device_id={"mp": peer},
        device_id_type=pl.DeviceIdType.MESH,
    )


def forward_kernel(rows, feat, fy, fz, out):
    plain_forward(feat, fy, fz, out, KY * rows)


TILE = 16
STEP = 4


def tile_of(ref, t):
    at = pl.multiple_of(t * TILE, TILE)
    return ref[:, pl.ds(at, TILE), :].reshape(C * TILE, NZ)


def put_tile(ref, t, value):
    at = pl.multiple_of(t * TILE, TILE)
    ref[:, pl.ds(at, TILE), :] = value.reshape(C, TILE, NZ)


def widen(weight):
    n = C * TILE
    row = lax.broadcasted_iota(jnp.int32, (n, C), 0) // TILE
    up = jnp.where(row == lax.broadcasted_iota(jnp.int32, (n, C), 1), 1.0, 0.0).astype(BF)
    left = dot(up, weight).astype(BF)
    full = lax.dot_general(left, up, (((1,), (1,)), ((), ())), preferred_element_type=F32)
    ri = lax.broadcasted_iota(jnp.int32, (n, n), 0)
    ci = lax.broadcasted_iota(jnp.int32, (n, n), 1)
    return jnp.where(ri % TILE == ci % TILE, full, 0.0).astype(BF)


def middle_kernel(
    rows, feat_hbm, cot_hbm, modes, weight, bias, gz, gy, fy, fz, pg_hbm, part, sums,
    field, acc, bacc, kron, feat, cot, pg, fsem, csem, psem,
):
    loads = load_groups(feat_hbm, feat, fsem) + load_groups(cot_hbm, cot, csem)
    kron[...] = widen(weight[...])
    acc[...] = jnp.zeros_like(acc)
    bacc[...] = jnp.zeros_like(bacc)
    plane_back(modes, gz, gy, field)
    for copy in loads:
        copy.wait()

    @pl.loop(0, rows * NY // (STEP * TILE))
    def _(s):
        f = jnp.concatenate([tile_of(feat, STEP * s + h) for h in range(STEP)], axis=1)
        mix = dot(kron[...], f)
        gs = []
        for h in range(STEP):
            t = STEP * s + h
            x = mix[:, h * NZ : (h + 1) * NZ] + tile_of(field, t) + bias[...]
            x2 = x * x
            a = math.sqrt(2.0 / math.pi)
            th = jnp.tanh(x * (a + (a * 0.044715) * x2))
            d = (0.5 + 0.5 * th) * (1.0 + (x * (1.0 - th)) * (a + (3.0 * a * 0.044715) * x2))
            g = (tile_of(cot, t).astype(F32) * d).astype(BF)
            put_tile(pg, t, g)
            gs.append(g)
        bacc[...] += sum(g.astype(F32) for g in gs)
        g = jnp.concatenate(gs, axis=1)
        acc[...] += lax.dot_general(g, f, (((1,), (1,)), ((), ())), preferred_element_type=F32)

    save = pltpu.make_async_copy(pg, pg_hbm, psem)
    save.start()
    size = C * TILE
    ri = lax.broadcasted_iota(jnp.int32, (size, size), 0)
    ci = lax.broadcasted_iota(jnp.int32, (size, size), 1)
    masked = jnp.where(ri % TILE == ci % TILE, acc[...], 0.0)
    rows_sum = jnp.sum(masked.reshape(C, TILE, size), axis=1)
    fold = jnp.where(
        lax.broadcasted_iota(jnp.int32, (size, LANES), 0) // TILE
        == lax.broadcasted_iota(jnp.int32, (size, LANES), 1),
        1.0,
        0.0,
    ).astype(F32)
    pw = jnp.dot(rows_sum, fold, precision=precise, preferred_element_type=F32)
    by_row = jnp.sum(bacc[...].reshape(C, TILE, NZ), axis=1)
    lane = lax.broadcasted_iota(jnp.int32, (C, LANES), 1)
    sums[...] = pw + jnp.where(lane == C, jnp.sum(by_row, axis=1, keepdims=True), 0.0)
    plain_forward(pg, fy, fz, part, KY * rows)
    save.wait()


def last_kernel(rows, pg_hbm, modes, weight, gz, gy, out_hbm, field, kron, pg, out, fsem, osem):
    loads = load_groups(pg_hbm, pg, fsem)
    kron[...] = widen(weight[...])
    plane_back(modes, gz, gy, field)
    for copy in loads:
        copy.wait()
    saves = []
    cells = rows * NY // SAVES
    for piece in range(SAVES):

        @pl.loop(0, cells // (STEP * TILE))
        def _(i):
            s = piece * (cells // (STEP * TILE)) + i
            f = jnp.concatenate([tile_of(pg, STEP * s + h) for h in range(STEP)], axis=1)
            mix = dot(kron[...], f)
            for h in range(STEP):
                t = STEP * s + h
                r = mix[:, h * NZ : (h + 1) * NZ] + tile_of(field, t)
                put_tile(out, t, r.astype(BF))

        at = pl.ds(piece * cells, cells)
        saves.append(pltpu.make_async_copy(out.at[:, at], out_hbm.at[:, at], osem.at[piece]))
        saves[-1].start()
    for copy in saves:
        copy.wait()


def exchange_kernel(n, arrays, *refs):
    me = lax.axis_index("mp")
    greet(n)
    srcs = refs[:arrays]
    dsts = refs[arrays : 2 * arrays]
    send, recv, own = refs[2 * arrays :]
    pl.semaphore_wait(pltpu.get_barrier_semaphore(), n - 1)

    @pl.loop(1, n)
    def _(s):
        peer = lax.rem(me + s, n)
        for i in range(arrays):
            remote(
                srcs[i].at[peer], dsts[i].at[me], send.at[i, peer], recv.at[i, me], peer
            ).start()

    for i in range(arrays):
        mine = pltpu.make_async_copy(srcs[i].at[me], dsts[i].at[me], own.at[i])
        mine.start()
        mine.wait()

    @pl.loop(1, n)
    def _(s):
        peer = lax.rem(me + s, n)
        for i in range(arrays):
            both = remote(
                srcs[i].at[peer], dsts[i].at[peer], send.at[i, peer], recv.at[i, peer], peer
            )
            both.wait_recv()
            both.wait_send()


def exchange(xs, n, cid):
    shapes = [jax.ShapeDtypeStruct(x.shape, x.dtype) for x in xs]
    return pl.pallas_call(
        functools.partial(exchange_kernel, n, len(xs)),
        out_shape=shapes,
        in_specs=[VMEM] * len(xs),
        out_specs=[VMEM] * len(xs),
        scratch_shapes=[
            pltpu.SemaphoreType.DMA((len(xs), n)),
            pltpu.SemaphoreType.DMA((len(xs), n)),
            pltpu.SemaphoreType.DMA((len(xs),)),
        ],
        compiler_params=pltpu.CompilerParams(
            collective_id=cid, has_side_effects=True, vmem_limit_bytes=16 << 20
        ),
        name=f"exchange{cid}",
    )(*xs)


def call(kernel, rows, outs, scratch, args, name, far=(), far_out=(), cid=None):
    outs = list(outs)
    params = {} if cid is None else {"collective_id": cid, "has_side_effects": True}
    return pl.pallas_call(
        functools.partial(kernel, rows),
        out_shape=outs,
        in_specs=[HBM if i in far else VMEM for i in range(len(args))],
        out_specs=[HBM if i in far_out else VMEM for i in range(len(outs))],
        scratch_shapes=scratch,
        compiler_params=pltpu.CompilerParams(vmem_limit_bytes=60 << 20, **params),
        name=name,
    )(*args)


def owner_blocks(part, n, rows):
    subs = n // KY
    if subs > 1:
        v = part.reshape(KY, rows, 2 * C, subs, KZ // subs)
        part = jnp.transpose(v, (0, 3, 1, 2, 4))
    return part.reshape(n, rows, 2 * C * KZ // subs)


def plane_blocks(got, n, rows):
    subs = n // KY
    if subs > 1:
        v = got.reshape(KY, subs, rows, 2 * C, KZ // subs)
        got = jnp.transpose(v, (0, 2, 3, 1, 4))
    return got.reshape(KY * rows, 2 * C * KZ)


def lines_forward(g, fx):
    g = g.reshape(NX, -1)
    t = jnp.einsum("qx,xl->ql", fx, g, precision=precise).reshape(2, KX, GROUPS, 2, OCT, -1)
    real = t[0, :, :, 0] + t[1, :, :, 1]
    imag = t[0, :, :, 1] - t[1, :, :, 0]
    real, imag = (jnp.transpose(v.reshape(KX, C, -1), (2, 0, 1)) for v in (real, imag))
    return real, imag


def lines_back(real, imag, gx, n, rows):
    u = jnp.stack([real, imag]).reshape(2, real.shape[0], KX, GROUPS, OCT)
    u = jnp.transpose(u, (2, 3, 0, 4, 1)).reshape(KX, -1)
    b = jnp.einsum("qa,al->ql", gx, u, precision=precise).reshape(2, NX, GROUPS, 2, -1)
    lines = jnp.stack([b[0, :, :, 0] - b[1, :, :, 1], b[0, :, :, 1] + b[1, :, :, 0]], 2)
    return lines.reshape(n, rows, -1)


HALF = OCT * KZ
FULL = 2 * KX * C
ONE = 1.0 / SCALE
RING = 8
QUAD = 4
EIGHT = 8
BATCH = 16
PAIR = 2 * NZ
DUO = 2 * NY
SUB = 128
ROOT = math.sqrt(2.0 / math.pi)


def sharp(a, b):
    return jnp.dot(a, b, precision=precise, preferred_element_type=F32)


def lane_weight():
    k = lax.broadcasted_iota(jnp.int32, (1, GLANES), 1) % HALF // OCT
    return jnp.where(k == 0, SCALE, 2.0 * SCALE)


def place():
    me = lax.axis_index("mp")
    return me // QUAD, lax.rem(me, QUAD)


def near_peers():
    slab, spot = place()
    mates = [lax.rem(spot + s, QUAD) for s in range(1, QUAD)]
    return [(mate, slab * QUAD + mate) for mate in mates]


def far_peers(slabs):
    slab, spot = place()
    others = [lax.rem(slab + s, slabs) for s in range(1, slabs)]
    return [(other, other * QUAD + spot) for other in others]


def meet(slabs):
    barrier = pltpu.get_barrier_semaphore()
    for _, peer in near_peers() + far_peers(slabs):
        pl.semaphore_signal(
            barrier, inc=1, device_id={"mp": peer}, device_id_type=pl.DeviceIdType.MESH
        )


def send_near(turn, g, src, dst, send, recv):
    _, spot = place()
    for mate, peer in near_peers():
        remote(src.at[g, mate], dst.at[g, spot], send.at[turn, g], recv.at[turn, g], peer).start()
    pltpu.make_async_copy(src.at[g, spot], dst.at[g, spot], recv.at[turn, g]).start()


def send_far(turn, g, pick, dst, send, recv, slabs):
    slab, _ = place()
    for other, peer in far_peers(slabs):
        remote(pick(other), dst.at[g, slab], send.at[turn, g], recv.at[turn, g], peer).start()
    pltpu.make_async_copy(pick(slab), dst.at[g, slab], recv.at[turn, g]).start()


def wait_bytes(ref, sem):
    pltpu.make_async_copy(ref, ref, sem).wait()


def wait_sent(turn, g, like, send):
    wait_bytes(like.at[g, pl.ds(0, like.shape[1] - 1)], send.at[turn, g])


def part_lines(near, g, fxs, far):
    slab, _ = place()
    columns = []
    for t in range(near.shape[2]):
        pair = [
            near[g, :, t, :, r * HALF : (r + 1) * HALF].reshape(fxs.shape[2] // 2, HALF)
            for r in range(2)
        ]
        columns.append(jnp.concatenate(pair, axis=0))
    res = sharp(fxs[slab], jnp.concatenate(columns, axis=1))
    for t in range(near.shape[2]):
        far[g, t] = res[:, t * HALF : (t + 1) * HALF]


def sum_lines(far, g):
    return sum(far[g, t] for t in range(1, far.shape[1])) + far[g, 0]


def spread_lines(far, g, gxs, src):
    slab, _ = place()
    rows = src.shape[3]
    both = sharp(gxs[slab], jnp.concatenate([far[g, z] for z in range(far.shape[1])], axis=1))
    for r in range(2):
        for q in range(QUAD):
            top = (r * QUAD + q) * rows
            for z in range(far.shape[1]):
                src[g, q, z, :, r * HALF : (r + 1) * HALF] = both[
                    top : top + rows, z * HALF : (z + 1) * HALF
                ]


def gather_channels(parts, k):
    lane = lax.broadcasted_iota(jnp.int32, (2 * KX, LANES), 1) // OCT
    out = jnp.zeros((2 * KX, LANES), F32)
    for g in range(GROUPS):
        shift = (g * OCT - k * OCT) % LANES
        moved = pltpu.roll(parts[g], shift, 1) if shift else parts[g]
        out = jnp.where(lane == g, moved, out)
    return out


def fill_lanes(v):
    v = v + pltpu.roll(v, C, 1)
    return v + pltpu.roll(v, 2 * C, 1)


def own_mode(m):
    row = lax.broadcasted_iota(jnp.int32, (2 * KX, LANES), 0) % KX
    lane = lax.broadcasted_iota(jnp.int32, (2 * KX, LANES), 1) // C
    return row == m * (LANES // C) + lane


def diagonal(spread):
    turned = jnp.concatenate([-spread[KX:], spread[:KX]], axis=0)
    blocks = [jnp.where(own_mode(m), v, 0.0) for v in (spread, turned) for m in range(KX * C // LANES)]
    return jnp.concatenate(blocks, axis=1)


def put_channels(parts, k, v):
    lane = lax.broadcasted_iota(jnp.int32, (2 * KX, LANES), 1) // OCT
    for g in range(GROUPS):
        shift = (k * OCT - g * OCT) % LANES
        moved = pltpu.roll(v, shift, 1) if shift else v
        parts[g] = jnp.where(lane == k, moved, parts[g])


def halves(ref, t):
    v = tile_of(ref, t).reshape(C, TILE, NZ).astype(F32)
    return [
        v[:, w * EIGHT : (w + 1) * EIGHT].reshape(C * EIGHT, NZ).astype(BF)
        for w in range(TILE // EIGHT)
    ]


def batch_of(ref, s):
    return jnp.concatenate([v for h in range(BATCH) for v in halves(ref, BATCH * s + h)], axis=1)


def unbatch(mix, h):
    return [
        mix[:, (2 * h + w) * NZ : (2 * h + w + 1) * NZ].reshape(C, EIGHT, NZ) for w in range(2)
    ]


def widen_with(weight, turn):
    n = C * EIGHT
    row = lax.broadcasted_iota(jnp.int32, (n, C), 0) // EIGHT
    up = jnp.where(row == lax.broadcasted_iota(jnp.int32, (n, C), 1), 1.0, 0.0).astype(BF)
    dims = (((1,), (1 if turn else 0,)), ((), ()))
    left = lax.dot_general(up, weight, dims, preferred_element_type=F32).astype(BF)
    full = lax.dot_general(left, up, (((1,), (1,)), ((), ())), preferred_element_type=F32)
    ri = lax.broadcasted_iota(jnp.int32, (n, n), 0)
    ci = lax.broadcasted_iota(jnp.int32, (n, n), 1)
    return jnp.where(ri % EIGHT == ci % EIGHT, full, 0.0).astype(BF)


def slope(x):
    x2 = x * x
    th = jnp.tanh(x * (ROOT + (ROOT * 0.044715) * x2))
    return (1.0 + th) * (0.5 + (1.0 - th) * (x * (0.5 * ROOT + (1.5 * ROOT * 0.044715) * x2)))


def fold_pair(outs):
    parts = []
    for h in range(2):
        for s in range(2):
            rows = [
                o[s * 2 * KY : (s + 1) * 2 * KY, h * NZ : (h + 1) * NZ] for o in outs
            ]
            parts.append(jnp.concatenate(rows, axis=0))
    return parts


def put_plane(parts, fz, weight, tmp, src, g, rows):
    res = dot(jnp.concatenate(parts, axis=1), fz[...])
    if weight is not None:
        res = res * weight
    for r in range(2):
        tmp[r] = res[:, r * HALF : (r + 1) * HALF]
    for j in range(KY):
        for r in range(2):
            src[g, j % QUAD, j // QUAD, :, r * HALF : (r + 1) * HALF] = tmp[
                r, pl.ds(j, rows, stride=KY), :
            ]


def unfold(lhs, gz, ub):
    lines = lhs.shape[0]
    u = dot(lhs, gz[...]).astype(BF)
    for q in range(OCT):
        for r in range(2):
            at = (2 * q + r) * NZ
            ub[r * lines : (r + 1) * lines, q * NZ : (q + 1) * NZ] = u[:, at : at + NZ]


def heart_kernel(
    rows, n, feat_hbm, cot_hbm, w_hbm, fy_hbm, fz_hbm, gy_hbm, gz_hbm, weight, bias, fxs, gxs,
    mix_hbm, back, vout, dout, total,
    feat, cot, pg, field, ring, wb, fy, fz, gy, gz, kron, acc, ub, stage, src_a, src_b,
    near_1, near_2, near_3, near_4, out_f, out_m, far_1, far_2, far_3, far_4,
    sums, sums_near, sums_mid, sums_far, tmp, fsem, csem, tsem, wsem, send, recv, ssem, rsem, osem,
):
    me = lax.axis_index("mp")
    cells = rows * NY
    lines = KY * rows
    steps = cells // (BATCH * TILE)
    duos = cells // DUO
    slabs = n // QUAD
    slab, spot = place()
    meet(slabs)
    early = [pltpu.make_async_copy(a, b, tsem.at[i]) for i, (a, b) in enumerate(((fy_hbm, fy), (fz_hbm, fz)))]
    late = [pltpu.make_async_copy(a, b, tsem.at[2 + i]) for i, (a, b) in enumerate(((gy_hbm, gy), (gz_hbm, gz)))]

    def feat_copy(g):
        part = pl.ds(g * OCT, OCT)
        return pltpu.make_async_copy(feat_hbm.at[part], feat.at[part], fsem.at[g])

    def cot_copy(g):
        part = pl.ds(g * OCT, OCT)
        return pltpu.make_async_copy(cot_hbm.at[part], cot.at[part], csem.at[g])

    def ring_copy(k, slot):
        return pltpu.make_async_copy(w_hbm.at[k], ring.at[slot], wsem.at[slot])

    for copy in early:
        copy.start()
    for g in range(GROUPS):
        feat_copy(g).start()
    for copy in early:
        copy.wait()

    @pl.loop(0, GROUPS)
    def _(g):
        feat_copy(g).wait()

        @pl.when(g == GROUPS - 2)
        def _():
            for k in range(RING):
                ring_copy(k, k).start()

        parts = []
        for q in range(0, OCT, 2):
            c = g * OCT + q
            outs = []
            for x in range(duos):
                at = slice(x * DUO, (x + 1) * DUO)
                both = jnp.concatenate([feat[c, at], feat[c + 1, at]], axis=1)
                outs.append(dot(fy[...], both).astype(BF))
            parts += fold_pair(outs)
        put_plane(parts, fz, None, tmp, src_a, g, rows)

        @pl.when(g == 0)
        def _():
            pl.semaphore_wait(pltpu.get_barrier_semaphore(), QUAD + slabs - 2)

        send_near(0, g, src_a, near_1, send, recv)

    def reduce_group(turn, g, near, far):
        wait_bytes(near.at[g], recv.at[turn, g])
        part_lines(near, g, fxs, out_f)
        send_far(turn + 1, g, lambda t: out_f.at[g, t], far, send, recv, slabs)

    def give_group(turn, g, far):
        send_far(turn, g, lambda t: out_m.at[g], far, send, recv, slabs)

    def open_group(turn, g, far, near):
        wait_bytes(far.at[g], recv.at[turn, g])
        spread_lines(far, g, gxs, src_b)
        send_near(turn + 1, g, src_b, near, send, recv)

    for copy in late:
        copy.start()
    for g in range(GROUPS):
        cot_copy(g).start()

    kron[...] = widen_with(weight[...], False)
    size = C * EIGHT
    row = lax.broadcasted_iota(jnp.int32, (size, C), 0) // EIGHT
    column = jnp.where(row == lax.broadcasted_iota(jnp.int32, (size, C), 1), bias[...], 0.0)
    shift = jnp.sum(column, axis=1, keepdims=True)

    def take_weights(i):
        for slot in range(RING):
            k = i * RING + slot
            ring_copy(k, slot).wait()
            wb[k] = ring[slot].astype(BF)
            if k + RING < KZ:
                ring_copy(k + RING, slot).start()

    take_weights(0)

    @pl.loop(0, steps)
    def _(s):
        mix = dot(kron[...], batch_of(feat, s)) + shift
        for h in range(BATCH):
            at = pl.multiple_of((BATCH * s + h) * TILE, TILE)
            for w, v in enumerate(unbatch(mix, h)):
                field[:, pl.ds(at + w * EIGHT, EIGHT), :] = v
        reduce_group(0, s, near_1, far_1)

    for i in range(1, KZ // RING):
        take_weights(i)
    for g in range(GROUPS):
        wait_bytes(far_1.at[g], recv.at[1, g])
        vout[g] = sum_lines(far_1, g)
    parts = [vout[g] for g in range(GROUPS)]
    mixed = [jnp.zeros((2 * KX, LANES), F32) for _ in range(GROUPS)]
    for k in range(KZ):
        left = diagonal(fill_lanes(gather_channels(parts, k))).astype(BF)
        stage[k, :, :C] = dot(left, wb[k])
    for k in range(KZ):
        put_channels(mixed, k, stage[k])
    for g in range(GROUPS):
        out_m[g] = mixed[g]
        give_group(2, g, far_2)
    for copy in late:
        copy.wait()
    for g in range(GROUPS):
        wait_sent(0, g, src_a, send)
        wait_sent(1, g, out_f, send)
        cot_copy(g).wait()
    open_group(2, 0, far_2, near_2)

    @pl.loop(0, GROUPS)
    def _(g):
        @pl.when(g + 1 < GROUPS)
        def _():
            open_group(2, g + 1, far_2, near_2)

        wait_bytes(near_2.at[g], recv.at[3, g])
        lhs = (near_2[g].reshape(lines, GLANES) * lane_weight()).astype(BF)
        unfold(lhs, gz, ub)

        parts = []
        for p in range(OCT // 2):
            uv = ub[:, p * PAIR : (p + 1) * PAIR]
            outs = []
            for d in range(duos):
                res = dot(gy[d * DUO : (d + 1) * DUO, :], uv)
                new = []
                for h in range(2):
                    c = g * OCT + 2 * p + h
                    pieces = []
                    for t in range(0, DUO, SUB):
                        at = slice(d * DUO + t, d * DUO + t + SUB)
                        x = res[t : t + SUB, h * NZ : (h + 1) * NZ] + field[c, at]
                        v = (cot[c, at].astype(F32) * slope(x)).astype(BF)
                        pg[c, at] = v
                        pieces.append(v)
                    new.append(jnp.concatenate(pieces, axis=0))
                outs.append(dot(fy[...], jnp.concatenate(new, axis=1)).astype(BF))
            parts += fold_pair(outs)
        put_plane(parts, fz, lane_weight(), tmp, src_a, g, rows)
        send_near(4, g, src_a, near_3, send, recv)

        @pl.when(g > 0)
        def _():
            reduce_group(4, g - 1, near_3, far_3)

    acc[...] = jnp.zeros_like(acc)

    @pl.loop(0, steps)
    def _(s):
        acc[...] += lax.dot_general(
            batch_of(pg, s), batch_of(feat, s), (((1,), (1,)), ((), ())),
            preferred_element_type=F32,
        )

        @pl.when(s == steps - 2)
        def _():
            reduce_group(4, GROUPS - 1, near_3, far_3)

    ri = lax.broadcasted_iota(jnp.int32, (size, size), 0)
    ci = lax.broadcasted_iota(jnp.int32, (size, size), 1)
    masked = jnp.where(ri % EIGHT == ci % EIGHT, acc[...], 0.0)
    rows_sum = jnp.sum(masked.reshape(C, EIGHT, size), axis=1)
    fold = jnp.where(
        lax.broadcasted_iota(jnp.int32, (size, LANES), 0) // EIGHT
        == lax.broadcasted_iota(jnp.int32, (size, LANES), 1),
        1.0,
        0.0,
    ).astype(F32)
    pw = sharp(rows_sum, fold)
    packed = pw[:8]
    for i in range(1, C // 8):
        packed = packed + pltpu.roll(pw[8 * i : 8 * i + 8], i * C, 1)
    sums[:8] = packed
    kron[...] = widen_with(weight[...], True)

    for g in range(GROUPS):
        wait_bytes(far_3.at[g], recv.at[5, g])
        dout[g] = sum_lines(far_3, g)
    parts = [dout[g] for g in range(GROUPS)]
    dc = jnp.zeros((1, LANES), F32)
    lane = lax.broadcasted_iota(jnp.int32, (1, LANES), 1)
    for g in range(GROUPS):
        v = parts[g][KX // 2 : KX // 2 + 1]
        v = pltpu.roll(v, g * OCT, 1) if g else v
        dc = jnp.where(lane // OCT == g, v * ONE, dc)
    owner = jnp.where(me == KY // 2, 1.0, 0.0)
    first = lax.broadcasted_iota(jnp.int32, (8, LANES), 0) == 0
    sums[8:] = jnp.where(first, dc * owner, 0.0)
    mixed = [jnp.zeros((2 * KX, LANES), F32) for _ in range(GROUPS)]
    half = KX * C
    for k in range(KZ):
        d = gather_channels(parts, k)[:, :C].astype(BF)
        full = lax.dot_general(d, wb[k], (((1,), (1,)), ((), ())), preferred_element_type=F32)
        a0 = jnp.zeros((2 * KX, LANES), F32)
        a1 = a0
        for m in range(half // LANES):
            own = own_mode(m)
            a0 = a0 + jnp.where(own, full[:, m * LANES : (m + 1) * LANES], 0.0)
            a1 = a1 + jnp.where(own, full[:, half + m * LANES : half + (m + 1) * LANES], 0.0)
        both = a0 + jnp.concatenate([a1[KX:], -a1[:KX]], axis=0)
        put_channels(mixed, k, fill_lanes(both))
    for g in range(GROUPS):
        wait_sent(2, g, far_2, send)
        wait_sent(3, g, src_b, send)
    for g in range(GROUPS):
        out_m[g] = mixed[g]
        give_group(6, g, far_4)
    for _, peer in near_peers():
        remote(sums, sums_near.at[spot], ssem.at[0], rsem.at[0], peer).start()
    pltpu.make_async_copy(sums, sums_near.at[spot], rsem.at[0]).start()

    def save_copy(s):
        part = pl.ds(pl.multiple_of(s * BATCH * TILE, BATCH * TILE), BATCH * TILE)
        return pltpu.make_async_copy(cot.at[:, part], mix_hbm.at[:, part], osem.at[s])

    @pl.loop(0, steps)
    def _(s):
        mix = dot(kron[...], batch_of(pg, s))
        for h in range(BATCH):
            both = jnp.concatenate(unbatch(mix, h), axis=1).astype(BF)
            put_tile(cot, BATCH * s + h, both.reshape(C * TILE, NZ))
        save_copy(s).start()
        open_group(6, s, far_4, near_4)

        @pl.when(s == 1)
        def _():
            wait_bytes(sums_near, rsem.at[0])
            sums_mid[...] = jnp.sum(sums_near[...], axis=0)
            for _, peer in far_peers(slabs):
                remote(sums_mid, sums_far.at[slab], ssem.at[1], rsem.at[1], peer).start()
            pltpu.make_async_copy(sums_mid, sums_far.at[slab], rsem.at[1]).start()

    for g in range(GROUPS):
        wait_bytes(near_4.at[g], recv.at[7, g])
        back[g] = near_4[g].reshape(lines, GLANES).astype(BF)
    wait_bytes(sums_far, rsem.at[1])
    total[...] = jnp.sum(sums_far[...], axis=0) * float(NX * NY * NZ) ** (-0.5)
    wait_bytes(sums_near.at[pl.ds(0, QUAD - 1)], ssem.at[0])
    wait_bytes(sums_far.at[pl.ds(0, slabs - 1)], ssem.at[1])
    for g in range(GROUPS):
        wait_sent(4, g, src_a, send)
        wait_sent(5, g, out_f, send)
        wait_sent(6, g, far_4, send)
        wait_sent(7, g, src_b, send)
    for s in range(steps):
        save_copy(s).wait()


def tail_kernel(
    rows, mix_hbm, gz_hbm, gy_hbm, back, v, d, total, grad_hbm, sg_hbm, pwg, bg,
    mix, out, gz, gy, ub, sg, msem, tsem, osem, ssem,
):
    cells = rows * NY
    tables_in = [pltpu.make_async_copy(a, b, tsem.at[i]) for i, (a, b) in enumerate(((gz_hbm, gz), (gy_hbm, gy)))]
    for copy in tables_in:
        copy.start()
    loads = [
        pltpu.make_async_copy(
            mix_hbm.at[pl.ds(g * OCT, OCT)], mix.at[pl.ds(g * OCT, OCT)], msem.at[g]
        )
        for g in range(GROUPS)
    ]
    for copy in loads[:2]:
        copy.start()
    t = total[...]
    for i in range(C // 8):
        part = pltpu.roll(t[:8], LANES - i * C, 1) if i else t[:8]
        pwg[8 * i : 8 * i + 8, :] = part[:, :C]
    bg[...] = t[8:9, :C]
    vs = [v[g] for g in range(GROUPS)]
    ds = [d[g] for g in range(GROUPS)]
    each = KZ // GROUPS
    for g in range(GROUPS):
        for k in range(g * each, (g + 1) * each):
            left = diagonal(fill_lanes(gather_channels(vs, k))).astype(BF)
            side = gather_channels(ds, k)[:, :C].astype(BF)
            sg[k] = lax.dot_general(
                left, side, (((0,), (0,)), ((), ())), preferred_element_type=F32
            )
            pltpu.make_async_copy(sg.at[k], sg_hbm.at[k], ssem.at[k]).start()
        if g == 0:
            for copy in tables_in:
                copy.wait()
        loads[g].wait()
        if g + 2 < GROUPS:
            loads[g + 2].start()
        unfold(back[g], gz, ub)

        for p in range(OCT // 2):
            uv = ub[:, p * PAIR : (p + 1) * PAIR]
            for r in range(0, cells, DUO):
                res = dot(gy[r : r + DUO, :], uv)
                for h in range(2):
                    c = g * OCT + 2 * p + h
                    at = slice(r, r + DUO)
                    out[c, at] = (res[:, h * NZ : (h + 1) * NZ] + mix[c, at].astype(F32)).astype(BF)

        part = pl.ds(g * OCT, OCT)
        pltpu.make_async_copy(out.at[part], grad_hbm.at[part], osem.at[g]).start()
    for g in range(GROUPS):
        part = pl.ds(g * OCT, OCT)
        pltpu.make_async_copy(out.at[part], grad_hbm.at[part], osem.at[g]).wait()
    for k in range(KZ):
        pltpu.make_async_copy(sg.at[k], sg_hbm.at[k], ssem.at[k]).wait()


def fused_shards(n, rows, features, cotangent, spectral_weight, pointwise_weight, biases):
    known = tables(rows)
    fz, gz, fy = [jnp.asarray(known[i]) for i in (10, 11, 12)]
    cells = rows * NY
    lines = KY * rows
    slabs = n // QUAD
    tall = QUAD * rows
    gy = known[1].reshape(cells, 2, slabs, QUAD, rows).transpose(0, 1, 3, 2, 4)
    gy = jnp.asarray(gy.reshape(known[1].shape))
    fxs = known[8].reshape(2 * KX, 2, slabs, tall).transpose(2, 0, 1, 3)
    fxs = jnp.asarray(fxs.reshape(slabs, 2 * KX, 2 * tall))
    gxs = known[9].reshape(2, slabs, tall, 2 * KX).transpose(1, 0, 2, 3)
    gxs = jnp.asarray(gxs.reshape(slabs, 2 * tall, 2 * KX))
    dma = pltpu.SemaphoreType.DMA
    block = pltpu.VMEM((C, cells, NZ), BF)
    shape = jax.ShapeDtypeStruct
    wide = C * EIGHT
    swap = pltpu.VMEM((GROUPS, QUAD, slabs, rows, GLANES), F32)
    far = pltpu.VMEM((GROUPS, slabs, 2 * KX, LANES), F32)
    few = pltpu.VMEM((16, LANES), F32)
    spec = shape((GROUPS, 2 * KX, LANES), F32)
    mix, back, v, d, total = pl.pallas_call(
        functools.partial(heart_kernel, rows, n),
        out_shape=[
            shape((C, cells, NZ), BF), shape((GROUPS, lines, GLANES), BF), spec, spec,
            shape((16, LANES), F32),
        ],
        in_specs=[HBM] * 7 + [VMEM] * 4,
        out_specs=[HBM] + [VMEM] * 4,
        scratch_shapes=[
            block, block, block, pltpu.VMEM((C, cells, NZ), F32),
            pltpu.VMEM((RING, FULL, C), F32), pltpu.VMEM((KZ, FULL, C), BF),
            pltpu.VMEM(fy.shape, BF), pltpu.VMEM(fz.shape, BF),
            pltpu.VMEM(gy.shape, BF), pltpu.VMEM(gz.shape, BF),
            pltpu.VMEM((wide, wide), BF), pltpu.VMEM((wide, wide), F32),
            pltpu.VMEM((2 * lines, OCT * NZ), BF), pltpu.VMEM((KZ, 2 * KX, LANES), F32),
            swap, swap, swap, swap, swap, swap, far,
            pltpu.VMEM((GROUPS, 2 * KX, LANES), F32), far, far, far, far,
            few, pltpu.VMEM((QUAD, 16, LANES), F32), few, pltpu.VMEM((slabs, 16, LANES), F32),
            pltpu.VMEM((2, lines, LANES), F32),
            dma((GROUPS,)), dma((GROUPS,)), dma((4,)), dma((RING,)),
            dma((8, GROUPS)), dma((8, GROUPS)), dma((2,)), dma((2,)),
            dma((cells // (BATCH * TILE),)),
        ],
        compiler_params=pltpu.CompilerParams(
            collective_id=1, has_side_effects=True, vmem_limit_bytes=62 << 20
        ),
        name="heart",
    )(
        features.reshape(C, cells, NZ), cotangent.reshape(C, cells, NZ),
        spectral_weight.reshape(KZ, FULL, C), fy, fz, gy, gz, pointwise_weight,
        biases.reshape(1, C), fxs, gxs,
    )
    grad, sg, pwg, bg = pl.pallas_call(
        functools.partial(tail_kernel, rows),
        out_shape=[
            shape((C, cells, NZ), BF), shape((KZ, FULL, C), F32), shape((C, C), F32),
            shape((1, C), F32),
        ],
        in_specs=[HBM] * 3 + [VMEM] * 4,
        out_specs=[HBM, HBM, VMEM, VMEM],
        scratch_shapes=[
            block, block, pltpu.VMEM(gz.shape, BF), pltpu.VMEM(gy.shape, BF),
            pltpu.VMEM((2 * lines, OCT * NZ), BF), pltpu.VMEM((KZ, FULL, C), F32),
            dma((GROUPS,)), dma((2,)), dma((GROUPS,)), dma((KZ,)),
        ],
        compiler_params=pltpu.CompilerParams(vmem_limit_bytes=56 << 20),
        name="tail",
    )(mix, gz, gy, back, v, d, total)
    return (
        grad.reshape(features.shape), sg.reshape(spectral_weight.shape), pwg, bg.reshape(C),
    )


def shards(features, cotangent, spectral_weight, pointwise_weight, biases):
    n = lax.axis_size("mp")
    rows = NX // n
    if n == KY:
        return fused_shards(
            n, rows, features, cotangent, spectral_weight, pointwise_weight, biases
        )
    fy, gy, fz, fz_w, gz, gz_w, fx, gx = [jnp.asarray(t) for t in tables(rows)[:8]]
    cells = rows * NY
    feat = features.reshape(C, cells, NZ)
    cot = cotangent.reshape(C, cells, NZ)
    bias = jnp.repeat(biases, TILE)[:, None]
    spread = jax.ShapeDtypeStruct((KY * rows, 2 * C * KZ), F32)
    whole = jax.ShapeDtypeStruct((C, cells, NZ), BF)
    field = pltpu.VMEM((C, cells, NZ), F32)
    block = pltpu.VMEM((C, cells, NZ), BF)
    wide = C * TILE
    dma = pltpu.SemaphoreType.DMA
    sems = dma((GROUPS,))
    part = call(forward_kernel, rows, [spread], [], (feat, fy, fz), "analysis")[0]
    v_r, v_i = lines_forward(exchange([owner_blocks(part, n, rows)], n, 1)[0], fx)
    w_r, w_i = spectral_weight[:, 0], spectral_weight[:, 1]
    s_r, s_i = v_r[..., None], v_i[..., None]
    u_r = jnp.sum(s_r * w_r - s_i * w_i, axis=2)
    u_i = jnp.sum(s_r * w_i + s_i * w_r, axis=2)
    modes = exchange([lines_back(u_r, u_i, gx, n, rows)], n, 2)[0]
    pg, dpart, sums = call(
        middle_kernel,
        rows,
        [whole, spread, jax.ShapeDtypeStruct((C, LANES), F32)],
        [
            field,
            pltpu.VMEM((wide, wide), F32),
            pltpu.VMEM((wide, NZ), F32),
            pltpu.VMEM((wide, wide), BF),
            block,
            block,
            block,
            sems,
            sems,
            dma,
        ],
        (feat, cot, plane_blocks(modes, n, rows), pointwise_weight, bias, gz_w, gy, fy, fz_w),
        "middle",
        far=(0, 1),
        far_out=(0,),
    )
    d_r, d_i = lines_forward(exchange([owner_blocks(dpart, n, rows)], n, 3)[0], fx)
    e_r, e_i = d_r[:, :, None, :], d_i[:, :, None, :]
    m_r = jnp.sum(e_r * w_r + e_i * w_i, axis=3)
    m_i = jnp.sum(e_i * w_r - e_r * w_i, axis=3)
    packed = jnp.concatenate(
        [sums[:, :C].reshape(-1, LANES), jnp.pad(sums[:, C], (0, LANES - C))[None]], axis=0
    )
    mine = jnp.broadcast_to(packed, (n, *packed.shape))
    back, every = exchange([lines_back(m_r, m_i, gx, n, rows), mine], n, 4)
    total = jnp.sum(every, axis=0)
    first = jnp.stack([v_r, -v_i], axis=1)[..., None]
    second = jnp.stack([v_i, v_r], axis=1)[..., None]
    spectral_grad = first * e_r[:, None] + second * e_i[:, None]
    grad = call(
        last_kernel,
        rows,
        [whole],
        [field, pltpu.VMEM((wide, wide), BF), block, block, sems, dma((SAVES,))],
        (pg, plane_blocks(back, n, rows), pointwise_weight.T, gz, gy),
        "synthesis",
        far=(0,),
        far_out=(0,),
    )[0]
    factor = float(NX * NY * NZ) ** (-0.5)
    total = total * factor
    return (grad.reshape(features.shape), spectral_grad, total[:-1].reshape(C, C), total[-1, :C])


def solution(mesh):
    return jax.shard_map(
        shards,
        mesh=mesh,
        in_specs=(
            P(None, ("groups", "mp"), None, None),
            P(None, ("groups", "mp"), None, None),
            P("mp", None, None, None, None),
            P(),
            P(),
        ),
        out_specs=(
            P(None, ("groups", "mp"), None, None),
            P(("groups", "mp"), None, None, None, None),
            P("groups", None),
            P("groups"),
        ),
        check_vma=False,
    )
```
